32 devices in a mesh: wide: 8 (over z, x), narrow: 4 (over y, core).
Axes of the slice: x: 2, y: 2, z: 4, core: 2. Of those that a mesh axis runs over, the one named last changes fastest.
Arguments:
- tokens: bfloat16 [2048, 128, 256], P(('wide', 'narrow')), may hold values from -6 to 6
- visible_index: int32 [2048, 112], P(('wide', 'narrow')), may hold values from 0 to 127, as said below
- visible_count: int32 [2048], P(('wide', 'narrow')), may hold values from 8 to 112, as said below
- ln1_gain: bfloat16 [256], replicated, may hold values from 0.5 to 1.5
- ln1_bias: bfloat16 [256], replicated, may hold values from -1.1953125 to 1.1953125
- qkv_weight: bfloat16 [256, 768], replicated, may hold values from -0.375 to 0.375
- query_bias: bfloat16 [256], replicated, may hold values from -1.796875 to 1.796875
- value_bias: bfloat16 [256], replicated, may hold values from -1.796875 to 1.796875
- out_weight: bfloat16 [256, 256], replicated, may hold values from -1.5 to 1.5
- out_bias: bfloat16 [256], replicated, may hold values from -1.1953125 to 1.1953125
- ln2_gain: bfloat16 [256], replicated, may hold values from 0.5 to 1.5
- ln2_bias: bfloat16 [256], replicated, may hold values from -1.1953125 to 1.1953125
- up_weight: bfloat16 [256, 1024], replicated, may hold values from -0.375 to 0.375
- up_bias: bfloat16 [1024], replicated, may hold values from -1.796875 to 1.796875
- down_weight: bfloat16 [1024, 256], replicated, may hold values from -0.375 to 0.375
- down_bias: bfloat16 [256], replicated, may hold values from -1.1953125 to 1.1953125
- out_grad: bfloat16 [2048, 112, 256], P(('wide', 'narrow')), may hold values from -6 to 6
Outputs:
- layer_out: bfloat16 [2048, 112, 256], P(('wide', 'narrow'))
- tokens_grad: bfloat16 [2048, 128, 256], P(('wide', 'narrow'))
- ln1_gain_grad: float32 [256], replicated
- ln1_bias_grad: float32 [256], replicated
- qkv_weight_grad: float32 [256, 768], replicated
- query_bias_grad: float32 [256], replicated
- value_bias_grad: float32 [256], replicated
- out_weight_grad: float32 [256, 256], replicated
- out_bias_grad: float32 [256], replicated
- ln2_gain_grad: float32 [256], replicated
- ln2_bias_grad: float32 [256], replicated
- up_weight_grad: float32 [256, 1024], replicated
- up_bias_grad: float32 [1024], replicated
- down_weight_grad: float32 [1024, 256], replicated
- down_bias_grad: float32 [256], replicated
The draws below stay inside these ranges and needn't reach their ends.
Inputs may be any that keep to these rules, and one draw needn't show every extreme that they name: `visible_index`: the entries of a row are distinct positions; entries at or beyond the row's visible count are not used. `visible_count`: in every block of 64 trajectories (those of one device) one trajectory has exactly 112.
All inputs are finite; a program needn't handle non-finite values.
Results may differ from the reference program's by a relative error of at most 0.012.
Values sent between devices are 32-bit elements; how exact they have to be, the bound alone decides.
No kernel may reach another device: no remote copies, remote signals or barrier semaphores. Data moves between devices by JAX's collectives and lax.ppermute only.
A program may use at most 256 MiB of HBM per device.

```python
import jax
import jax.numpy as jnp
from jax import lax

D = 256
HEADS = 4
FF = 1024
HEAD = 64
SEQ = 128
CAP = 112
MINV = 8
TRAJ_DEV = 64
TRAJ = 2048


def draw_visible_index(key, part):
    key = jax.random.fold_in(key, 5)
    ranked = jax.random.randint(key, (TRAJ, SEQ), 0, 1 << 20) * SEQ + jnp.arange(SEQ, dtype=jnp.int32)[None, :]
    ranked = jnp.argsort(ranked, axis=1)
    return ranked[:, :CAP].astype(jnp.int32)


def draw_visible_count(key, part):
    key = jax.random.fold_in(key, 11)
    first_key, second_key = jax.random.split(key)
    counts = jax.random.randint(first_key, (TRAJ,), MINV, CAP + 1)
    blocks = TRAJ // TRAJ_DEV
    chosen = jax.random.randint(second_key, (blocks,), 0, TRAJ_DEV)
    filled = (jnp.arange(TRAJ_DEV, dtype=jnp.int32)[None, :] == chosen[:, None]).reshape(TRAJ)
    return jnp.where(filled, CAP, counts).astype(jnp.int32)


def level_of(stream_key, shape, pieces, low, high):
    gain = 1.0
    for dim, shards_of in pieces:
        steps = jax.random.uniform(jax.random.fold_in(jax.random.fold_in(stream_key, 6), dim), (shards_of,), jnp.float32, low / len(pieces), high / len(pieces))
        gain = gain * jnp.repeat(jnp.exp(steps), shape[dim] // shards_of).reshape((-1,) + (1,) * (len(shape) - 1 - dim))
    return gain


def noise(key, extent, scale, limit, cuts=(), kind=jnp.bfloat16):
    values = jax.random.normal(key, extent, jnp.float32) * scale
    if len(cuts) > 0:
        values = level_of(key, extent, cuts, -0.22, 0.18) * values
    return jnp.clip(values, min=-limit, max=limit).astype(kind)


def setup_inputs(seed: int = 0) -> dict:
    splits = jax.random.split(jax.random.key(seed), 18)
    tokens = noise(splits[0], (TRAJ, SEQ, D), 1.0, 6.0, ((0, 32),))
    visible_index = draw_visible_index(jax.random.fold_in(splits[17], 71), 0)
    visible_count = draw_visible_count(jax.random.fold_in(splits[17], 71), 0)
    ln1_gain = jnp.clip(1.0 + 0.1 * jax.random.normal(splits[3], (D,), jnp.float32), 0.5, 1.5).astype(jnp.bfloat16)
    ln1_bias = noise(splits[4], (D,), 0.2, 1.1953125)
    qkv_weight = noise(splits[5], (D, 3 * D), D ** -0.5, 0.375)
    query_bias = noise(splits[6], (D,), 0.3, 1.796875)
    value_bias = noise(splits[7], (D,), 0.3, 1.796875)
    out_weight = noise(splits[8], (D, D), (D // 16) ** -0.5, 1.5)
    out_bias = noise(splits[9], (D,), 0.2, 1.1953125)
    ln2_gain = jnp.clip(1.0 + 0.1 * jax.random.normal(splits[10], (D,), jnp.float32), 0.5, 1.5).astype(jnp.bfloat16)
    ln2_bias = noise(splits[11], (D,), 0.2, 1.1953125)
    up_weight = noise(splits[12], (D, FF), D ** -0.5, 0.375)
    up_bias = noise(splits[13], (FF,), 0.3, 1.796875)
    down_weight = noise(splits[14], (FF, D), (FF // 4) ** -0.5, 0.375)
    down_bias = noise(splits[15], (D,), 0.2, 1.1953125)
    out_grad = noise(splits[16], (TRAJ, CAP, D), 1.0, 6.0, ((0, 32),))
    return {"tokens": tokens, "visible_index": visible_index, "visible_count": visible_count, "ln1_gain": ln1_gain, "ln1_bias": ln1_bias, "qkv_weight": qkv_weight, "query_bias": query_bias, "value_bias": value_bias, "out_weight": out_weight, "out_bias": out_bias, "ln2_gain": ln2_gain, "ln2_bias": ln2_bias, "up_weight": up_weight, "up_bias": up_bias, "down_weight": down_weight, "down_bias": down_bias, "out_grad": out_grad}


@jax.custom_vjp
def low(v):
    return lax.optimization_barrier(v.astype(jnp.bfloat16)).astype(jnp.float32)

@jax.custom_vjp
def low_back(v):
    return v

def low_keep(v):
    return (low(v), None)

def low_pass(kept, grad):
    return (grad,)

def back_keep(v):
    return (v, None)

def back_low(kept, grad):
    return (low(grad),)
low.defvjp(low_keep, low_pass)
low_back.defvjp(back_keep, back_low)

def matmul(left, right):
    return jnp.dot(left, right, precision=lax.Precision.HIGHEST, preferred_element_type=jnp.float32)

def normalize(rows):
    centered = rows - lax.optimization_barrier(jnp.mean(rows, axis=-1, keepdims=True))
    spread = lax.optimization_barrier(jnp.mean(centered * centered, axis=-1, keepdims=True))
    return centered * lax.rsqrt(spread + 1e-05)

def layer_forward(traj_tokens, params, traj_index, usable):
    ln1_g, ln1_c, qkv_w, query_b, value_b, out_w, out_b, ln2_g, ln2_c, up_w, up_b, down_w, down_projection_bias = params
    traj_num = traj_index.shape[0]
    gathered = jnp.take_along_axis(traj_tokens, traj_index[:, :, None], axis=1) * usable[:, :, None]
    gathered = gathered.reshape(-1, D)
    first_in = low(normalize(gathered) * ln1_g + ln1_c)
    bias_row = jnp.concatenate([query_b, jnp.zeros_like(query_b), value_b])
    qkv_all = low_back(low(matmul(first_in, qkv_w) + bias_row))
    qkv_all = qkv_all.reshape(traj_num, CAP, 3, HEADS, HEAD).transpose(2, 0, 3, 1, 4)
    queries, key_rows, values = (qkv_all[0], qkv_all[1], qkv_all[2])
    scores = jnp.einsum('thqe,thke->thqk', queries, key_rows, precision=lax.Precision.HIGHEST)
    scores = low_back(scores * HEAD ** (-0.5))
    scores = jnp.where(usable[:, None, None, :] > 0, scores, -1e+30)
    top_score = lax.optimization_barrier(jnp.max(scores, axis=-1, keepdims=True))
    raised = jnp.exp(scores - top_score)
    attn_probs = raised / lax.optimization_barrier(jnp.sum(raised, axis=-1, keepdims=True))
    attended = jnp.einsum('thqk,thke->thqe', low(attn_probs), values, precision=lax.Precision.HIGHEST)
    attended = low_back(low(attended))
    attended = attended.transpose(0, 2, 1, 3).reshape(-1, D)
    hidden_layer_rows = gathered + low_back(matmul(attended, out_w) + out_b)
    second_in = low(normalize(hidden_layer_rows) * ln2_g + ln2_c)
    pre_act = low_back(matmul(second_in, up_w) + up_b)
    activated = low(jax.nn.gelu(pre_act, approximate=True))
    mlp_rows = low_back(matmul(activated, down_w) + down_projection_bias)
    final_rows = (hidden_layer_rows + mlp_rows) * usable.reshape(-1, 1)
    return final_rows.reshape(traj_num, CAP, D)

def reference(tokens, visible_index, visible_count, ln1_gain, ln1_bias, qkv_weight, query_bias, value_bias, out_weight, out_bias, ln2_gain, ln2_bias, up_weight, up_bias, down_weight, down_bias, out_grad):
    weights = tuple((w.astype(jnp.float32) for w in (ln1_gain, ln1_bias, qkv_weight, query_bias, value_bias, out_weight, out_bias, ln2_gain, ln2_bias, up_weight, up_bias, down_weight, down_bias)))
    groups = tokens.shape[0] // TRAJ_DEV

    def shaped(array):
        return array.reshape((groups, TRAJ_DEV) + array.shape[1:])

    def one_group(totals, batch):
        traj_tokens, traj_index, traj_count, traj_cotan = batch
        usable = (jnp.arange(CAP, dtype=jnp.int32)[None, :] < traj_count[:, None]).astype(jnp.float32)

        def forward(tokens_float, params):
            return layer_forward(tokens_float, params, traj_index, usable)
        result, pullback = jax.vjp(forward, traj_tokens.astype(jnp.float32), weights)
        tok_grad, param_grads = pullback(traj_cotan.astype(jnp.float32))
        totals = tuple((a + b for a, b in zip(totals, param_grads)))
        return (totals, (result.astype(jnp.bfloat16), tok_grad.astype(jnp.bfloat16)))
    initial = tuple((jnp.zeros_like(w) for w in weights))
    totals, (outputs, grads_tok) = lax.scan(one_group, initial, (shaped(tokens), shaped(visible_index), shaped(visible_count), shaped(out_grad)))
    layer_out = outputs.reshape(tokens.shape[0], CAP, D)
    tokens_grad = grads_tok.reshape(tokens.shape)
    return (layer_out, tokens_grad, totals[0], totals[1], totals[2], totals[3], totals[4], totals[5], totals[6], totals[7], totals[8], totals[9], totals[10], totals[11], totals[12])
```

```python
import jax
import jax.numpy as jnp
from jax import lax
from jax.experimental import pallas as pl
from jax.experimental.pallas import tpu as pltpu
from jax.sharding import Mesh, PartitionSpec as P

AXES = ("wide", "square", "core")
HEADS = 4
EPS = 1e-05
BIN = 128
PAIR = 2 * BIN
BINS = 4
TILE = BINS * BIN
BINS_A = 8
TILE_A = BINS_A * BIN
F32 = jnp.float32
BF16 = jnp.bfloat16
GELU_A = 0.7978845608028654
GELU_B = 0.044715 * GELU_A

NN = (((1,), (0,)), ((), ()))
NT = (((1,), (1,)), ((), ()))
TN = (((0,), (0,)), ((), ()))

MIB = 1024 * 1024
HBM = pl.BlockSpec(memory_space=pl.ANY)


def mm(left, right, dims=NN):
    return lax.dot_general(left, right, dims, preferred_element_type=F32)


class Meta:
    def __init__(self, ref, traj):
        self.ref = ref
        self.width = traj + 8

    @staticmethod
    def size(traj):
        return 4 * (traj + 8) + 16

    def bin(self, b):
        return tuple(self.ref[j * self.width + b] for j in range(4))

    def put(self, b, *values):
        for j, value in enumerate(values):
            self.ref[j * self.width + b] = value

    @property
    def tiles_at(self):
        return 4 * self.width

    def tiles(self):
        return self.ref[self.tiles_at]

    def bit(self, b):
        return self.ref[self.tiles_at + 1 + b]


def plan_kernel(count_ref, rank_ref, meta_ref, first_ref, order_ref):
    traj = count_ref.shape[0]
    top = first_ref.shape[0]
    meta = Meta(meta_ref, traj)

    def clear(v, carry):
        first_ref[v] = 0
        return carry

    lax.fori_loop(0, top, clear, 0, unroll=16)

    def tally(t, carry):
        c = count_ref[t]
        first_ref[c] = first_ref[c] + 1
        return carry

    lax.fori_loop(0, traj, tally, 0, unroll=8)

    def starts(i, run):
        v = top - 1 - i
        n = first_ref[v]
        first_ref[v] = run
        return run + n

    lax.fori_loop(0, top, starts, 0, unroll=16)

    def place(t, carry):
        c = count_ref[t]
        at = first_ref[c]
        order_ref[at] = t
        first_ref[c] = at + 1
        return carry

    lax.fori_loop(0, traj, place, 0, unroll=8)

    def pair(carry):
        hi, lo, n = carry
        t_hi = order_ref[hi]
        t_lo = order_ref[lo]
        c_hi = count_ref[t_hi]
        c_lo = count_ref[t_lo]
        fits = jnp.logical_and(hi < lo, c_hi + c_lo <= BIN)
        meta.put(n, t_hi, jnp.where(fits, t_lo, t_hi), c_hi, jnp.where(fits, c_lo, 0))
        return hi + 1, jnp.where(fits, lo - 1, lo), n + 1

    _, _, n = lax.while_loop(lambda c: c[0] <= c[1], pair, (jnp.int32(0), jnp.int32(traj - 1), jnp.int32(0)))
    last = meta_ref[n - 1]
    for j in range(BINS_A - 1):
        meta.put(n + j, last, last, 0, 0)
    meta_ref[meta.tiles_at] = lax.shift_right_logical(n + BINS - 1, BINS.bit_length() - 1)
    for b in range(15):
        meta_ref[meta.tiles_at + 1 + b] = jnp.bitwise_and(lax.shift_right_logical(rank_ref[0], b), 1)


def make_plan(counts, rank, slots):
    traj = counts.shape[0]
    smem = pl.BlockSpec(memory_space=pltpu.SMEM)
    return pl.pallas_call(
        plan_kernel,
        in_specs=[smem, smem],
        out_specs=smem,
        out_shape=jax.ShapeDtypeStruct((Meta.size(traj),), jnp.int32),
        scratch_shapes=[pltpu.SMEM((-(-(slots + 1) // 16) * 16,), jnp.int32), pltpu.SMEM((traj,), jnp.int32)],
        name="plan",
    )(counts, rank)


def bin_onehot(idx_ref, ta, tb, ca, cb, seq):
    lane = lax.broadcasted_iota(jnp.int32, (8, BIN), 1)
    ia = jnp.broadcast_to(idx_ref[pl.ds(ta, 1), :], (8, BIN))
    ib = jnp.broadcast_to(idx_ref[pl.ds(tb, 1), :], (8, BIN))
    ib = pltpu.roll(ib, ca, 1)
    code = jnp.where(lane < ca, ia, jnp.where(lane < ca + cb, ib + seq, -1))[0:1, :]
    pos = lax.broadcasted_iota(jnp.int32, (2 * seq, BIN), 0)
    return jnp.where(pos == code, 1.0, 0.0).astype(BF16)


def bin_slots(ca, cb):
    row = lax.broadcasted_iota(jnp.int32, (BIN, BIN), 0)
    lane = lax.broadcasted_iota(jnp.int32, (BIN, BIN), 1)
    first = jnp.logical_and(lane == row, row < ca)
    second = jnp.logical_and(lane == row + ca, row < cb)
    return jnp.concatenate([jnp.where(x, 1.0, 0.0).astype(BF16) for x in (first, second)], axis=0)


def bin_mask(ca, cb):
    row = lax.broadcasted_iota(jnp.int32, (BIN, BIN), 0)
    lane = lax.broadcasted_iota(jnp.int32, (BIN, BIN), 1)
    key = jnp.where(row < ca, 0, jnp.where(row < ca + cb, 1, 2))
    query = jnp.where(lane < ca, 0, jnp.where(lane < ca + cb, 1, 3))
    return jnp.where(key == query, 0.0, -1e30)


def center(x):
    mean = jnp.mean(x, axis=0, keepdims=True)
    xc = x - mean
    var = jnp.mean(xc * xc, axis=0, keepdims=True)
    rstd = lax.rsqrt(var + EPS)
    return xc * rstd, rstd


def lanes_into_rows(acc):
    return jnp.sum(acc.T, axis=0, keepdims=True)


def two(x):
    return jnp.concatenate([x, x], axis=1)


def bin_lanes(b):
    return slice(b * BIN, (b + 1) * BIN)


def pair_lanes(t):
    return slice(t * PAIR, (t + 1) * PAIR)


def departures(meta, tile, rows_s, slot, to_ref, rows, sems, act):
    half = rows_s.shape[2] // 2
    for b in range(BINS):
        ta, tb, ca, cb = meta.bin(tile * BINS + b)
        for part, (t, c) in enumerate(((ta, ca), (tb, cb))):

            @pl.when(c > 0)
            def _():
                act(
                    pltpu.make_async_copy(
                        rows_s.at[slot, b, pl.ds(part * half, rows)], to_ref.at[t], sems.at[slot, b, part]
                    )
                )


class Share:
    def __init__(self, first, last):
        self.first, self.last = first, last

    def start(self, tiles):
        return lax.shift_right_logical(tiles * self.first, 4)

    def stop(self, tiles):
        return lax.shift_right_logical(tiles * self.last, 4)

    def most(self, fewest, most):
        return max((n * self.last >> 4) - (n * self.first >> 4) for n in range(fewest, most + 1))

    def block(self, tiles_at):
        return lambda i, meta: jnp.minimum(self.start(meta[tiles_at]) + i, self.stop(meta[tiles_at]) - 1)


def shares(*cuts):
    return [Share(a, b) for a, b in zip(cuts[:-1], cuts[1:])]


def keep_half(meta, acc_s, keep_ref, send_ref):
    half = keep_ref.shape[0]
    core = meta.bit(CORE)
    keep_ref[...] = acc_s[pl.ds(pl.multiple_of(core * half, 8), half), :]
    send_ref[...] = acc_s[pl.ds(pl.multiple_of((1 - core) * half, 8), half), :]


def late_kernel(
    meta_ref,
    idx_ref,
    tok_ref,
    og_ref,
    g1_ref,
    c1_ref,
    bq_ref,
    bv_ref,
    bo_ref,
    g2_ref,
    c2_ref,
    bup_ref,
    wqkv_ref,
    wo_ref,
    wup_ref,
    wdn_ref,
    wdnt_s,
    nhat1_ref,
    rstd1_ref,
    qkv_ref,
    prob_ref,
    gatt_ref,
    gmid_ref,
    act_ref,
    mid_ref,
    keep_ref,
    send_ref,
    dvec_ref,
    tok_s,
    og_s,
    in_sem,
    idx_s,
    vec_s,
    col_s,
    wqkvt_s,
    wot_s,
    wupt_s,
    gath_s,
    first_s,
    bd_s,
    score_s,
    att_s,
    nhat_s,
    sec_s,
    gm_s,
    u_s,
    ga_s,
    gp_s,
    gb_s,
    gs_s,
    acc_s,
    bacc_s,
):
    step = pl.program_id(0)
    traj, seq, d = tok_ref.shape
    slots = og_ref.shape[1]
    ff = wup_ref.shape[1]
    hs = d // HEADS
    scale = hs**-0.5
    meta = Meta(meta_ref, traj)
    steps = lax.shift_right_logical(meta.tiles() + 1, 1)

    def arrivals(i, act):
        slot = jnp.bitwise_and(i, 1)
        for b in range(BINS_A):
            for part, t in enumerate(meta.bin(i * BINS_A + b)[0:2]):
                sems = in_sem.at[slot, b, part]
                act(pltpu.make_async_copy(tok_ref.at[t], tok_s.at[slot, b, pl.ds(part * seq, seq)], sems.at[0]))
                act(pltpu.make_async_copy(og_ref.at[t], og_s.at[slot, b, pl.ds(part * BIN, slots)], sems.at[1]))

    @pl.when(step == 0)
    def _():
        for part in range(2):
            og_s[:, :, part * BIN + slots : (part + 1) * BIN, :] = jnp.zeros((2, BINS_A, BIN - slots, d), BF16)
        arrivals(0, lambda c: c.start())
        idx_s[...] = jnp.zeros_like(idx_s)
        idx_s[:, 0:slots] = idx_ref[...]
        vec_s[...] = jnp.zeros_like(vec_s)
        rows = [(0, g1_ref), (1, c1_ref), (2, bq_ref), (4, bv_ref), (5, bo_ref), (6, g2_ref), (7, c2_ref)]
        for j, ref in rows:
            vec_s[j : j + 1, :] = ref[...].astype(F32).reshape(1, d)
        for j in range(ff // d):
            vec_s[8 + j : 9 + j, :] = bup_ref[j * d : (j + 1) * d].astype(F32).reshape(1, d)
        vec_s[2:3, :] = vec_s[2:3, :] * scale
        cols = vec_s[...].T
        for j in range(12):
            col_s[j * d : (j + 1) * d, :] = jnp.broadcast_to(cols[:, j : j + 1], (d, BIN))
        wqkvt_s[...] = wqkv_ref[...].T
        wqkvt_s[0:d, :] = (wqkvt_s[0:d, :].astype(F32) * scale).astype(BF16)
        wot_s[...] = wo_ref[...].T
        wupt_s[...] = wup_ref[...].T
        wdnt_s[...] = wdn_ref[...].T
        bd_s[...] = jnp.zeros_like(bd_s)
        bacc_s[...] = jnp.zeros_like(bacc_s)
        acc_s[...] = jnp.zeros_like(acc_s)

    def col(j, n=1):
        return col_s[j * d : (j + n) * d, :]

    @pl.when(step < steps)
    def _():
        slot = jnp.bitwise_and(step, 1)
        arrivals(step, lambda c: c.wait())

        @pl.when(step + 1 < steps)
        def _():
            arrivals(step + 1, lambda c: c.start())

        metas = [meta.bin(step * BINS_A + b) for b in range(BINS_A)]
        rstds = {}

        def gather(b):
            lanes = bin_lanes(b)
            gath_s[:, lanes] = mm(tok_s[slot, b], bin_onehot(idx_s, *metas[b], seq), TN)

        def first_norm(b):
            lanes = bin_lanes(b)
            nhat, rstd = center(gath_s[:, lanes])
            nhat1_ref[0, :, lanes] = nhat.astype(BF16)
            rstd1_ref[0, :, lanes] = jnp.broadcast_to(rstd, (8, BIN))
            first_s[:, lanes] = (nhat * col(0) + col(1)).astype(BF16)

        def cotangent(b):
            gm_s[:, bin_lanes(b)] = mm(og_s[slot, b], bin_slots(*metas[b][2:]), TN).astype(BF16)

        def project(t):
            lanes = pair_lanes(t)
            qkv_ref[0, :, lanes] = (mm(wqkvt_s[...], first_s[:, lanes]) + two(col(2, 3))).astype(BF16)

        def scores(b, p):
            lanes = bin_lanes(b)
            f0 = p * 2 * hs
            at = b * (HEADS // 2) + p
            bd_s[at, 0:hs, 0:BIN] = qkv_ref[0, f0 : f0 + hs, lanes]
            bd_s[at, hs : 2 * hs, BIN:PAIR] = qkv_ref[0, f0 + hs : f0 + 2 * hs, lanes]
            score_s[at] = mm(qkv_ref[0, d + f0 : d + f0 + 2 * hs, lanes], bd_s[at], TN)

        def softmax(b):
            mask = two(bin_mask(*metas[b][2:]))
            for p in range(HEADS // 2):
                s = score_s[b * (HEADS // 2) + p] + mask
                e = jnp.exp(s - jnp.max(s, axis=0, keepdims=True))
                prob_ref[0, b, :, pair_lanes(p)] = (e * (1.0 / jnp.sum(e, axis=0, keepdims=True))).astype(BF16)

        def attend(b, p):
            lanes = bin_lanes(b)
            f0 = p * 2 * hs
            both = mm(qkv_ref[0, 2 * d + f0 : 2 * d + f0 + 2 * hs, lanes], prob_ref[0, b, :, pair_lanes(p)])
            for h in range(2):
                att_s[f0 + h * hs : f0 + (h + 1) * hs, lanes] = both[h * hs : (h + 1) * hs, bin_lanes(h)].astype(BF16)

        def residual(t):
            lanes = pair_lanes(t)
            mid_ref[0, :, lanes] = mm(wot_s[...], att_s[:, lanes])

        def second_norm(b):
            lanes = bin_lanes(b)
            mid = mid_ref[0, :, lanes] + gath_s[:, lanes] + col(5)
            mid_ref[0, :, lanes] = mid
            nhat, rstds[b] = center(mid)
            nhat_s[:, lanes] = nhat
            sec_s[:, lanes] = (nhat * col(6) + col(7)).astype(BF16)

        def up(t):
            lanes = pair_lanes(t)
            u_s[:, lanes] = mm(wupt_s[...], sec_s[:, lanes])
            ga_s[:, lanes] = mm(wdn_ref[...], gm_s[:, lanes])

        def gelu(t, rows):
            lanes = pair_lanes(t)
            u = u_s[rows, lanes] + two(col_s[8 * d + rows.start : 8 * d + rows.stop, :])
            q = u * u * GELU_B + GELU_A
            sg = 0.5 * jnp.tanh(u * q) + 0.5
            act = u * sg
            gp = (act * (1.0 - sg) * (6.0 * q - 4.0 * GELU_A) + sg) * ga_s[rows, lanes]
            act_ref[0, rows, lanes] = act.astype(BF16)
            gp_s[rows, lanes] = gp.astype(BF16)
            bacc_s[d + rows.start : d + rows.stop, :] += gp[:, 0:BIN] + gp[:, BIN:PAIR]

        def down(t):
            lanes = pair_lanes(t)
            gs_s[:, lanes] = mm(wup_ref[...], gp_s[:, lanes])

        def second_norm_back(b):
            lanes = bin_lanes(b)
            gs = gs_s[:, lanes]
            nhat = nhat_s[:, lanes]
            bacc_s[0:d, :] += gs * nhat
            a = gs * col(6)
            m1 = jnp.mean(a, axis=0, keepdims=True)
            m2 = jnp.mean(a * nhat, axis=0, keepdims=True)
            gm = gm_s[:, lanes].astype(F32)
            gmid = gm + rstds[b] * (a - m1 - nhat * m2)
            gmid_ref[0, :, lanes] = gmid
            gb_s[:, lanes] = gmid.astype(BF16)
            bacc_s[d + ff : 2 * d + ff, :] += gm
            bacc_s[2 * d + ff : 3 * d + ff, :] += gmid

        def grad_attended(t):
            lanes = pair_lanes(t)
            gatt_ref[0, :, lanes] = mm(wo_ref[...], gb_s[:, lanes]).astype(BF16)

        def work(count):
            bins, tiles, chunk, lanes = range(count), range(count // 2), 32, slice(0, count * BIN)
            for b in bins:
                gather(b)
            for b in bins:
                cotangent(b)
            for b in bins:
                first_norm(b)
            for t in tiles:
                project(t)
            pairs = [(b, p) for b in bins for p in range(HEADS // 2)]
            for b, p in pairs:
                scores(b, p)
            for b in bins:
                softmax(b)
            for b, p in pairs:
                attend(b, p)
            for t in tiles:
                residual(t)
            for b in bins:
                second_norm(b)
            for t in tiles:
                up(t)
            for t in tiles:
                for j in range(ff // chunk):
                    gelu(t, slice(j * chunk, (j + 1) * chunk))
            acc_s[0:ff, :] += mm(act_ref[0, :, lanes], gm_s[:, lanes], NT)
            acc_s[ff : 2 * ff, :] += mm(gp_s[:, lanes], sec_s[:, lanes], NT)
            for t in tiles:
                down(t)
            for b in bins:
                second_norm_back(b)
            acc_s[2 * ff : 2 * ff + d, :] += mm(att_s[:, lanes], gb_s[:, lanes], NT)
            for t in tiles:
                grad_attended(t)

        full = 2 * step + 1 < meta.tiles()

        @pl.when(full)
        def _():
            work(BINS_A)

        @pl.when(jnp.logical_not(full))
        def _():
            work(BINS)

        @pl.when(step == steps - 1)
        def _():
            dvec_ref[...] = jnp.zeros_like(dvec_ref)
            keep_half(meta, acc_s, keep_ref, send_ref)
            for j in range(7):
                dvec_ref[j : j + 1, :] = lanes_into_rows(bacc_s[j * d : (j + 1) * d, :])


def attention_kernel(
    traj,
    meta_ref,
    nhat1_ref,
    qkv_ref,
    prob_ref,
    gatt_ref,
    dvec_ref,
    gq_ref,
    keep_ref,
    send_ref,
    bd_s,
    bdq_s,
    dp_s,
    ds_s,
    bacc_s,
    acc_s,
):
    step = pl.program_id(0)
    d = nhat1_ref.shape[1]
    hs = d // HEADS
    scale = hs**-0.5
    meta = Meta(meta_ref, traj)

    @pl.when(step == 0)
    def _():
        bd_s[...] = jnp.zeros_like(bd_s)
        bdq_s[...] = jnp.zeros_like(bdq_s)
        bacc_s[...] = jnp.zeros_like(bacc_s)
        acc_s[...] = jnp.zeros_like(acc_s)

    def work(count):
        pairs = [(b, p * 2 * hs, b * (HEADS // 2) + p, p) for b in range(count) for p in range(HEADS // 2)]
        for b, f0, at, _ in pairs:
            lanes = bin_lanes(b)
            bd_s[at, 0:hs, 0:BIN] = gatt_ref[0, f0 : f0 + hs, lanes]
            bd_s[at, hs : 2 * hs, BIN:PAIR] = gatt_ref[0, f0 + hs : f0 + 2 * hs, lanes]
            bdq_s[at, 0:hs, 0:BIN] = qkv_ref[0, f0 : f0 + hs, lanes]
            bdq_s[at, hs : 2 * hs, BIN:PAIR] = qkv_ref[0, f0 + hs : f0 + 2 * hs, lanes]
        for b, f0, at, _ in pairs:
            dp_s[at] = mm(qkv_ref[0, 2 * d + f0 : 2 * d + f0 + 2 * hs, bin_lanes(b)], bd_s[at], TN)
        for b, f0, at, p in pairs:
            pr = prob_ref[0, b, :, pair_lanes(p)].astype(F32)
            t = pr * dp_s[at]
            ds_s[at] = (t - pr * jnp.sum(t, axis=0, keepdims=True)).astype(BF16)

        def put(b, row, part):
            gq_ref[0, row : row + 2 * hs, bin_lanes(b)] = part.astype(BF16)
            bacc_s[row : row + 2 * hs, :] += part

        for b, f0, at, _ in pairs:
            both = mm(qkv_ref[0, d + f0 : d + f0 + 2 * hs, bin_lanes(b)], ds_s[at]) * scale
            put(b, f0, jnp.concatenate([both[0:hs, 0:BIN], both[hs : 2 * hs, BIN:PAIR]], axis=0))
        for b, f0, at, _ in pairs:
            put(b, d + f0, mm(bdq_s[at], ds_s[at], NT))
        for b, f0, at, p in pairs:
            put(b, 2 * d + f0, mm(bd_s[at], prob_ref[0, b, :, pair_lanes(p)], NT))
        lanes = slice(0, count * BIN)
        acc_s[0 : 3 * d, :] += mm(gq_ref[0, :, lanes], nhat1_ref[0, :, lanes], NT)

    @pl.when(2 * step + 1 < meta.tiles())
    def _():
        work(BINS_A)

    @pl.when(2 * step + 1 == meta.tiles())
    def _():
        work(BINS)

    @pl.when(step == pl.num_programs(0) - 1)
    def _():
        for j in range(3):
            acc_s[3 * d + j : 3 * d + j + 1, :] = lanes_into_rows(bacc_s[j * d : (j + 1) * d, :])
        acc_s[3 * d + 3 : 3 * d + 11, :] = dvec_ref[...]
        keep_half(meta, acc_s, keep_ref, send_ref)


def token_kernel(share, meta_ref, idx_ref, g1_ref, wqkv_ref, nhat1_ref, rstd1_ref, gq_ref, gmid_ref, *refs):
    tg_ref, idx_s, col_s, gg_s, rows_s, sems = refs[-6:]
    step = pl.program_id(0)
    traj, slots = idx_ref.shape
    seq, d = tg_ref.shape[1:]
    meta = Meta(meta_ref, traj)

    @pl.when(step == 0)
    def _():
        idx_s[...] = jnp.zeros_like(idx_s)
        idx_s[:, 0:slots] = idx_ref[...]
        row = jnp.broadcast_to(g1_ref[...].astype(F32).reshape(1, d), (8, d))
        col_s[...] = jnp.broadcast_to(row.T[:, 0:1], (d, BIN))

    def rows_of(tile, slot):
        gfs = [mm(wqkv_ref[...], gq_ref[0, :, pair_lanes(t)]) for t in range(BINS // 2)]
        for b in range(BINS):
            lanes = bin_lanes(b)
            nhat = nhat1_ref[0, :, lanes].astype(F32)
            a = gfs[b // 2][:, bin_lanes(b % 2)] * col_s[...]
            m1 = jnp.mean(a, axis=0, keepdims=True)
            m2 = jnp.mean(a * nhat, axis=0, keepdims=True)
            rstd = rstd1_ref[0, 0:1, lanes]
            gg_s[:, lanes] = (gmid_ref[0, :, lanes] + rstd * (a - m1 - nhat * m2)).astype(BF16)
        for b in range(BINS):
            onehot = bin_onehot(idx_s, *meta.bin(tile * BINS + b), seq)
            rows_s[slot, b] = mm(onehot, gg_s[:, bin_lanes(b)], NT).astype(BF16)

    store_tiles(share, meta, step, rows_of, rows_s, tg_ref, seq, sems)


def store_tiles(share, meta, step, rows_of, rows_s, to_ref, rows, sems):
    first, stop = share.start(meta.tiles()), share.stop(meta.tiles())
    tile = first + step
    slot = jnp.bitwise_and(step, 1)

    def leave(tile, slot, act):
        departures(meta, tile, rows_s, slot, to_ref, rows, sems, act)

    @pl.when(tile < stop)
    def _():
        @pl.when(step >= 2)
        def _():
            leave(tile - 2, slot, lambda c: c.wait())

        rows_of(tile, slot)
        leave(tile, slot, lambda c: c.start())

    @pl.when(step == pl.num_programs(0) - 1)
    def _():
        done = stop - first

        @pl.when(done >= 2)
        def _():
            leave(stop - 2, jnp.bitwise_and(done, 1), lambda c: c.wait())

        leave(stop - 1, jnp.bitwise_and(done - 1, 1), lambda c: c.wait())


def output_kernel(share, traj, meta_ref, bdn_ref, wdnt_ref, act_ref, mid_ref, *refs):
    lay_ref, col_s, y_s, rows_s, sems = refs[-5:]
    step = pl.program_id(0)
    slots, d = lay_ref.shape[1:]
    meta = Meta(meta_ref, traj)

    @pl.when(step == 0)
    def _():
        row = jnp.broadcast_to(bdn_ref[...].astype(F32).reshape(1, d), (8, d))
        col_s[...] = jnp.broadcast_to(row.T[:, 0:1], (d, BIN))

    def rows_of(tile, slot):
        for t in range(BINS // 2):
            lanes = pair_lanes(t)
            mlp = mm(wdnt_ref[...], act_ref[0, :, lanes])
            y_s[:, lanes] = (mlp + mid_ref[0, :, lanes] + two(col_s[...])).astype(BF16)
        for b in range(BINS):
            _, _, ca, cb = meta.bin(tile * BINS + b)
            rows_s[slot, b] = mm(bin_slots(ca, cb), y_s[:, bin_lanes(b)], NT).astype(BF16)

    store_tiles(share, meta, step, rows_of, rows_s, lay_ref, slots, sems)


CORE, Y, X, Z = 0, 1, 2, 3


def row_at(const=0, **bits):
    return const, tuple(({"core": CORE, "y": Y, "x": X, "z": Z}[name], coef) for name, coef in bits.items())


def mine(bit, rows, base=0):
    return base, ((bit, rows),)


def other(bit, rows, base=0):
    return base + rows, ((bit, -rows),)


class Step:
    def __init__(self, inputs, out_rows, parts, sends=()):
        self.inputs, self.out_rows, self.parts, self.sends = list(inputs), list(out_rows), list(parts), dict(sends)


def combine_kernel(step, bits_at, meta_ref, *refs):
    ins, outs = refs[: len(step.inputs)], refs[len(step.inputs) :]

    def row(start):
        if isinstance(start, int):
            return start
        const, bits = start
        for bit, coef in bits:
            const = const + meta_ref[bits_at + bit] * coef
        return const

    def rows(start, n):
        return pl.ds(start if isinstance(start, int) else pl.multiple_of(start, 8), n)

    for n, terms, goes in step.parts:
        for out, start, first, count in goes:
            total = None
            for ref, at in terms:
                term = ins[ref][rows(row(at) + row(first), count), :]
                total = term if total is None else total + term
            outs[out][rows(row(start), count), :] = total


def combine(step, meta, bits_at, width):
    vmem = pl.BlockSpec(memory_space=pltpu.VMEM)
    return pl.pallas_call(
        lambda *refs: combine_kernel(step, bits_at, *refs),
        in_specs=[pl.BlockSpec(memory_space=pltpu.SMEM)] + [vmem] * len(step.inputs),
        out_specs=[vmem] * len(step.out_rows),
        out_shape=[jax.ShapeDtypeStruct((n, width), F32) for n in step.out_rows],
        compiler_params=pltpu.CompilerParams(vmem_limit_bytes=2 * MIB),
        name="combine",
    )(meta, *step.inputs)


def bucket_sum(bits, keep, send, half, halve_z):
    q, e, f = half // 4, half // 8, half // 16
    _, (got,) = yield Step([send], [], [], {0: CORE})
    (k0, k1, _, _), (g0, g1) = yield Step(
        [keep, got],
        [q, q, q, q],
        [
            (2 * q, [(0, row_at()), (1, row_at())], [(0, row_at(), mine(X, q), q), (2, row_at(), other(X, q), q)]),
            (
                2 * q,
                [(0, row_at(2 * q)), (1, row_at(2 * q))],
                [(1, row_at(), mine(Y, q), q), (3, row_at(), other(Y, q), q)],
            ),
        ],
        {2: X, 3: Y},
    )
    (a0, a1, _, _), (g0, g1) = yield Step(
        [k0, k1, g0, g1],
        [e, e, e, e],
        [
            (q, [(0, row_at()), (2, row_at())], [(0, row_at(), mine(Y, e), e), (2, row_at(), other(Y, e), e)]),
            (q, [(1, row_at()), (3, row_at())], [(1, row_at(), mine(X, e), e), (3, row_at(), other(X, e), e)]),
        ],
        {2: Y, 3: X},
    )
    if halve_z:
        (z, _), (got,) = yield Step(
            [a0, a1, g0, g1],
            [e, e],
            [
                (
                    e,
                    [(c, row_at()), (2 + c, row_at())],
                    [(0, row_at(c * f), mine(Z, f), f), (1, row_at(c * f), other(Z, f), f)],
                )
                for c in range(2)
            ],
            {1: Z},
        )
        for bit in [*range(Z + 1, bits), Z]:
            (z,), (got,) = yield Step([z, got], [e], [(e, [(0, row_at()), (1, row_at())], [(0, row_at(), 0, e)])], {0: bit})
        (e0, e1), (g0, g1) = yield Step(
            [z, got],
            [e, e],
            [
                (f, [(ref, row_at(c * f))], [(c, side(Z, f), 0, f)])
                for ref, side in enumerate((mine, other))
                for c in range(2)
            ],
            {0: Y, 1: X},
        )
    else:
        (z,), (got,) = yield Step(
            [a0, a1, g0, g1],
            [2 * e],
            [(e, [(c, row_at()), (2 + c, row_at())], [(0, row_at(c * e), 0, e)]) for c in range(2)],
            {0: bits - 1},
        )
        for bit in range(bits - 2, Z - 1, -1):
            (z,), (got,) = yield Step(
                [z, got], [2 * e], [(2 * e, [(0, row_at()), (1, row_at())], [(0, row_at(), 0, 2 * e)])], {0: bit}
            )
        (e0, e1), (g0, g1) = yield Step(
            [z, got],
            [e, e],
            [(2 * e, [(0, row_at()), (1, row_at())], [(0, row_at(), 0, e), (1, row_at(), e, e)])],
            {0: Y, 1: X},
        )
    (f0, f1), (g0, g1) = yield Step(
        [e0, e1, g0, g1],
        [q, q],
        [
            (e, [(0, row_at())], [(0, mine(Y, e), 0, e)]),
            (e, [(2, row_at())], [(0, other(Y, e), 0, e)]),
            (e, [(1, row_at())], [(1, mine(X, e), 0, e)]),
            (e, [(3, row_at())], [(1, other(X, e), 0, e)]),
        ],
        {0: X, 1: Y},
    )
    (near,), (far,) = yield Step(
        [f0, f1, g0, g1],
        [half],
        [
            (q, [(0, row_at())], [(0, mine(X, q), 0, q)]),
            (q, [(2, row_at())], [(0, other(X, q), 0, q)]),
            (q, [(1, row_at())], [(0, mine(Y, q, 2 * q), 0, q)]),
            (q, [(3, row_at())], [(0, other(Y, q, 2 * q), 0, q)]),
        ],
        {0: CORE},
    )
    return near, far


class Sums:
    def __init__(self, ranks, meta, bits_at, width):
        self.ranks, self.meta, self.bits_at, self.width = ranks, meta, bits_at, width
        self.arrays, self.arrived, self.sent = [], [], []
        self.running, self.results = {}, {}

    def view(self, array):
        self.arrays.append(array)
        return (len(self.arrays) - 1, 0)

    def add(self, name, steps):
        self.running[name] = (steps, next(steps))

    def advance(self, after=None):
        if after is not None and self.arrived:
            tied = lax.optimization_barrier((*[self.arrays[k] for k in self.arrived], after))
            for k, array in zip(self.arrived, tied):
                self.arrays[k] = array
        inputs, out_rows, parts, places, sends = [], [], [], {}, {}
        for name, (_, step) in self.running.items():
            outs = []
            for out, rows in enumerate(step.out_rows):
                bit = step.sends.get(out)
                if bit in sends:
                    at = sends[bit]
                    outs.append((at, out_rows[at]))
                    out_rows[at] += rows
                    continue
                if bit is not None:
                    sends[bit] = len(out_rows)
                outs.append((len(out_rows), 0))
                out_rows.append(rows)
            places[name] = outs
            for rows, terms, goes in step.parts:
                moved = []
                for ref, (const, bits) in terms:
                    k, row = step.inputs[ref]
                    if k not in inputs:
                        inputs.append(k)
                    moved.append((inputs.index(k), (const + row, bits)))
                parts.append(
                    (
                        rows,
                        moved,
                        [(outs[out][0], (const + outs[out][1], bits), *rest) for out, (const, bits), *rest in goes],
                    )
                )
        base = len(self.arrays)
        if out_rows:
            merged = Step([self.arrays[k] for k in inputs], out_rows, parts)
            self.arrays += list(combine(merged, self.meta, self.bits_at, self.width))
        to_send = {bit: base + out for bit, out in sends.items()}
        raw = {name: step for name, (_, step) in self.running.items() if not step.parts}
        for step in raw.values():
            for out, bit in step.sends.items():
                to_send[(bit, id(step))] = step.inputs[out][0]
        self.sent = [self.arrays[k] for k in to_send.values()]
        received = {}
        for key, k in to_send.items():
            bit = key[0] if isinstance(key, tuple) else key
            perm = [(r, r ^ (1 << bit)) for r in range(self.ranks)]
            received[key] = self.view(lax.ppermute(self.arrays[k], AXES, perm))[0]
        self.arrived = list(received.values())
        for name, (steps, step) in list(self.running.items()):
            if name in raw:
                outs = []
                got = [(received[(bit, id(step))], 0) for bit in step.sends.values()]
            else:
                outs = [(base + out, row) for out, row in places[name]]
                got = [(received[bit], places[name][out][1]) for out, bit in step.sends.items()]
            try:
                self.running[name] = (steps, steps.send((outs, got)))
            except StopIteration as stop:
                self.results[name] = stop.value
                del self.running[name]

    def ordered(self, value):
        return lax.optimization_barrier((value, *self.sent))[0]


def finish_kernel(
    bits_at, rows_at, meta_ref, late0_ref, late1_ref, first0_ref, first1_ref, g1_ref, c1_ref, wqkv_ref, wup_ref,
    dwn_ref, dup_ref, dwo_ref, dqkv_ref, dg1_ref, dc1_ref, dbq_ref, dbv_ref, dbo_ref, dg2_ref, dc2_ref, dbup_ref, dbdn_ref,
    late_s, first_s, first_sem, late_sem, out_sem,
):
    ff, d = dwn_ref.shape
    core = meta_ref[bits_at + CORE]
    late_near, late_far, first_near, first_far = rows_at
    first, late = [], []
    for to_s, copies, sems, sides in (
        (late_s, late, late_sem, ((late0_ref, late_near, core), (late1_ref, late_far, 1 - core))),
        (first_s, first, first_sem, ((first0_ref, first_near, core), (first1_ref, first_far, 1 - core))),
    ):
        half = to_s.shape[0] // 2
        for k, (ref, row, side) in enumerate(sides):
            to = to_s.at[pl.ds(pl.multiple_of(side * half, 8), half)]
            copies.append(pltpu.make_async_copy(ref.at[pl.ds(row, half)], to, sems.at[k]))
    for copy in late + first:
        copy.start()
    for copy in late:
        copy.wait()
    copies = [
        pltpu.make_async_copy(late_s.at[pl.ds(0, ff)], dwn_ref, out_sem.at[0]),
        pltpu.make_async_copy(late_s.at[pl.ds(2 * ff, d)], dwo_ref, out_sem.at[1]),
    ]
    for copy in copies:
        copy.start()
    for j in range(ff // d):
        dup_ref[:, j * d : (j + 1) * d] = late_s[ff + j * d : ff + (j + 1) * d, :].T
    for copy in first:
        copy.wait()

    def late_row(j):
        return first_s[3 * d + 3 + j : 3 * d + 4 + j, :].reshape(d)

    dg2_ref[...] = late_row(0)
    for j in range(ff // d):
        dbup_ref[j * d : (j + 1) * d] = late_row(1 + j)
    dbdn_ref[...] = late_row(5)
    dbo_ref[...] = late_row(6)

    def times(weight_ref, row, n):
        total = jnp.zeros((8, d), F32)
        for j in range(n):
            left = jnp.broadcast_to(first_s[row + j : row + j + 1, :], (8, d))
            for _ in range(3):
                low = left.astype(BF16)
                left = left - low.astype(F32)
                total = total + mm(low, weight_ref[:, j * d : (j + 1) * d], NT)
        return total[0:1, :]

    dc2_ref[...] = times(wup_ref, 3 * d + 4, ff // d).reshape(d)
    dc1_ref[...] = times(wqkv_ref, 3 * d, 3).reshape(d)

    gain = jnp.broadcast_to(g1_ref[...].astype(F32).reshape(1, d), (8, d)).T[:, 0:1]
    bias = jnp.broadcast_to(c1_ref[...].astype(F32).reshape(1, d), (8, d)).T[:, 0:1]
    gain_grad = jnp.zeros((d, d), F32)
    for j in range(3):
        block = slice(j * d, (j + 1) * d)
        total = first_s[3 * d + j : 3 * d + j + 1, :]
        product = first_s[block, :].T
        weight = wqkv_ref[:, block].astype(F32)
        dqkv_ref[:, block] = gain * product + bias * total
        gain_grad += weight * product
    dg1_ref[...] = jnp.sum(gain_grad.T, axis=0, keepdims=True).reshape(d)
    dbq_ref[...] = first_s[3 * d : 3 * d + 1, :].reshape(d)
    dbv_ref[...] = first_s[3 * d + 2 : 3 * d + 3, :].reshape(d)
    for copy in copies:
        copy.wait()


def whole(shape):
    zeros = (0,) * len(shape)
    return pl.BlockSpec(shape, lambda i, *_: zeros, pipeline_mode=pl.Buffered(1))


def per_step(shape, at):
    rest = (0,) * len(shape)
    return pl.BlockSpec((1,) + shape, lambda i, meta: (at(i, meta),) + rest)


def per_tile(shape, at):
    axis = 0 if len(shape) == 3 else len(shape) - 1

    def index(i, meta):
        tile = at(i, meta)
        place = [0] * len(shape)
        place[axis] = jnp.bitwise_and(tile, 1)
        return (lax.shift_right_logical(tile, 1), *place)

    return pl.BlockSpec((1,) + shape, index)


def doubled(shape):
    if len(shape) == 3:
        return (2 * shape[0],) + shape[1:]
    return shape[:-1] + (2 * shape[-1],)


SHARES_C = shares(0, 5, 8, 10, 16)
SHARES_D = shares(0, 6, 9, 16)


def strided(first, pieces, tiles_at, halved=0):
    def at(i, meta):
        bits = pieces.bit_length() - 1
        count = lax.shift_right_logical(meta[tiles_at] + halved, halved)
        last = first + lax.shift_left(lax.shift_right_logical(count - 1 - first, bits), bits)
        return jnp.minimum(i * pieces + first, last)

    return at


def body(
    ranks,
    tokens,
    visible_index,
    visible_count,
    ln1_gain,
    ln1_bias,
    qkv_weight,
    query_bias,
    value_bias,
    out_weight,
    out_bias,
    ln2_gain,
    ln2_bias,
    up_weight,
    up_bias,
    down_weight,
    down_bias,
    out_grad,
):
    traj, slots = visible_index.shape
    seq, d = tokens.shape[1:]
    ff = up_weight.shape[1]
    hs = d // HEADS
    steps_a = -(-traj // BINS_A)
    tiles = 2 * steps_a
    tiles_at = Meta.size(traj) - 16
    bits = ranks.bit_length() - 1
    rank = lax.axis_index(AXES).astype(jnp.int32).reshape(1)
    meta = make_plan(visible_count, rank, slots)
    sums = Sums(ranks, meta, tiles_at + 1, d)

    shapes = dict(
        nhat=((d, TILE), BF16),
        rstd=((8, TILE), F32),
        qkv=((3 * d, TILE), BF16),
        prob=((BINS, BIN, HEADS * BIN), BF16),
        gatt=((d, TILE), BF16),
        gmid=((d, TILE), F32),
        act=((ff, TILE), BF16),
        mid=((d, TILE), F32),
    )

    def stored(name):
        shape, kind = shapes[name]
        return jax.ShapeDtypeStruct((steps_a,) + doubled(shape), kind)

    at_a = strided(0, 1, tiles_at, 1)

    def params(mib):
        return pltpu.CompilerParams(dimension_semantics=("arbitrary",), vmem_limit_bytes=mib * MIB)

    late_shape = (2 * ff + d, d)
    vectors = [ln1_gain, ln1_bias, query_bias, value_bias, out_bias, ln2_gain, ln2_bias, up_bias]
    weights = [qkv_weight, out_weight, up_weight, down_weight]
    down_weight_t, nhat, rstd, qkv, prob, gatt, gmid, act, mid, late_keep, late_send, late_vectors = pl.pallas_call(
        late_kernel,
        grid_spec=pltpu.PrefetchScalarGridSpec(
            num_scalar_prefetch=1,
            grid=(steps_a,),
            in_specs=[whole((traj, slots)), HBM, HBM] + [whole(v.shape) for v in vectors + weights],
            out_specs=[whole((d, ff))]
            + [per_step(doubled(shapes[n][0]), at_a) for n in shapes]
            + [whole((late_shape[0] // 2, d))] * 2
            + [whole((8, d))],
            scratch_shapes=[
                pltpu.VMEM((2, BINS_A, 2 * seq, d), BF16),
                pltpu.VMEM((2, BINS_A, 2 * BIN, d), BF16),
                pltpu.SemaphoreType.DMA((2, BINS_A, 2, 2)),
                pltpu.VMEM((traj, BIN), jnp.int32),
                pltpu.VMEM((16, d), F32),
                pltpu.VMEM((12 * d, BIN), F32),
                pltpu.VMEM((3 * d, d), BF16),
                pltpu.VMEM((d, d), BF16),
                pltpu.VMEM((ff, d), BF16),
                pltpu.VMEM((d, TILE_A), F32),
                pltpu.VMEM((d, TILE_A), BF16),
                pltpu.VMEM((BINS_A * HEADS // 2, 2 * hs, PAIR), BF16),
                pltpu.VMEM((BINS_A * HEADS // 2, BIN, PAIR), F32),
                pltpu.VMEM((d, TILE_A), BF16),
                pltpu.VMEM((d, TILE_A), F32),
                pltpu.VMEM((d, TILE_A), BF16),
                pltpu.VMEM((d, TILE_A), BF16),
                pltpu.VMEM((ff, TILE_A), F32),
                pltpu.VMEM((ff, TILE_A), F32),
                pltpu.VMEM((ff, TILE_A), BF16),
                pltpu.VMEM((d, TILE_A), BF16),
                pltpu.VMEM((d, TILE_A), F32),
                pltpu.VMEM(late_shape, F32),
                pltpu.VMEM((3 * d + ff, BIN), F32),
            ],
        ),
        out_shape=[jax.ShapeDtypeStruct((d, ff), BF16)]
        + [stored(n) for n in shapes]
        + [jax.ShapeDtypeStruct(n, F32) for n in ((late_shape[0] // 2, d), (late_shape[0] // 2, d), (8, d))],
        compiler_params=params(56),
        name="forward_mlp",
    )(meta, visible_index, tokens, out_grad, *vectors, *weights)
    late = bucket_sum(bits, sums.view(late_keep), sums.view(late_send), late_shape[0] // 2, True)
    sums.add("late", late)
    sums.advance()

    acc_shape = (-(-(3 * d + 11) // 128) * 128, d)
    send_shape = (acc_shape[0] // 2, d)
    at = strided(0, 1, tiles_at, 1)
    grad_qkv, first_keep, first_send = pl.pallas_call(
        lambda *refs: attention_kernel(traj, *refs),
        grid_spec=pltpu.PrefetchScalarGridSpec(
            num_scalar_prefetch=1,
            grid=(steps_a,),
            in_specs=[per_step(doubled(shapes[n][0]), at) for n in ("nhat", "qkv", "prob", "gatt")] + [whole((8, d))],
            out_specs=[per_step((3 * d, TILE_A), at)] + [whole(send_shape)] * 2,
            scratch_shapes=[pltpu.VMEM((BINS_A * HEADS // 2, 2 * hs, PAIR), BF16)] * 2
            + [
                pltpu.VMEM((BINS_A * HEADS // 2, BIN, PAIR), F32),
                pltpu.VMEM((BINS_A * HEADS // 2, BIN, PAIR), BF16),
                pltpu.VMEM((3 * d, BIN), F32),
                pltpu.VMEM(acc_shape, F32),
            ],
        ),
        out_shape=[jax.ShapeDtypeStruct((steps_a, 3 * d, TILE_A), BF16)] + [jax.ShapeDtypeStruct(send_shape, F32)] * 2,
        compiler_params=params(56),
        cost_estimate=pl.CostEstimate(flops=5 * 10**9, bytes_accessed=16 * 10**6, transcendentals=0),
        name="attention_backward",
    )(sums.ordered(meta), nhat, qkv, prob, gatt, late_vectors)
    first = bucket_sum(bits, sums.view(first_keep), sums.view(first_send), send_shape[0], False)
    sums.add("first", first)
    sums.advance(first_keep)

    fewest = -(-traj // (2 * BINS))

    def stores(kernel, share, name, inputs, in_specs, rows, scratch, earlier):
        given = [] if earlier is None else [earlier]
        return pl.pallas_call(
            kernel,
            grid_spec=pltpu.PrefetchScalarGridSpec(
                num_scalar_prefetch=1,
                grid=(share.most(fewest, tiles),),
                in_specs=in_specs + [HBM] * len(given),
                out_specs=HBM,
                scratch_shapes=scratch
                + [pltpu.VMEM((2, BINS, 2 * BIN, d), BF16), pltpu.SemaphoreType.DMA((2, BINS, 2))],
            ),
            out_shape=jax.ShapeDtypeStruct((traj, rows, d), BF16),
            input_output_aliases={1 + len(inputs): 0} if given else {},
            compiler_params=params(56),
            cost_estimate=pl.CostEstimate(flops=2 * 10**9, bytes_accessed=8 * 10**6, transcendentals=0),
            name=name,
        )(sums.ordered(meta), *inputs, *given)

    tokens_grad = None
    for share in SHARES_C:
        at = share.block(tiles_at)
        tokens_grad = stores(
            lambda *refs, share=share: token_kernel(share, *refs),
            share,
            "tokens_backward",
            [visible_index, ln1_gain, qkv_weight, nhat, rstd, grad_qkv, gmid],
            [whole((traj, slots)), whole((d,)), whole((d, 3 * d))]
            + [per_tile(shapes["nhat"][0], at), per_tile(shapes["rstd"][0], at)]
            + [per_tile((3 * d, TILE), at), per_tile(shapes["gmid"][0], at)],
            seq,
            [pltpu.VMEM((traj, BIN), jnp.int32), pltpu.VMEM((d, BIN), F32), pltpu.VMEM((d, TILE), BF16)],
            tokens_grad,
        )
        sums.advance(tokens_grad)
    layer_out = None
    for share in SHARES_D:
        at = share.block(tiles_at)
        layer_out = stores(
            lambda *refs, share=share: output_kernel(share, traj, *refs),
            share,
            "layer_output",
            [down_bias, down_weight_t, act, mid],
            [whole((d,)), whole((d, ff)), per_tile(shapes["act"][0], at), per_tile(shapes["mid"][0], at)],
            slots,
            [pltpu.VMEM((d, BIN), F32), pltpu.VMEM((d, TILE), BF16)],
            layer_out,
        )
        sums.advance(layer_out)
    while sums.running:
        sums.advance()
    views = sums.results["late"] + sums.results["first"]
    near_far = [sums.arrays[k] for k, _ in views]
    rows_at = tuple(row for _, row in views)

    vmem = pl.BlockSpec(memory_space=pltpu.VMEM)
    vector = jax.ShapeDtypeStruct((d,), F32)
    dwn, dup, dwo, dqkv, dg1, dc1, dbq, dbv, dbo, dg2, dc2, dbup, dbdn = pl.pallas_call(
        lambda *refs: finish_kernel(tiles_at + 1, rows_at, *refs),
        in_specs=[pl.BlockSpec(memory_space=pltpu.SMEM)] + [HBM] * 4 + [vmem] * 4,
        out_specs=[HBM, vmem, HBM] + [vmem] * 10,
        out_shape=[
            jax.ShapeDtypeStruct((ff, d), F32),
            jax.ShapeDtypeStruct((d, ff), F32),
            jax.ShapeDtypeStruct((d, d), F32),
            jax.ShapeDtypeStruct((d, 3 * d), F32),
        ]
        + [vector] * 7
        + [jax.ShapeDtypeStruct((ff,), F32), vector],
        scratch_shapes=[
            pltpu.VMEM(late_shape, F32),
            pltpu.VMEM(acc_shape, F32),
            pltpu.SemaphoreType.DMA((2,)),
            pltpu.SemaphoreType.DMA((2,)),
            pltpu.SemaphoreType.DMA((2,)),
        ],
        compiler_params=pltpu.CompilerParams(vmem_limit_bytes=24 * MIB),
        name="finish",
    )(meta, *near_far, ln1_gain, ln1_bias, qkv_weight, up_weight)
    return layer_out, tokens_grad, dg1, dc1, dqkv, dbq, dbv, dwo, dbo, dg2, dc2, dup, dbup, dwn, dbdn


def solution(mesh):
    devices = mesh.devices
    ranks = devices.size
    mesh = Mesh(devices.reshape(devices.shape[0], devices.shape[1] // 2, 2), AXES)
    rows = P(AXES)
    placed = (rows, rows, rows) + (P(),) * 13 + (rows,)
    return jax.shard_map(
        lambda *args: body(ranks, *args),
        mesh=mesh,
        in_specs=placed,
        out_specs=(rows, rows) + (P(),) * 13,
        check_vma=False,
    )
```

```python
import jax
import jax.numpy as jnp
from jax import lax
from jax.experimental import pallas as pl
from jax.experimental.pallas import tpu as pltpu
from jax.sharding import Mesh, PartitionSpec as P

AXES = ("wide", "square", "core")
HEADS = 4
EPS = 1e-05
BIN = 128
PAIR = 2 * BIN
BINS = 4
TILE = BINS * BIN
BINS_A = 8
TILE_A = BINS_A * BIN
F32 = jnp.float32
BF16 = jnp.bfloat16
GELU_A = 0.7978845608028654
GELU_B = 0.044715 * GELU_A

NN = (((1,), (0,)), ((), ()))
NT = (((1,), (1,)), ((), ()))
TN = (((0,), (0,)), ((), ()))

MIB = 1024 * 1024
HBM = pl.BlockSpec(memory_space=pl.ANY)


def mm(left, right, dims=NN):
    return lax.dot_general(left, right, dims, preferred_element_type=F32)


class Meta:
    def __init__(self, ref, traj):
        self.ref = ref
        self.width = traj + 8

    @staticmethod
    def size(traj):
        return 4 * (traj + 8) + 16

    def bin(self, b):
        return tuple(self.ref[j * self.width + b] for j in range(4))

    def put(self, b, *values):
        for j, value in enumerate(values):
            self.ref[j * self.width + b] = value

    @property
    def tiles_at(self):
        return 4 * self.width

    def tiles(self):
        return self.ref[self.tiles_at]

    def bit(self, b):
        return self.ref[self.tiles_at + 1 + b]


def plan_kernel(count_ref, rank_ref, meta_ref, first_ref, order_ref):
    traj = count_ref.shape[0]
    top = first_ref.shape[0]
    meta = Meta(meta_ref, traj)

    def clear(v, carry):
        first_ref[v] = 0
        return carry

    lax.fori_loop(0, top, clear, 0, unroll=16)

    def tally(t, carry):
        c = count_ref[t]
        first_ref[c] = first_ref[c] + 1
        return carry

    lax.fori_loop(0, traj, tally, 0, unroll=8)

    def starts(i, run):
        v = top - 1 - i
        n = first_ref[v]
        first_ref[v] = run
        return run + n

    lax.fori_loop(0, top, starts, 0, unroll=16)

    def place(t, carry):
        c = count_ref[t]
        at = first_ref[c]
        order_ref[at] = t
        first_ref[c] = at + 1
        return carry

    lax.fori_loop(0, traj, place, 0, unroll=8)

    def pair(carry):
        hi, lo, n = carry
        t_hi = order_ref[hi]
        t_lo = order_ref[lo]
        c_hi = count_ref[t_hi]
        c_lo = count_ref[t_lo]
        fits = jnp.logical_and(hi < lo, c_hi + c_lo <= BIN)
        meta.put(n, t_hi, jnp.where(fits, t_lo, t_hi), c_hi, jnp.where(fits, c_lo, 0))
        return hi + 1, jnp.where(fits, lo - 1, lo), n + 1

    _, _, n = lax.while_loop(lambda c: c[0] <= c[1], pair, (jnp.int32(0), jnp.int32(traj - 1), jnp.int32(0)))
    last = meta_ref[n - 1]
    for j in range(BINS_A - 1):
        meta.put(n + j, last, last, 0, 0)
    meta_ref[meta.tiles_at] = lax.shift_right_logical(n + BINS - 1, BINS.bit_length() - 1)
    for b in range(15):
        meta_ref[meta.tiles_at + 1 + b] = jnp.bitwise_and(lax.shift_right_logical(rank_ref[0], b), 1)


def make_plan(counts, rank, slots):
    traj = counts.shape[0]
    smem = pl.BlockSpec(memory_space=pltpu.SMEM)
    return pl.pallas_call(
        plan_kernel,
        in_specs=[smem, smem],
        out_specs=smem,
        out_shape=jax.ShapeDtypeStruct((Meta.size(traj),), jnp.int32),
        scratch_shapes=[pltpu.SMEM((-(-(slots + 1) // 16) * 16,), jnp.int32), pltpu.SMEM((traj,), jnp.int32)],
        name="plan",
    )(counts, rank)


def bin_onehot(idx_ref, ta, tb, ca, cb, seq):
    lane = lax.broadcasted_iota(jnp.int32, (8, BIN), 1)
    ia = jnp.broadcast_to(idx_ref[pl.ds(ta, 1), :], (8, BIN))
    ib = jnp.broadcast_to(idx_ref[pl.ds(tb, 1), :], (8, BIN))
    ib = pltpu.roll(ib, ca, 1)
    code = jnp.where(lane < ca, ia, jnp.where(lane < ca + cb, ib + seq, -1))[0:1, :]
    pos = lax.broadcasted_iota(jnp.int32, (2 * seq, BIN), 0)
    return jnp.where(pos == code, 1.0, 0.0).astype(BF16)


def bin_slots(ca, cb):
    row = lax.broadcasted_iota(jnp.int32, (BIN, BIN), 0)
    lane = lax.broadcasted_iota(jnp.int32, (BIN, BIN), 1)
    first = jnp.logical_and(lane == row, row < ca)
    second = jnp.logical_and(lane == row + ca, row < cb)
    return jnp.concatenate([jnp.where(x, 1.0, 0.0).astype(BF16) for x in (first, second)], axis=0)


def bin_mask(ca, cb):
    row = lax.broadcasted_iota(jnp.int32, (BIN, BIN), 0)
    lane = lax.broadcasted_iota(jnp.int32, (BIN, BIN), 1)
    key = jnp.where(row < ca, 0, jnp.where(row < ca + cb, 1, 2))
    query = jnp.where(lane < ca, 0, jnp.where(lane < ca + cb, 1, 3))
    return jnp.where(key == query, 0.0, -1e30)


def center(x):
    mean = jnp.mean(x, axis=0, keepdims=True)
    xc = x - mean
    var = jnp.mean(xc * xc, axis=0, keepdims=True)
    rstd = lax.rsqrt(var + EPS)
    return xc * rstd, rstd


def lanes_into_rows(acc):
    return jnp.sum(acc.T, axis=0, keepdims=True)


def two(x):
    return jnp.concatenate([x, x], axis=1)


def bin_lanes(b):
    return slice(b * BIN, (b + 1) * BIN)


def pair_lanes(t):
    return slice(t * PAIR, (t + 1) * PAIR)


def departures(meta, tile, rows_s, slot, to_ref, rows, sems, act):
    half = rows_s.shape[2] // 2
    for b in range(BINS):
        ta, tb, ca, cb = meta.bin(tile * BINS + b)
        for part, (t, c) in enumerate(((ta, ca), (tb, cb))):

            @pl.when(c > 0)
            def _():
                act(
                    pltpu.make_async_copy(
                        rows_s.at[slot, b, pl.ds(part * half, rows)], to_ref.at[t], sems.at[slot, b, part]
                    )
                )


class Share:
    def __init__(self, first, last):
        self.first, self.last = first, last

    def start(self, tiles):
        return lax.shift_right_logical(tiles * self.first, 4)

    def stop(self, tiles):
        return lax.shift_right_logical(tiles * self.last, 4)


def shares(*cuts):
    return [Share(a, b) for a, b in zip(cuts[:-1], cuts[1:])]


def keep_half(meta, acc_s, keep_ref, send_ref):
    half = keep_ref.shape[0]
    core = meta.bit(CORE)
    keep_ref[...] = acc_s[pl.ds(pl.multiple_of(core * half, 8), half), :]
    send_ref[...] = acc_s[pl.ds(pl.multiple_of((1 - core) * half, 8), half), :]


def late_kernel(
    meta_ref,
    idx_ref,
    tok_ref,
    og_ref,
    g1_ref,
    c1_ref,
    bq_ref,
    bv_ref,
    bo_ref,
    g2_ref,
    c2_ref,
    bup_ref,
    wqkv_ref,
    wo_ref,
    wup_ref,
    wdn_ref,
    wdnt_s,
    nhat1_ref,
    rstd1_ref,
    qkv_ref,
    prob_ref,
    gatt_ref,
    gmid_ref,
    act_ref,
    mid_ref,
    keep_ref,
    send_ref,
    dvec_ref,
    tok_s,
    og_s,
    in_sem,
    idx_s,
    vec_s,
    col_s,
    wqkvt_s,
    wot_s,
    wupt_s,
    gath_s,
    first_s,
    bd_s,
    score_s,
    att_s,
    nhat_s,
    sec_s,
    gm_s,
    u_s,
    ga_s,
    gp_s,
    mid_s,
    gs_s,
    acc_s,
    bacc_s,
):
    step = pl.program_id(0)
    traj, seq, d = tok_ref.shape
    slots = og_ref.shape[1]
    ff = wup_ref.shape[1]
    hs = d // HEADS
    scale = hs**-0.5
    meta = Meta(meta_ref, traj)
    steps = lax.shift_right_logical(meta.tiles() + 1, 1)

    def arrivals(i, act):
        slot = jnp.bitwise_and(i, 1)
        for b in range(BINS_A):
            for part, t in enumerate(meta.bin(i * BINS_A + b)[0:2]):
                sems = in_sem.at[slot, b, part]
                act(pltpu.make_async_copy(tok_ref.at[t], tok_s.at[slot, b, pl.ds(part * seq, seq)], sems.at[0]))
                act(pltpu.make_async_copy(og_ref.at[t], og_s.at[slot, b, pl.ds(part * BIN, slots)], sems.at[1]))

    @pl.when(step == 0)
    def _():
        for part in range(2):
            og_s[:, :, part * BIN + slots : (part + 1) * BIN, :] = jnp.zeros((2, BINS_A, BIN - slots, d), BF16)
        arrivals(0, lambda c: c.start())
        idx_s[...] = jnp.zeros_like(idx_s)
        idx_s[:, 0:slots] = idx_ref[...]
        vec_s[...] = jnp.zeros_like(vec_s)
        rows = [(0, g1_ref), (1, c1_ref), (2, bq_ref), (4, bv_ref), (5, bo_ref), (6, g2_ref), (7, c2_ref)]
        for j, ref in rows:
            vec_s[j : j + 1, :] = ref[...].astype(F32).reshape(1, d)
        for j in range(ff // d):
            vec_s[8 + j : 9 + j, :] = bup_ref[j * d : (j + 1) * d].astype(F32).reshape(1, d)
        vec_s[2:3, :] = vec_s[2:3, :] * scale
        cols = vec_s[...].T
        for j in range(12):
            col_s[j * d : (j + 1) * d, :] = jnp.broadcast_to(cols[:, j : j + 1], (d, BIN))
        wqkvt_s[...] = wqkv_ref[...].T
        wqkvt_s[0:d, :] = (wqkvt_s[0:d, :].astype(F32) * scale).astype(BF16)
        wot_s[...] = wo_ref[...].T
        wupt_s[...] = wup_ref[...].T
        wdnt_s[...] = wdn_ref[...].T
        bd_s[...] = jnp.zeros_like(bd_s)
        bacc_s[...] = jnp.zeros_like(bacc_s)
        acc_s[...] = jnp.zeros_like(acc_s)

    def col(j, n=1):
        return col_s[j * d : (j + n) * d, :]

    @pl.when(step < steps)
    def _():
        slot = jnp.bitwise_and(step, 1)
        arrivals(step, lambda c: c.wait())

        @pl.when(step + 1 < steps)
        def _():
            arrivals(step + 1, lambda c: c.start())

        metas = [meta.bin(step * BINS_A + b) for b in range(BINS_A)]
        rstds = {}

        def gather(b):
            lanes = bin_lanes(b)
            gath_s[:, lanes] = mm(tok_s[slot, b], bin_onehot(idx_s, *metas[b], seq), TN)

        def first_norm(b):
            lanes = bin_lanes(b)
            nhat, rstd = center(gath_s[:, lanes])
            nhat1_ref[0, :, lanes] = nhat.astype(BF16)
            rstd1_ref[0, :, lanes] = jnp.broadcast_to(rstd, (8, BIN))
            first_s[:, lanes] = (nhat * col(0) + col(1)).astype(BF16)

        def cotangent(b):
            gm_s[:, bin_lanes(b)] = mm(og_s[slot, b], bin_slots(*metas[b][2:]), TN).astype(BF16)

        def project(t):
            lanes = pair_lanes(t)
            qkv_ref[0, :, lanes] = (mm(wqkvt_s[...], first_s[:, lanes]) + two(col(2, 3))).astype(BF16)

        def scores(b, p):
            lanes = bin_lanes(b)
            f0 = p * 2 * hs
            at = b * (HEADS // 2) + p
            bd_s[at, 0:hs, 0:BIN] = qkv_ref[0, f0 : f0 + hs, lanes]
            bd_s[at, hs : 2 * hs, BIN:PAIR] = qkv_ref[0, f0 + hs : f0 + 2 * hs, lanes]
            score_s[at] = mm(qkv_ref[0, d + f0 : d + f0 + 2 * hs, lanes], bd_s[at], TN)

        def softmax(b):
            mask = two(bin_mask(*metas[b][2:]))
            for p in range(HEADS // 2):
                s = score_s[b * (HEADS // 2) + p] + mask
                e = jnp.exp(s - jnp.max(s, axis=0, keepdims=True))
                prob_ref[0, b, :, pair_lanes(p)] = (e * (1.0 / jnp.sum(e, axis=0, keepdims=True))).astype(BF16)

        def attend(b, p):
            lanes = bin_lanes(b)
            f0 = p * 2 * hs
            both = mm(qkv_ref[0, 2 * d + f0 : 2 * d + f0 + 2 * hs, lanes], prob_ref[0, b, :, pair_lanes(p)])
            for h in range(2):
                att_s[f0 + h * hs : f0 + (h + 1) * hs, lanes] = both[h * hs : (h + 1) * hs, bin_lanes(h)].astype(BF16)

        def residual(t):
            lanes = pair_lanes(t)
            mid_s[:, lanes] = mm(wot_s[...], att_s[:, lanes])

        def second_norm(b):
            lanes = bin_lanes(b)
            mid = mid_s[:, lanes] + gath_s[:, lanes] + col(5)
            mid_ref[0, :, lanes] = mid.astype(BF16)
            nhat, rstds[b] = center(mid)
            nhat_s[:, lanes] = nhat
            sec_s[:, lanes] = (nhat * col(6) + col(7)).astype(BF16)

        def up(t):
            lanes = pair_lanes(t)
            u_s[:, lanes] = mm(wupt_s[...], sec_s[:, lanes])
            ga_s[:, lanes] = mm(wdn_ref[...], gm_s[:, lanes])

        def gelu(t, rows):
            lanes = pair_lanes(t)
            u = u_s[rows, lanes] + two(col_s[8 * d + rows.start : 8 * d + rows.stop, :])
            q = u * u * GELU_B + GELU_A
            sg = 0.5 * jnp.tanh(u * q) + 0.5
            act = u * sg
            gp = (act * (1.0 - sg) * (6.0 * q - 4.0 * GELU_A) + sg) * ga_s[rows, lanes]
            act_ref[0, rows, lanes] = act.astype(BF16)
            gp_s[rows, lanes] = gp.astype(BF16)
            bacc_s[d + rows.start : d + rows.stop, :] += gp[:, 0:BIN] + gp[:, BIN:PAIR]

        def grad_second(t):
            lanes = pair_lanes(t)
            gs_s[:, lanes] = mm(wup_ref[...], gp_s[:, lanes])

        def second_norm_back(b):
            lanes = bin_lanes(b)
            gs = gs_s[:, lanes]
            nhat = nhat_s[:, lanes]
            bacc_s[0:d, :] += gs * nhat
            a = gs * col(6)
            m1 = jnp.mean(a, axis=0, keepdims=True)
            m2 = jnp.mean(a * nhat, axis=0, keepdims=True)
            gm = gm_s[:, lanes].astype(F32)
            gmid = gm + rstds[b] * (a - m1 - nhat * m2)
            gmid_ref[0, :, lanes] = gmid.astype(BF16)
            bacc_s[d + ff : 2 * d + ff, :] += gm
            bacc_s[2 * d + ff : 3 * d + ff, :] += gmid

        def grad_attended(t):
            lanes = pair_lanes(t)
            gatt_ref[0, :, lanes] = mm(wo_ref[...], gmid_ref[0, :, lanes]).astype(BF16)

        def work(count):
            bins, tiles, chunk, lanes = range(count), range(count // 2), 32, slice(0, count * BIN)
            pairs = [[(b, p) for b in (2 * t, 2 * t + 1) for p in range(HEADS // 2)] for t in tiles]
            stages = dict(
                cotangent=lambda t: [cotangent(b) for b in (2 * t, 2 * t + 1)],
                first_norm=lambda t: [first_norm(b) for b in (2 * t, 2 * t + 1)],
                project=project,
                scores=lambda t: [scores(b, p) for b, p in pairs[t]],
                softmax=lambda t: [softmax(b) for b in (2 * t, 2 * t + 1)],
                attend=lambda t: [attend(b, p) for b, p in pairs[t]],
                residual=residual,
                second_norm=lambda t: [second_norm(b) for b in (2 * t, 2 * t + 1)],
                up=up,
                gelu=lambda t: [gelu(t, slice(j, j + chunk)) for j in range(0, ff, chunk)],
                grad_second=grad_second,
            )
            for b in bins:
                gather(b)
            for when in range(len(tiles) + len(stages) - 1):
                for n, stage in enumerate(stages.values()):
                    if 0 <= when - n < len(tiles):
                        stage(when - n)
            acc_s[0:ff, :] += mm(act_ref[0, :, lanes], gm_s[:, lanes], NT)
            for b in bins[: count // 2]:
                second_norm_back(b)
            acc_s[ff : 2 * ff, :] += mm(gp_s[:, lanes], sec_s[:, lanes], NT)
            for b in bins[count // 2 :]:
                second_norm_back(b)
            acc_s[2 * ff : 2 * ff + d, :] += mm(att_s[:, lanes], gmid_ref[0, :, lanes], NT)
            for t in tiles:
                grad_attended(t)

        full = 2 * step + 1 < meta.tiles()

        @pl.when(full)
        def _():
            work(BINS_A)

        @pl.when(jnp.logical_not(full))
        def _():
            work(BINS)

        @pl.when(step == steps - 1)
        def _():
            dvec_ref[...] = jnp.zeros_like(dvec_ref)
            keep_half(meta, acc_s, keep_ref, send_ref)
            for j in range(7):
                dvec_ref[j : j + 1, :] = lanes_into_rows(bacc_s[j * d : (j + 1) * d, :])


def attention_kernel(
    traj,
    meta_ref,
    nhat1_ref,
    qkv_ref,
    prob_ref,
    gatt_ref,
    dvec_ref,
    gq_ref,
    keep_ref,
    send_ref,
    bd_s,
    bdq_s,
    dp_s,
    ds_s,
    bacc_s,
    acc_s,
):
    step = pl.program_id(0)
    d = nhat1_ref.shape[1]
    hs = d // HEADS
    scale = hs**-0.5
    meta = Meta(meta_ref, traj)

    @pl.when(step == 0)
    def _():
        bd_s[...] = jnp.zeros_like(bd_s)
        bdq_s[...] = jnp.zeros_like(bdq_s)
        bacc_s[...] = jnp.zeros_like(bacc_s)
        acc_s[...] = jnp.zeros_like(acc_s)

    def work(count):
        pairs = [(b, p * 2 * hs, b * (HEADS // 2) + p, p) for b in range(count) for p in range(HEADS // 2)]
        for b, f0, at, _ in pairs:
            lanes = bin_lanes(b)
            bd_s[at, 0:hs, 0:BIN] = gatt_ref[0, f0 : f0 + hs, lanes]
            bd_s[at, hs : 2 * hs, BIN:PAIR] = gatt_ref[0, f0 + hs : f0 + 2 * hs, lanes]
            bdq_s[at, 0:hs, 0:BIN] = qkv_ref[0, f0 : f0 + hs, lanes]
            bdq_s[at, hs : 2 * hs, BIN:PAIR] = qkv_ref[0, f0 + hs : f0 + 2 * hs, lanes]
        for b, f0, at, _ in pairs:
            dp_s[at] = mm(qkv_ref[0, 2 * d + f0 : 2 * d + f0 + 2 * hs, bin_lanes(b)], bd_s[at], TN)
        for b, f0, at, p in pairs:
            pr = prob_ref[0, b, :, pair_lanes(p)].astype(F32)
            t = pr * dp_s[at]
            ds_s[at] = (t - pr * jnp.sum(t, axis=0, keepdims=True)).astype(BF16)

        def put(b, row, part):
            gq_ref[0, row : row + 2 * hs, bin_lanes(b)] = part.astype(BF16)
            bacc_s[row : row + 2 * hs, :] += part

        for b, f0, at, _ in pairs:
            both = mm(qkv_ref[0, d + f0 : d + f0 + 2 * hs, bin_lanes(b)], ds_s[at]) * scale
            put(b, f0, jnp.concatenate([both[0:hs, 0:BIN], both[hs : 2 * hs, BIN:PAIR]], axis=0))
        for b, f0, at, _ in pairs:
            put(b, d + f0, mm(bdq_s[at], ds_s[at], NT))
        for b, f0, at, p in pairs:
            put(b, 2 * d + f0, mm(bd_s[at], prob_ref[0, b, :, pair_lanes(p)], NT))
        lanes = slice(0, count * BIN)
        acc_s[0 : 3 * d, :] += mm(gq_ref[0, :, lanes], nhat1_ref[0, :, lanes], NT)

    @pl.when(2 * step + 1 < meta.tiles())
    def _():
        work(BINS_A)

    @pl.when(2 * step + 1 == meta.tiles())
    def _():
        work(BINS)

    @pl.when(step == pl.num_programs(0) - 1)
    def _():
        for j in range(3):
            acc_s[3 * d + j : 3 * d + j + 1, :] = lanes_into_rows(bacc_s[j * d : (j + 1) * d, :])
        acc_s[3 * d + 3 : 3 * d + 11, :] = dvec_ref[...]
        keep_half(meta, acc_s, keep_ref, send_ref)


def token_kernel(share, meta_ref, g1_ref, idx_ref, wqkv_ref, nhat1_ref, rstd1_ref, gq_ref, gmid_ref, *refs):
    tg_ref, idx_in, wqkv_s, nhat1_s, rstd1_s, gq_s, gmid_s, sems, idx_s, col_s, gg_s, rows_s, out_sems = refs[-13:]
    traj, slots = idx_ref.shape
    seq, d = tg_ref.shape[1:]
    meta = Meta(meta_ref, traj)

    def prepare():
        idx_s[...] = jnp.zeros_like(idx_s)
        idx_s[:, 0:slots] = idx_in[...]
        row = jnp.broadcast_to(g1_ref[...].astype(F32).reshape(1, d), (8, d))
        col_s[...] = jnp.broadcast_to(row.T[:, 0:1], (d, BIN))

    def rows_of(tile, slot):
        for b in range(BINS):
            gg_s[:, bin_lanes(b)] = bin_onehot(idx_s, *meta.bin(tile * BINS + b), seq)
        gfs = [mm(wqkv_s[...], gq_s[slot, :, pair_lanes(t)]) for t in range(BINS // 2)]
        grads = []
        for b in range(BINS):
            lanes = bin_lanes(b)
            nhat = nhat1_s[slot, :, lanes].astype(F32)
            a = gfs[b // 2][:, bin_lanes(b % 2)] * col_s[...]
            m1 = jnp.mean(a, axis=0, keepdims=True)
            m2 = jnp.mean(a * nhat, axis=0, keepdims=True)
            rstd = rstd1_s[slot, 0:1, lanes]
            grads.append((gmid_s[slot, :, lanes].astype(F32) + rstd * (a - m1 - nhat * m2)).astype(BF16))
        for b in range(BINS):
            rows_s[slot, b] = mm(gg_s[:, bin_lanes(b)], grads[b], NT).astype(BF16)

    store_tiles(
        share,
        meta,
        [(idx_ref, idx_in), (wqkv_ref, wqkv_s)],
        [(nhat1_ref, nhat1_s), (rstd1_ref, rstd1_s), (gq_ref, gq_s), (gmid_ref, gmid_s)],
        sems,
        prepare,
        rows_of,
        rows_s,
        tg_ref,
        seq,
        out_sems,
    )


def store_tiles(share, meta, once, each, sems, prepare, rows_of, rows_s, to_ref, rows, out_sems):
    first, stop = share.start(meta.tiles()), share.stop(meta.tiles())
    done = stop - first

    def constant(act):
        for k, (ref, place) in enumerate(once):
            act(pltpu.make_async_copy(ref, place, sems.at[2, k]))

    def come(tile, slot, act):
        lanes = pl.ds(pl.multiple_of(jnp.bitwise_and(tile, 1) * TILE, TILE), TILE)
        for k, (ref, place) in enumerate(each):
            act(
                pltpu.make_async_copy(
                    ref.at[lax.shift_right_logical(tile, 1), :, lanes], place.at[slot], sems.at[slot, k]
                )
            )

    def leave(i, act):
        departures(meta, first + i, rows_s, jnp.bitwise_and(i, 1), to_ref, rows, out_sems, act)

    constant(lambda c: c.start())
    come(first, 0, lambda c: c.start())
    constant(lambda c: c.wait())
    prepare()

    def step(i, carry):
        slot = jnp.bitwise_and(i, 1)
        come(first + i, slot, lambda c: c.wait())

        @pl.when(i + 1 < done)
        def _():
            come(first + i + 1, 1 - slot, lambda c: c.start())

        @pl.when(i >= 2)
        def _():
            leave(i - 2, lambda c: c.wait())

        rows_of(first + i, slot)
        leave(i, lambda c: c.start())
        return carry

    lax.fori_loop(0, done, step, 0)

    @pl.when(done >= 2)
    def _():
        leave(done - 2, lambda c: c.wait())

    leave(done - 1, lambda c: c.wait())


def output_kernel(share, traj, meta_ref, bdn_ref, wdnt_ref, act_ref, mid_ref, *refs):
    lay_ref, wdnt_s, act_s, mid_s, sems, col_s, y_s, rows_s, out_sems = refs[-9:]
    slots, d = lay_ref.shape[1:]
    meta = Meta(meta_ref, traj)

    def prepare():
        row = jnp.broadcast_to(bdn_ref[...].astype(F32).reshape(1, d), (8, d))
        col_s[...] = jnp.broadcast_to(row.T[:, 0:1], (d, BIN))

    def rows_of(tile, slot):
        for t in range(BINS // 2):
            lanes = pair_lanes(t)
            mlp = mm(wdnt_s[...], act_s[slot, :, lanes])
            y_s[:, lanes] = (mlp + mid_s[slot, :, lanes].astype(F32) + two(col_s[...])).astype(BF16)
        for b in range(BINS):
            _, _, ca, cb = meta.bin(tile * BINS + b)
            rows_s[slot, b] = mm(bin_slots(ca, cb), y_s[:, bin_lanes(b)], NT).astype(BF16)

    store_tiles(
        share,
        meta,
        [(wdnt_ref, wdnt_s)],
        [(act_ref, act_s), (mid_ref, mid_s)],
        sems,
        prepare,
        rows_of,
        rows_s,
        lay_ref,
        slots,
        out_sems,
    )


CORE, Y, X, Z = 0, 1, 2, 3


def row_at(const=0, **bits):
    return const, tuple(({"core": CORE, "y": Y, "x": X, "z": Z}[name], coef) for name, coef in bits.items())


def mine(bit, rows, base=0):
    return base, ((bit, rows),)


def other(bit, rows, base=0):
    return base + rows, ((bit, -rows),)


class Step:
    def __init__(self, inputs, out_rows, parts, sends=()):
        self.inputs, self.out_rows, self.parts, self.sends = list(inputs), list(out_rows), list(parts), dict(sends)


def combine_kernel(step, bits_at, meta_ref, *refs):
    ins, outs = refs[: len(step.inputs)], refs[len(step.inputs) :]

    def row(start):
        if isinstance(start, int):
            return start
        const, bits = start
        for bit, coef in bits:
            const = const + meta_ref[bits_at + bit] * coef
        return const

    def rows(start, n):
        return pl.ds(start if isinstance(start, int) else pl.multiple_of(start, 8), n)

    for n, terms, goes in step.parts:
        for out, start, first, count in goes:
            total = None
            for ref, at in terms:
                term = ins[ref][rows(row(at) + row(first), count), :]
                total = term if total is None else total + term
            outs[out][rows(row(start), count), :] = total


def combine(step, meta, bits_at, width):
    vmem = pl.BlockSpec(memory_space=pltpu.VMEM)
    return pl.pallas_call(
        lambda *refs: combine_kernel(step, bits_at, *refs),
        in_specs=[pl.BlockSpec(memory_space=pltpu.SMEM)] + [vmem] * len(step.inputs),
        out_specs=[vmem] * len(step.out_rows),
        out_shape=[jax.ShapeDtypeStruct((n, width), F32) for n in step.out_rows],
        compiler_params=pltpu.CompilerParams(vmem_limit_bytes=2 * MIB),
        name="combine",
    )(meta, *step.inputs)


def bucket_sum(bits, keep, send, half, halve_z):
    q, e, f = half // 4, half // 8, half // 16
    _, (got,) = yield Step([send], [], [], {0: CORE})
    (k0, k1, _, _), (g0, g1) = yield Step(
        [keep, got],
        [q, q, q, q],
        [
            (2 * q, [(0, row_at()), (1, row_at())], [(0, row_at(), mine(X, q), q), (2, row_at(), other(X, q), q)]),
            (
                2 * q,
                [(0, row_at(2 * q)), (1, row_at(2 * q))],
                [(1, row_at(), mine(Y, q), q), (3, row_at(), other(Y, q), q)],
            ),
        ],
        {2: X, 3: Y},
    )
    (a0, a1, _, _), (g0, g1) = yield Step(
        [k0, k1, g0, g1],
        [e, e, e, e],
        [
            (q, [(0, row_at()), (2, row_at())], [(0, row_at(), mine(Y, e), e), (2, row_at(), other(Y, e), e)]),
            (q, [(1, row_at()), (3, row_at())], [(1, row_at(), mine(X, e), e), (3, row_at(), other(X, e), e)]),
        ],
        {2: Y, 3: X},
    )
    if halve_z:
        (z, _), (got,) = yield Step(
            [a0, a1, g0, g1],
            [e, e],
            [
                (
                    e,
                    [(c, row_at()), (2 + c, row_at())],
                    [(0, row_at(c * f), mine(Z, f), f), (1, row_at(c * f), other(Z, f), f)],
                )
                for c in range(2)
            ],
            {1: Z},
        )
        for bit in [*range(Z + 1, bits), Z]:
            (z,), (got,) = yield Step([z, got], [e], [(e, [(0, row_at()), (1, row_at())], [(0, row_at(), 0, e)])], {0: bit})
        (e0, e1), (g0, g1) = yield Step(
            [z, got],
            [e, e],
            [
                (f, [(ref, row_at(c * f))], [(c, side(Z, f), 0, f)])
                for ref, side in enumerate((mine, other))
                for c in range(2)
            ],
            {0: Y, 1: X},
        )
    else:
        (z,), (got,) = yield Step(
            [a0, a1, g0, g1],
            [2 * e],
            [(e, [(c, row_at()), (2 + c, row_at())], [(0, row_at(c * e), 0, e)]) for c in range(2)],
            {0: bits - 1},
        )
        for bit in range(bits - 2, Z - 1, -1):
            (z,), (got,) = yield Step(
                [z, got], [2 * e], [(2 * e, [(0, row_at()), (1, row_at())], [(0, row_at(), 0, 2 * e)])], {0: bit}
            )
        (e0, e1), (g0, g1) = yield Step(
            [z, got],
            [e, e],
            [(2 * e, [(0, row_at()), (1, row_at())], [(0, row_at(), 0, e), (1, row_at(), e, e)])],
            {0: Y, 1: X},
        )
    (f0, f1), (g0, g1) = yield Step(
        [e0, e1, g0, g1],
        [q, q],
        [
            (e, [(0, row_at())], [(0, mine(Y, e), 0, e)]),
            (e, [(2, row_at())], [(0, other(Y, e), 0, e)]),
            (e, [(1, row_at())], [(1, mine(X, e), 0, e)]),
            (e, [(3, row_at())], [(1, other(X, e), 0, e)]),
        ],
        {0: X, 1: Y},
    )
    (near,), (far,) = yield Step(
        [f0, f1, g0, g1],
        [half],
        [
            (q, [(0, row_at())], [(0, mine(X, q), 0, q)]),
            (q, [(2, row_at())], [(0, other(X, q), 0, q)]),
            (q, [(1, row_at())], [(0, mine(Y, q, 2 * q), 0, q)]),
            (q, [(3, row_at())], [(0, other(Y, q, 2 * q), 0, q)]),
        ],
        {0: CORE},
    )
    return near, far


class Sums:
    def __init__(self, ranks, meta, bits_at, width):
        self.ranks, self.meta, self.bits_at, self.width = ranks, meta, bits_at, width
        self.arrays, self.arrived, self.sent = [], [], []
        self.running, self.results = {}, {}

    def view(self, array):
        self.arrays.append(array)
        return (len(self.arrays) - 1, 0)

    def add(self, name, steps):
        self.running[name] = (steps, next(steps))

    def advance(self, after=None):
        if after is not None and self.arrived:
            tied = lax.optimization_barrier((*[self.arrays[k] for k in self.arrived], after))
            for k, array in zip(self.arrived, tied):
                self.arrays[k] = array
        inputs, out_rows, parts, places, sends = [], [], [], {}, {}
        for name, (_, step) in self.running.items():
            outs = []
            for out, rows in enumerate(step.out_rows):
                bit = step.sends.get(out)
                if bit in sends:
                    at = sends[bit]
                    outs.append((at, out_rows[at]))
                    out_rows[at] += rows
                    continue
                if bit is not None:
                    sends[bit] = len(out_rows)
                outs.append((len(out_rows), 0))
                out_rows.append(rows)
            places[name] = outs
            for rows, terms, goes in step.parts:
                moved = []
                for ref, (const, bits) in terms:
                    k, row = step.inputs[ref]
                    if k not in inputs:
                        inputs.append(k)
                    moved.append((inputs.index(k), (const + row, bits)))
                parts.append(
                    (
                        rows,
                        moved,
                        [(outs[out][0], (const + outs[out][1], bits), *rest) for out, (const, bits), *rest in goes],
                    )
                )
        base = len(self.arrays)
        if out_rows:
            merged = Step([self.arrays[k] for k in inputs], out_rows, parts)
            self.arrays += list(combine(merged, self.meta, self.bits_at, self.width))
        to_send = {bit: base + out for bit, out in sends.items()}
        raw = {name: step for name, (_, step) in self.running.items() if not step.parts}
        for step in raw.values():
            for out, bit in step.sends.items():
                to_send[(bit, id(step))] = step.inputs[out][0]
        self.sent = [self.arrays[k] for k in to_send.values()]
        received = {}
        for key, k in to_send.items():
            bit = key[0] if isinstance(key, tuple) else key
            perm = [(r, r ^ (1 << bit)) for r in range(self.ranks)]
            received[key] = self.view(lax.ppermute(self.arrays[k], AXES, perm))[0]
        self.arrived = list(received.values())
        for name, (steps, step) in list(self.running.items()):
            if name in raw:
                outs = []
                got = [(received[(bit, id(step))], 0) for bit in step.sends.values()]
            else:
                outs = [(base + out, row) for out, row in places[name]]
                got = [(received[bit], places[name][out][1]) for out, bit in step.sends.items()]
            try:
                self.running[name] = (steps, steps.send((outs, got)))
            except StopIteration as stop:
                self.results[name] = stop.value
                del self.running[name]

    def ordered(self, value):
        return lax.optimization_barrier((value, *self.sent))[0]


def finish_kernel(
    bits_at, rows_at, meta_ref, late0_ref, late1_ref, first0_ref, first1_ref, g1_ref, c1_ref, wqkv_ref, wup_ref,
    dwn_ref, dup_ref, dwo_ref, dqkv_ref, dg1_ref, dc1_ref, dbq_ref, dbv_ref, dbo_ref, dg2_ref, dc2_ref, dbup_ref, dbdn_ref,
    late_s, first_s, first_sem, late_sem, out_sem,
):
    ff, d = dwn_ref.shape
    core = meta_ref[bits_at + CORE]
    late_near, late_far, first_near, first_far = rows_at
    first, late = [], []
    for to_s, copies, sems, sides in (
        (late_s, late, late_sem, ((late0_ref, late_near, core), (late1_ref, late_far, 1 - core))),
        (first_s, first, first_sem, ((first0_ref, first_near, core), (first1_ref, first_far, 1 - core))),
    ):
        half = to_s.shape[0] // 2
        for k, (ref, row, side) in enumerate(sides):
            to = to_s.at[pl.ds(pl.multiple_of(side * half, 8), half)]
            copies.append(pltpu.make_async_copy(ref.at[pl.ds(row, half)], to, sems.at[k]))
    for copy in late + first:
        copy.start()
    for copy in late:
        copy.wait()
    copies = [
        pltpu.make_async_copy(late_s.at[pl.ds(0, ff)], dwn_ref, out_sem.at[0]),
        pltpu.make_async_copy(late_s.at[pl.ds(2 * ff, d)], dwo_ref, out_sem.at[1]),
    ]
    for copy in copies:
        copy.start()
    for j in range(ff // d):
        dup_ref[:, j * d : (j + 1) * d] = late_s[ff + j * d : ff + (j + 1) * d, :].T
    for copy in first:
        copy.wait()

    def late_row(j):
        return first_s[3 * d + 3 + j : 3 * d + 4 + j, :].reshape(d)

    dg2_ref[...] = late_row(0)
    for j in range(ff // d):
        dbup_ref[j * d : (j + 1) * d] = late_row(1 + j)
    dbdn_ref[...] = late_row(5)
    dbo_ref[...] = late_row(6)

    def times(weight_ref, row, n):
        total = jnp.zeros((8, d), F32)
        for j in range(n):
            left = jnp.broadcast_to(first_s[row + j : row + j + 1, :], (8, d))
            for _ in range(3):
                low = left.astype(BF16)
                left = left - low.astype(F32)
                total = total + mm(low, weight_ref[:, j * d : (j + 1) * d], NT)
        return total[0:1, :]

    dc2_ref[...] = times(wup_ref, 3 * d + 4, ff // d).reshape(d)
    dc1_ref[...] = times(wqkv_ref, 3 * d, 3).reshape(d)

    gain = jnp.broadcast_to(g1_ref[...].astype(F32).reshape(1, d), (8, d)).T[:, 0:1]
    bias = jnp.broadcast_to(c1_ref[...].astype(F32).reshape(1, d), (8, d)).T[:, 0:1]
    gain_grad = jnp.zeros((d, d), F32)
    for j in range(3):
        block = slice(j * d, (j + 1) * d)
        total = first_s[3 * d + j : 3 * d + j + 1, :]
        product = first_s[block, :].T
        weight = wqkv_ref[:, block].astype(F32)
        dqkv_ref[:, block] = gain * product + bias * total
        gain_grad += weight * product
    dg1_ref[...] = jnp.sum(gain_grad.T, axis=0, keepdims=True).reshape(d)
    dbq_ref[...] = first_s[3 * d : 3 * d + 1, :].reshape(d)
    dbv_ref[...] = first_s[3 * d + 2 : 3 * d + 3, :].reshape(d)
    for copy in copies:
        copy.wait()


def whole(shape):
    zeros = (0,) * len(shape)
    return pl.BlockSpec(shape, lambda i, *_: zeros, pipeline_mode=pl.Buffered(1))


def per_step(shape, at):
    rest = (0,) * len(shape)
    return pl.BlockSpec((1,) + shape, lambda i, meta: (at(i, meta),) + rest)


def doubled(shape):
    if len(shape) == 3:
        return (2 * shape[0],) + shape[1:]
    return shape[:-1] + (2 * shape[-1],)


SHARES_C = shares(0, 5, 8, 10, 16)
SHARES_D = shares(0, 6, 9, 16)


def strided(first, pieces, tiles_at, halved=0):
    def at(i, meta):
        bits = pieces.bit_length() - 1
        count = lax.shift_right_logical(meta[tiles_at] + halved, halved)
        last = first + lax.shift_left(lax.shift_right_logical(count - 1 - first, bits), bits)
        return jnp.minimum(i * pieces + first, last)

    return at


def body(
    ranks,
    tokens,
    visible_index,
    visible_count,
    ln1_gain,
    ln1_bias,
    qkv_weight,
    query_bias,
    value_bias,
    out_weight,
    out_bias,
    ln2_gain,
    ln2_bias,
    up_weight,
    up_bias,
    down_weight,
    down_bias,
    out_grad,
):
    traj, slots = visible_index.shape
    seq, d = tokens.shape[1:]
    ff = up_weight.shape[1]
    hs = d // HEADS
    steps_a = -(-traj // BINS_A)
    tiles = 2 * steps_a
    tiles_at = Meta.size(traj) - 16
    bits = ranks.bit_length() - 1
    rank = lax.axis_index(AXES).astype(jnp.int32).reshape(1)
    meta = make_plan(visible_count, rank, slots)
    sums = Sums(ranks, meta, tiles_at + 1, d)

    shapes = dict(
        nhat=((d, TILE), BF16),
        rstd=((8, TILE), F32),
        qkv=((3 * d, TILE), BF16),
        prob=((BINS, BIN, HEADS * BIN), BF16),
        gatt=((d, TILE), BF16),
        gmid=((d, TILE), BF16),
        act=((ff, TILE), BF16),
        mid=((d, TILE), BF16),
    )

    def stored(name):
        shape, kind = shapes[name]
        return jax.ShapeDtypeStruct((steps_a,) + doubled(shape), kind)

    at_a = strided(0, 1, tiles_at, 1)

    def params(mib):
        return pltpu.CompilerParams(dimension_semantics=("arbitrary",), vmem_limit_bytes=mib * MIB)

    late_shape = (2 * ff + d, d)
    vectors = [ln1_gain, ln1_bias, query_bias, value_bias, out_bias, ln2_gain, ln2_bias, up_bias]
    weights = [qkv_weight, out_weight, up_weight, down_weight]
    down_weight_t, nhat, rstd, qkv, prob, gatt, gmid, act, mid, late_keep, late_send, late_vectors = pl.pallas_call(
        late_kernel,
        grid_spec=pltpu.PrefetchScalarGridSpec(
            num_scalar_prefetch=1,
            grid=(steps_a,),
            in_specs=[whole((traj, slots)), HBM, HBM] + [whole(v.shape) for v in vectors + weights],
            out_specs=[whole((d, ff))]
            + [per_step(doubled(shapes[n][0]), at_a) for n in shapes]
            + [whole((late_shape[0] // 2, d))] * 2
            + [whole((8, d))],
            scratch_shapes=[
                pltpu.VMEM((2, BINS_A, 2 * seq, d), BF16),
                pltpu.VMEM((2, BINS_A, 2 * BIN, d), BF16),
                pltpu.SemaphoreType.DMA((2, BINS_A, 2, 2)),
                pltpu.VMEM((traj, BIN), jnp.int32),
                pltpu.VMEM((16, d), F32),
                pltpu.VMEM((12 * d, BIN), F32),
                pltpu.VMEM((3 * d, d), BF16),
                pltpu.VMEM((d, d), BF16),
                pltpu.VMEM((ff, d), BF16),
                pltpu.VMEM((d, TILE_A), F32),
                pltpu.VMEM((d, TILE_A), BF16),
                pltpu.VMEM((BINS_A * HEADS // 2, 2 * hs, PAIR), BF16),
                pltpu.VMEM((BINS_A * HEADS // 2, BIN, PAIR), F32),
                pltpu.VMEM((d, TILE_A), BF16),
                pltpu.VMEM((d, TILE_A), F32),
                pltpu.VMEM((d, TILE_A), BF16),
                pltpu.VMEM((d, TILE_A), BF16),
                pltpu.VMEM((ff, TILE_A), F32),
                pltpu.VMEM((ff, TILE_A), F32),
                pltpu.VMEM((ff, TILE_A), BF16),
                pltpu.VMEM((d, TILE_A), F32),
                pltpu.VMEM((d, TILE_A), F32),
                pltpu.VMEM(late_shape, F32),
                pltpu.VMEM((3 * d + ff, BIN), F32),
            ],
        ),
        out_shape=[jax.ShapeDtypeStruct((d, ff), BF16)]
        + [stored(n) for n in shapes]
        + [jax.ShapeDtypeStruct(n, F32) for n in ((late_shape[0] // 2, d), (late_shape[0] // 2, d), (8, d))],
        compiler_params=params(56),
        name="forward_mlp",
    )(meta, visible_index, tokens, out_grad, *vectors, *weights)
    late = bucket_sum(bits, sums.view(late_keep), sums.view(late_send), late_shape[0] // 2, True)
    sums.add("late", late)
    sums.advance()

    acc_shape = (-(-(3 * d + 11) // 128) * 128, d)
    send_shape = (acc_shape[0] // 2, d)
    at = strided(0, 1, tiles_at, 1)
    grad_qkv, first_keep, first_send = pl.pallas_call(
        lambda *refs: attention_kernel(traj, *refs),
        grid_spec=pltpu.PrefetchScalarGridSpec(
            num_scalar_prefetch=1,
            grid=(steps_a,),
            in_specs=[per_step(doubled(shapes[n][0]), at) for n in ("nhat", "qkv", "prob", "gatt")] + [whole((8, d))],
            out_specs=[per_step((3 * d, TILE_A), at)] + [whole(send_shape)] * 2,
            scratch_shapes=[pltpu.VMEM((BINS_A * HEADS // 2, 2 * hs, PAIR), BF16)] * 2
            + [
                pltpu.VMEM((BINS_A * HEADS // 2, BIN, PAIR), F32),
                pltpu.VMEM((BINS_A * HEADS // 2, BIN, PAIR), BF16),
                pltpu.VMEM((3 * d, BIN), F32),
                pltpu.VMEM(acc_shape, F32),
            ],
        ),
        out_shape=[jax.ShapeDtypeStruct((steps_a, 3 * d, TILE_A), BF16)] + [jax.ShapeDtypeStruct(send_shape, F32)] * 2,
        compiler_params=params(56),
        cost_estimate=pl.CostEstimate(flops=5 * 10**9, bytes_accessed=16 * 10**6, transcendentals=0),
        name="attention_backward",
    )(sums.ordered(meta), nhat, qkv, prob, gatt, late_vectors)
    first = bucket_sum(bits, sums.view(first_keep), sums.view(first_send), send_shape[0], False)
    sums.add("first", first)
    sums.advance(first_keep)

    smem, vmem = (pl.BlockSpec(memory_space=m) for m in (pltpu.SMEM, pltpu.VMEM))

    def tile_places(*names):
        shapes_of = dict(shapes, gq=((3 * d, TILE), BF16))
        return [pltpu.VMEM((2,) + shapes_of[n][0], shapes_of[n][1]) for n in names]

    def stores(kernel, name, vector, inputs, rows, scratch, earlier):
        given = [] if earlier is None else [earlier]
        return pl.pallas_call(
            kernel,
            in_specs=[smem, vmem] + [HBM] * (len(inputs) + len(given)),
            out_specs=HBM,
            scratch_shapes=scratch
            + [pltpu.VMEM((2, BINS, 2 * BIN, d), BF16), pltpu.SemaphoreType.DMA((2, BINS, 2))],
            out_shape=jax.ShapeDtypeStruct((traj, rows, d), BF16),
            input_output_aliases={2 + len(inputs): 0} if given else {},
            compiler_params=pltpu.CompilerParams(vmem_limit_bytes=56 * MIB),
            cost_estimate=pl.CostEstimate(flops=2 * 10**9, bytes_accessed=8 * 10**6, transcendentals=0),
            name=name,
        )(sums.ordered(meta), vector, *inputs, *given)

    tokens_grad = None
    for share in SHARES_C:
        tokens_grad = stores(
            lambda *refs, share=share: token_kernel(share, *refs),
            "tokens_backward",
            ln1_gain,
            [visible_index, qkv_weight, nhat, rstd, grad_qkv, gmid],
            seq,
            [pltpu.VMEM((traj, slots), jnp.int32), pltpu.VMEM((d, 3 * d), BF16)]
            + tile_places("nhat", "rstd", "gq", "gmid")
            + [pltpu.SemaphoreType.DMA((3, 4))]
            + [pltpu.VMEM((traj, BIN), jnp.int32), pltpu.VMEM((d, BIN), F32), pltpu.VMEM((d, TILE), BF16)],
            tokens_grad,
        )
        sums.advance(tokens_grad)
    layer_out = None
    for share in SHARES_D:
        layer_out = stores(
            lambda *refs, share=share: output_kernel(share, traj, *refs),
            "layer_output",
            down_bias,
            [down_weight_t, act, mid],
            slots,
            [pltpu.VMEM((d, ff), BF16)]
            + tile_places("act", "mid")
            + [pltpu.SemaphoreType.DMA((3, 4))]
            + [pltpu.VMEM((d, BIN), F32), pltpu.VMEM((d, TILE), BF16)],
            layer_out,
        )
        sums.advance(layer_out)
    while sums.running:
        sums.advance()
    views = sums.results["late"] + sums.results["first"]
    near_far = [sums.arrays[k] for k, _ in views]
    rows_at = tuple(row for _, row in views)

    vmem = pl.BlockSpec(memory_space=pltpu.VMEM)
    vector = jax.ShapeDtypeStruct((d,), F32)
    dwn, dup, dwo, dqkv, dg1, dc1, dbq, dbv, dbo, dg2, dc2, dbup, dbdn = pl.pallas_call(
        lambda *refs: finish_kernel(tiles_at + 1, rows_at, *refs),
        in_specs=[pl.BlockSpec(memory_space=pltpu.SMEM)] + [HBM] * 4 + [vmem] * 4,
        out_specs=[HBM, vmem, HBM] + [vmem] * 10,
        out_shape=[
            jax.ShapeDtypeStruct((ff, d), F32),
            jax.ShapeDtypeStruct((d, ff), F32),
            jax.ShapeDtypeStruct((d, d), F32),
            jax.ShapeDtypeStruct((d, 3 * d), F32),
        ]
        + [vector] * 7
        + [jax.ShapeDtypeStruct((ff,), F32), vector],
        scratch_shapes=[
            pltpu.VMEM(late_shape, F32),
            pltpu.VMEM(acc_shape, F32),
            pltpu.SemaphoreType.DMA((2,)),
            pltpu.SemaphoreType.DMA((2,)),
            pltpu.SemaphoreType.DMA((2,)),
        ],
        compiler_params=pltpu.CompilerParams(vmem_limit_bytes=24 * MIB),
        name="finish",
    )(meta, *near_far, ln1_gain, ln1_bias, qkv_weight, up_weight)
    return layer_out, tokens_grad, dg1, dc1, dqkv, dbq, dbv, dwo, dbo, dg2, dc2, dup, dbup, dwn, dbdn


def solution(mesh):
    devices = mesh.devices
    ranks = devices.size
    mesh = Mesh(devices.reshape(devices.shape[0], devices.shape[1] // 2, 2), AXES)
    rows = P(AXES)
    placed = (rows, rows, rows) + (P(),) * 13 + (rows,)
    return jax.shard_map(
        lambda *args: body(ranks, *args),
        mesh=mesh,
        in_specs=placed,
        out_specs=(rows, rows) + (P(),) * 13,
        check_vma=False,
    )
```

```python
import jax
import jax.numpy as jnp
from jax import lax
from jax.experimental import pallas as pl
from jax.experimental.pallas import tpu as pltpu
from jax.sharding import Mesh, PartitionSpec as P

AXES = ("wide", "square", "core")
HEADS = 4
EPS = 1e-05
BIN = 128
PAIR = 2 * BIN
BINS = 4
TILE = BINS * BIN
BINS_A = 8
TILE_A = BINS_A * BIN
F32 = jnp.float32
BF16 = jnp.bfloat16
GELU_A = 0.7978845608028654
GELU_B = 0.044715 * GELU_A

NN = (((1,), (0,)), ((), ()))
NT = (((1,), (1,)), ((), ()))
TN = (((0,), (0,)), ((), ()))

MIB = 1024 * 1024
HBM = pl.BlockSpec(memory_space=pl.ANY)


def mm(left, right, dims=NN):
    return lax.dot_general(left, right, dims, preferred_element_type=F32)


class Meta:
    def __init__(self, ref, traj):
        self.ref = ref
        self.width = traj + 8

    @staticmethod
    def size(traj):
        return 4 * (traj + 8) + 16

    def bin(self, b):
        return tuple(self.ref[j * self.width + b] for j in range(4))

    def put(self, b, *values):
        for j, value in enumerate(values):
            self.ref[j * self.width + b] = value

    @property
    def tiles_at(self):
        return 4 * self.width

    def tiles(self):
        return self.ref[self.tiles_at]

    def bit(self, b):
        return self.ref[self.tiles_at + 1 + b]


def plan_kernel(count_ref, rank_ref, meta_ref, first_ref, order_ref):
    traj = count_ref.shape[0]
    top = first_ref.shape[0]
    meta = Meta(meta_ref, traj)

    def clear(v, carry):
        first_ref[v] = 0
        return carry

    lax.fori_loop(0, top, clear, 0, unroll=16)

    def tally(t, carry):
        c = count_ref[t]
        first_ref[c] = first_ref[c] + 1
        return carry

    lax.fori_loop(0, traj, tally, 0, unroll=8)

    def starts(i, run):
        v = top - 1 - i
        n = first_ref[v]
        first_ref[v] = run
        return run + n

    lax.fori_loop(0, top, starts, 0, unroll=16)

    def place(t, carry):
        c = count_ref[t]
        at = first_ref[c]
        order_ref[at] = t
        first_ref[c] = at + 1
        return carry

    lax.fori_loop(0, traj, place, 0, unroll=8)

    def pair(carry):
        hi, lo, n = carry
        t_hi = order_ref[hi]
        t_lo = order_ref[lo]
        c_hi = count_ref[t_hi]
        c_lo = count_ref[t_lo]
        fits = jnp.logical_and(hi < lo, c_hi + c_lo <= BIN)
        meta.put(n, t_hi, jnp.where(fits, t_lo, t_hi), c_hi, jnp.where(fits, c_lo, 0))
        return hi + 1, jnp.where(fits, lo - 1, lo), n + 1

    _, _, n = lax.while_loop(lambda c: c[0] <= c[1], pair, (jnp.int32(0), jnp.int32(traj - 1), jnp.int32(0)))
    last = meta_ref[n - 1]
    for j in range(BINS_A - 1):
        meta.put(n + j, last, last, 0, 0)
    meta_ref[meta.tiles_at] = lax.shift_right_logical(n + BINS - 1, BINS.bit_length() - 1)
    for b in range(15):
        meta_ref[meta.tiles_at + 1 + b] = jnp.bitwise_and(lax.shift_right_logical(rank_ref[0], b), 1)


def make_plan(counts, rank, slots):
    traj = counts.shape[0]
    smem = pl.BlockSpec(memory_space=pltpu.SMEM)
    return pl.pallas_call(
        plan_kernel,
        in_specs=[smem, smem],
        out_specs=smem,
        out_shape=jax.ShapeDtypeStruct((Meta.size(traj),), jnp.int32),
        scratch_shapes=[pltpu.SMEM((-(-(slots + 1) // 16) * 16,), jnp.int32), pltpu.SMEM((traj,), jnp.int32)],
        name="plan",
    )(counts, rank)


def bin_onehot(idx_ref, ta, tb, ca, cb, seq):
    lane = lax.broadcasted_iota(jnp.int32, (8, BIN), 1)
    ia = jnp.broadcast_to(idx_ref[pl.ds(ta, 1), :], (8, BIN))
    ib = jnp.broadcast_to(idx_ref[pl.ds(tb, 1), :], (8, BIN))
    ib = pltpu.roll(ib, ca, 1)
    code = jnp.where(lane < ca, ia, jnp.where(lane < ca + cb, ib + seq, -1))[0:1, :]
    pos = lax.broadcasted_iota(jnp.int32, (2 * seq, BIN), 0)
    return jnp.where(pos == code, 1.0, 0.0).astype(BF16)


def bin_slots(ca, cb):
    row = lax.broadcasted_iota(jnp.int32, (BIN, BIN), 0)
    lane = lax.broadcasted_iota(jnp.int32, (BIN, BIN), 1)
    first = jnp.logical_and(lane == row, row < ca)
    second = jnp.logical_and(lane == row + ca, row < cb)
    return jnp.concatenate([jnp.where(x, 1.0, 0.0).astype(BF16) for x in (first, second)], axis=0)


def bin_mask(ca, cb):
    row = lax.broadcasted_iota(jnp.int32, (BIN, BIN), 0)
    lane = lax.broadcasted_iota(jnp.int32, (BIN, BIN), 1)
    key = jnp.where(row < ca, 0, jnp.where(row < ca + cb, 1, 2))
    query = jnp.where(lane < ca, 0, jnp.where(lane < ca + cb, 1, 3))
    return jnp.where(key == query, 0.0, -1e30)


def center(x):
    mean = jnp.mean(x, axis=0, keepdims=True)
    xc = x - mean
    var = jnp.mean(xc * xc, axis=0, keepdims=True)
    rstd = lax.rsqrt(var + EPS)
    return xc * rstd, rstd


def lanes_into_rows(acc):
    return jnp.sum(acc.T, axis=0, keepdims=True)


def two(x):
    return jnp.concatenate([x, x], axis=1)


def bin_lanes(b):
    return slice(b * BIN, (b + 1) * BIN)


def pair_lanes(t):
    return slice(t * PAIR, (t + 1) * PAIR)


def departures(meta, tile, rows_s, slot, to_ref, rows, sems, act):
    half = rows_s.shape[2] // 2
    for b in range(BINS):
        ta, tb, ca, cb = meta.bin(tile * BINS + b)
        for part, (t, c) in enumerate(((ta, ca), (tb, cb))):

            @pl.when(c > 0)
            def _():
                act(
                    pltpu.make_async_copy(
                        rows_s.at[slot, b, pl.ds(part * half, rows)], to_ref.at[t], sems.at[slot, b, part]
                    )
                )


class Share:
    def __init__(self, first, last):
        self.first, self.last = first, last

    def start(self, tiles):
        return lax.shift_right_logical(tiles * self.first, 4)

    def stop(self, tiles):
        return lax.shift_right_logical(tiles * self.last, 4)


def shares(*cuts):
    return [Share(a, b) for a, b in zip(cuts[:-1], cuts[1:])]


def keep_half(meta, acc_s, keep_ref, send_ref):
    half = keep_ref.shape[0]
    core = meta.bit(CORE)
    keep_ref[...] = acc_s[pl.ds(pl.multiple_of(core * half, 8), half), :]
    send_ref[...] = acc_s[pl.ds(pl.multiple_of((1 - core) * half, 8), half), :]


def late_kernel(
    meta_ref,
    idx_ref,
    tok_ref,
    og_ref,
    g1_ref,
    c1_ref,
    bq_ref,
    bv_ref,
    bo_ref,
    g2_ref,
    c2_ref,
    bup_ref,
    wqkv_ref,
    wo_ref,
    wup_ref,
    wdn_ref,
    wdnt_s,
    nhat1_hbm,
    rstd1_hbm,
    qkv_hbm,
    prob_hbm,
    gatt_hbm,
    gmid_hbm,
    act_hbm,
    mid_hbm,
    keep_ref,
    send_ref,
    dvec_ref,
    tok_s,
    og_s,
    in_sem,
    nhat1_b,
    rstd1_b,
    qkv_b,
    prob_b,
    gatt_b,
    gmid_b,
    act_b,
    mid_b,
    out_sem,
    idx_s,
    vec_s,
    col_s,
    wqkvt_s,
    wot_s,
    wupt_s,
    gath_s,
    first_s,
    bd_s,
    score_s,
    att_s,
    nhat_s,
    sec_s,
    gm_s,
    u_s,
    ga_s,
    gp_s,
    mid_s,
    gs_s,
    acc_s,
    bacc_s,
):
    traj, seq, d = tok_ref.shape
    slots = og_ref.shape[1]
    ff = wup_ref.shape[1]
    hs = d // HEADS
    scale = hs**-0.5
    meta = Meta(meta_ref, traj)
    steps = lax.shift_right_logical(meta.tiles() + 1, 1)

    def arrivals(i, slot, act):
        for b in range(BINS_A):
            for part, t in enumerate(meta.bin(i * BINS_A + b)[0:2]):
                sems = in_sem.at[slot, b, part]
                act(pltpu.make_async_copy(tok_ref.at[t], tok_s.at[slot, b, pl.ds(part * seq, seq)], sems.at[0]))
                act(pltpu.make_async_copy(og_ref.at[t], og_s.at[slot, b, pl.ds(part * BIN, slots)], sems.at[1]))

    saved = (
        (nhat1_b, nhat1_hbm), (rstd1_b, rstd1_hbm), (qkv_b, qkv_hbm), (prob_b, prob_hbm),
        (act_b, act_hbm), (mid_b, mid_hbm), (gatt_b, gatt_hbm), (gmid_b, gmid_hbm),
    )

    def departures(i, which, act):
        slot = jnp.bitwise_and(i, 1)
        for k in which:
            place, ref = saved[k]
            act(pltpu.make_async_copy(place.at[slot], ref.at[i], out_sem.at[slot, k]))

    for part in range(2):
        og_s[:, :, part * BIN + slots : (part + 1) * BIN, :] = jnp.zeros((2, BINS_A, BIN - slots, d), BF16)
    arrivals(0, 0, lambda c: c.start())
    idx_s[...] = jnp.zeros_like(idx_s)
    idx_s[:, 0:slots] = idx_ref[...]
    vec_s[...] = jnp.zeros_like(vec_s)
    rows = [(0, g1_ref), (1, c1_ref), (2, bq_ref), (4, bv_ref), (5, bo_ref), (6, g2_ref), (7, c2_ref)]
    for j, ref in rows:
        vec_s[j : j + 1, :] = ref[...].astype(F32).reshape(1, d)
    for j in range(ff // d):
        vec_s[8 + j : 9 + j, :] = bup_ref[j * d : (j + 1) * d].astype(F32).reshape(1, d)
    vec_s[2:3, :] = vec_s[2:3, :] * scale
    cols = vec_s[...].T
    for j in range(12):
        col_s[j * d : (j + 1) * d, :] = jnp.broadcast_to(cols[:, j : j + 1], (d, BIN))
    wqkvt_s[...] = wqkv_ref[...].T
    wqkvt_s[0:d, :] = (wqkvt_s[0:d, :].astype(F32) * scale).astype(BF16)
    wot_s[...] = wo_ref[...].T
    wupt_s[...] = wup_ref[...].T
    wdnt_s[...] = wdn_ref[...].T
    bd_s[...] = jnp.zeros_like(bd_s)
    bacc_s[...] = jnp.zeros_like(bacc_s)
    acc_s[...] = jnp.zeros_like(acc_s)

    def col(j, n=1):
        return col_s[j * d : (j + n) * d, :]

    def work_on(step, carry):
        slot = jnp.bitwise_and(step, 1)
        arrivals(step, slot, lambda c: c.wait())

        @pl.when(step >= 2)
        def _():
            departures(step - 2, range(8), lambda c: c.wait())

        nhat1_ref, rstd1_ref, qkv_ref, prob_ref, act_ref, mid_ref, gatt_ref, gmid_ref = (
            place.at[pl.ds(slot, 1)] for place, _ in saved
        )
        metas = [meta.bin(step * BINS_A + b) for b in range(BINS_A)]
        rstds = {}

        def gather(b):
            lanes = bin_lanes(b)
            gath_s[:, lanes] = mm(tok_s[slot, b], bin_onehot(idx_s, *metas[b], seq), TN)

        def first_norm(b):
            lanes = bin_lanes(b)
            nhat, rstd = center(gath_s[:, lanes])
            nhat1_ref[0, :, lanes] = nhat.astype(BF16)
            rstd1_ref[0, :, lanes] = jnp.broadcast_to(rstd, (8, BIN))
            first_s[:, lanes] = (nhat * col(0) + col(1)).astype(BF16)

        def cotangent(b):
            gm_s[:, bin_lanes(b)] = mm(og_s[slot, b], bin_slots(*metas[b][2:]), TN).astype(BF16)

        def project(t):
            lanes = pair_lanes(t)
            qkv_ref[0, :, lanes] = (mm(wqkvt_s[...], first_s[:, lanes]) + two(col(2, 3))).astype(BF16)

        def scores(b, p):
            lanes = bin_lanes(b)
            f0 = p * 2 * hs
            at = b * (HEADS // 2) + p
            bd_s[at, 0:hs, 0:BIN] = qkv_ref[0, f0 : f0 + hs, lanes]
            bd_s[at, hs : 2 * hs, BIN:PAIR] = qkv_ref[0, f0 + hs : f0 + 2 * hs, lanes]
            score_s[at] = mm(qkv_ref[0, d + f0 : d + f0 + 2 * hs, lanes], bd_s[at], TN)

        def softmax(b):
            mask = two(bin_mask(*metas[b][2:]))
            for p in range(HEADS // 2):
                s = score_s[b * (HEADS // 2) + p] + mask
                e = jnp.exp(s - jnp.max(s, axis=0, keepdims=True))
                prob_ref[0, b, :, pair_lanes(p)] = (e * (1.0 / jnp.sum(e, axis=0, keepdims=True))).astype(BF16)

        def attend(b, p):
            lanes = bin_lanes(b)
            f0 = p * 2 * hs
            both = mm(qkv_ref[0, 2 * d + f0 : 2 * d + f0 + 2 * hs, lanes], prob_ref[0, b, :, pair_lanes(p)])
            for h in range(2):
                att_s[f0 + h * hs : f0 + (h + 1) * hs, lanes] = both[h * hs : (h + 1) * hs, bin_lanes(h)].astype(BF16)

        def residual(t):
            lanes = pair_lanes(t)
            mid_s[:, lanes] = mm(wot_s[...], att_s[:, lanes])

        def second_norm(b):
            lanes = bin_lanes(b)
            mid = mid_s[:, lanes] + gath_s[:, lanes] + col(5)
            mid_ref[0, :, lanes] = mid.astype(BF16)
            nhat, rstds[b] = center(mid)
            nhat_s[:, lanes] = nhat
            sec_s[:, lanes] = (nhat * col(6) + col(7)).astype(BF16)

        def up(t):
            lanes = pair_lanes(t)
            u_s[:, lanes] = (mm(wupt_s[...], sec_s[:, lanes]) + two(col_s[8 * d : 8 * d + ff, :])).astype(BF16)
            ga_s[:, lanes] = mm(wdn_ref[...], gm_s[:, lanes]).astype(BF16)

        def gelu(t, rows):
            lanes = pair_lanes(t)
            u = u_s[rows, lanes]
            u2 = u * u
            sg = 0.5 * jnp.tanh(u * (u2 * GELU_B + GELU_A)) + 0.5
            act = u * sg
            gp = (act * (1.0 - sg) * (u2 * (6.0 * GELU_B) + 2.0 * GELU_A) + sg) * ga_s[rows, lanes]
            act_ref[0, rows, lanes] = act
            gp_s[rows, lanes] = gp
            bacc_s[d + rows.start : d + rows.stop, :] += (gp[:, 0:BIN] + gp[:, BIN:PAIR]).astype(F32)

        def grad_second(t):
            lanes = pair_lanes(t)
            gs_s[:, lanes] = mm(wup_ref[...], gp_s[:, lanes])

        def second_norm_back(b):
            lanes = bin_lanes(b)
            gs = gs_s[:, lanes]
            nhat = nhat_s[:, lanes]
            bacc_s[0:d, :] += gs * nhat
            a = gs * col(6)
            m1 = jnp.mean(a, axis=0, keepdims=True)
            m2 = jnp.mean(a * nhat, axis=0, keepdims=True)
            gm = gm_s[:, lanes].astype(F32)
            gmid = gm + rstds[b] * (a - m1 - nhat * m2)
            gmid_ref[0, :, lanes] = gmid.astype(BF16)
            bacc_s[d + ff : 2 * d + ff, :] += gm
            bacc_s[2 * d + ff : 3 * d + ff, :] += gmid

        def grad_attended(t):
            lanes = pair_lanes(t)
            gatt_ref[0, :, lanes] = mm(wo_ref[...], gmid_ref[0, :, lanes]).astype(BF16)

        def work(count):
            bins, tiles, chunk, lanes = range(count), range(count // 2), 64, slice(0, count * BIN)
            pairs = [[(b, p) for b in (2 * t, 2 * t + 1) for p in range(HEADS // 2)] for t in tiles]
            stages = dict(
                cotangent=lambda t: [cotangent(b) for b in (2 * t, 2 * t + 1)],
                first_norm=lambda t: [first_norm(b) for b in (2 * t, 2 * t + 1)],
                project=project,
                scores=lambda t: [scores(b, p) for b, p in pairs[t]],
                softmax=lambda t: [softmax(b) for b in (2 * t, 2 * t + 1)],
                attend=lambda t: [attend(b, p) for b, p in pairs[t]],
                residual=residual,
                second_norm=lambda t: [second_norm(b) for b in (2 * t, 2 * t + 1)],
                up=up,
                gelu=lambda t: [gelu(t, slice(j, j + chunk)) for j in range(0, ff, chunk)],
                grad_second=grad_second,
            )
            arrivals(jnp.minimum(step + 1, steps - 1), 1 - slot, lambda c: c.start())
            for b in bins:
                gather(b)
            for when in range(len(tiles) + len(stages) - 1):
                for n, stage in enumerate(stages.values()):
                    if 0 <= when - n < len(tiles):
                        stage(when - n)
            departures(step, range(6), lambda c: c.start())
            acc_s[0:ff, :] += mm(act_ref[0, :, lanes], gm_s[:, lanes], NT)
            for b in bins[: count // 2]:
                second_norm_back(b)
            acc_s[ff : 2 * ff, :] += mm(gp_s[:, lanes], sec_s[:, lanes], NT)
            for b in bins[count // 2 :]:
                second_norm_back(b)
            acc_s[2 * ff : 2 * ff + d, :] += mm(att_s[:, lanes], gmid_ref[0, :, lanes], NT)
            for t in tiles:
                grad_attended(t)

        full = 2 * step + 1 < meta.tiles()

        @pl.when(full)
        def _():
            work(BINS_A)

        @pl.when(jnp.logical_not(full))
        def _():
            work(BINS)

        departures(step, range(6, 8), lambda c: c.start())
        return carry

    lax.fori_loop(0, steps, work_on, 0)
    keep_half(meta, acc_s, keep_ref, send_ref)
    for j in range(7):
        dvec_ref[j : j + 1, :] = lanes_into_rows(bacc_s[j * d : (j + 1) * d, :])
    dvec_ref[7:8, :] = jnp.zeros((1, d), F32)
    arrivals(steps - 1, jnp.bitwise_and(steps, 1), lambda c: c.wait())

    @pl.when(steps >= 2)
    def _():
        departures(steps - 2, range(8), lambda c: c.wait())

    departures(steps - 1, range(8), lambda c: c.wait())


def attention_kernel(
    traj,
    meta_ref,
    nhat1_hbm,
    qkv_hbm,
    prob_hbm,
    gatt_hbm,
    dvec_ref,
    gq_hbm,
    keep_ref,
    send_ref,
    nhat1_s,
    qkv_s,
    prob_s,
    gatt_s,
    gq_s,
    in_sem,
    out_sem,
    bd_s,
    bdq_s,
    dp_s,
    ds_s,
    bacc_s,
    acc_s,
):
    d = nhat1_hbm.shape[1]
    hs = d // HEADS
    scale = hs**-0.5
    meta = Meta(meta_ref, traj)
    steps = lax.shift_right_logical(meta.tiles() + 1, 1)

    def come(i, act):
        slot = jnp.bitwise_and(i, 1)
        for k, (ref, place) in enumerate(
            ((gatt_hbm, gatt_s), (qkv_hbm, qkv_s), (prob_hbm, prob_s), (nhat1_hbm, nhat1_s))
        ):
            act(pltpu.make_async_copy(ref.at[i], place.at[slot], in_sem.at[slot, k]))

    def leave(i, act):
        slot = jnp.bitwise_and(i, 1)
        act(pltpu.make_async_copy(gq_s.at[slot], gq_hbm.at[i], out_sem.at[slot]))

    come(0, lambda c: c.start())
    bd_s[...] = jnp.zeros_like(bd_s)
    bdq_s[...] = jnp.zeros_like(bdq_s)
    bacc_s[...] = jnp.zeros_like(bacc_s)
    acc_s[...] = jnp.zeros_like(acc_s)

    def step(i, carry):
        slot = jnp.bitwise_and(i, 1)
        come(i, lambda c: c.wait())

        @pl.when(i + 1 < steps)
        def _():
            come(i + 1, lambda c: c.start())

        @pl.when(i >= 2)
        def _():
            leave(i - 2, lambda c: c.wait())

        refs = [ref.at[pl.ds(slot, 1)] for ref in (nhat1_s, qkv_s, prob_s, gatt_s, gq_s)]

        @pl.when(2 * i + 1 < meta.tiles())
        def _():
            work(BINS_A, *refs)

        @pl.when(2 * i + 1 == meta.tiles())
        def _():
            work(BINS, *refs)

        leave(i, lambda c: c.start())
        return carry

    def work(count, nhat1_ref, qkv_ref, prob_ref, gatt_ref, gq_ref):
        pairs = [(b, p * 2 * hs, b * (HEADS // 2) + p, p) for b in range(count) for p in range(HEADS // 2)]
        for b, f0, at, _ in pairs:
            lanes = bin_lanes(b)
            bd_s[at, 0:hs, 0:BIN] = gatt_ref[0, f0 : f0 + hs, lanes]
            bd_s[at, hs : 2 * hs, BIN:PAIR] = gatt_ref[0, f0 + hs : f0 + 2 * hs, lanes]
            bdq_s[at, 0:hs, 0:BIN] = qkv_ref[0, f0 : f0 + hs, lanes]
            bdq_s[at, hs : 2 * hs, BIN:PAIR] = qkv_ref[0, f0 + hs : f0 + 2 * hs, lanes]
        for b, f0, at, _ in pairs:
            dp_s[at] = mm(qkv_ref[0, 2 * d + f0 : 2 * d + f0 + 2 * hs, bin_lanes(b)], bd_s[at], TN)
        for b, f0, at, p in pairs:
            pr = prob_ref[0, b, :, pair_lanes(p)].astype(F32)
            t = pr * dp_s[at]
            ds_s[at] = (t - pr * jnp.sum(t, axis=0, keepdims=True)).astype(BF16)

        def put(b, row, part):
            gq_ref[0, row : row + 2 * hs, bin_lanes(b)] = part.astype(BF16)
            bacc_s[row : row + 2 * hs, :] += part

        for b, f0, at, _ in pairs:
            both = mm(qkv_ref[0, d + f0 : d + f0 + 2 * hs, bin_lanes(b)], ds_s[at]) * scale
            put(b, f0, jnp.concatenate([both[0:hs, 0:BIN], both[hs : 2 * hs, BIN:PAIR]], axis=0))
        for b, f0, at, _ in pairs:
            put(b, d + f0, mm(bdq_s[at], ds_s[at], NT))
        for b, f0, at, p in pairs:
            put(b, 2 * d + f0, mm(bd_s[at], prob_ref[0, b, :, pair_lanes(p)], NT))
        lanes = slice(0, count * BIN)
        acc_s[0 : 3 * d, :] += mm(gq_ref[0, :, lanes], nhat1_ref[0, :, lanes], NT)

    lax.fori_loop(0, steps, step, 0)
    for j in range(3):
        acc_s[3 * d + j : 3 * d + j + 1, :] = lanes_into_rows(bacc_s[j * d : (j + 1) * d, :])
    acc_s[3 * d + 3 : 3 * d + 11, :] = dvec_ref[...]
    keep_half(meta, acc_s, keep_ref, send_ref)

    @pl.when(steps >= 2)
    def _():
        leave(steps - 2, lambda c: c.wait())

    leave(steps - 1, lambda c: c.wait())


def token_kernel(share, meta_ref, g1_ref, idx_ref, wqkv_ref, nhat1_ref, rstd1_ref, gq_ref, gmid_ref, *refs):
    tg_ref, idx_in, wqkv_s, nhat1_s, rstd1_s, gq_s, gmid_s, sems, idx_s, col_s, gg_s, rows_s, out_sems = refs[-13:]
    traj, slots = idx_ref.shape
    seq, d = tg_ref.shape[1:]
    meta = Meta(meta_ref, traj)

    def prepare():
        idx_s[...] = jnp.zeros_like(idx_s)
        idx_s[:, 0:slots] = idx_in[...]
        row = jnp.broadcast_to(g1_ref[...].astype(F32).reshape(1, d), (8, d))
        col_s[...] = jnp.broadcast_to(row.T[:, 0:1], (d, BIN))

    def rows_of(tile, slot):
        for b in range(BINS):
            gg_s[:, bin_lanes(b)] = bin_onehot(idx_s, *meta.bin(tile * BINS + b), seq)
        gfs = [mm(wqkv_s[...], gq_s[slot, :, pair_lanes(t)]) for t in range(BINS // 2)]
        grads = []
        for b in range(BINS):
            lanes = bin_lanes(b)
            nhat = nhat1_s[slot, :, lanes].astype(F32)
            a = gfs[b // 2][:, bin_lanes(b % 2)] * col_s[...]
            m1 = jnp.mean(a, axis=0, keepdims=True)
            m2 = jnp.mean(a * nhat, axis=0, keepdims=True)
            rstd = rstd1_s[slot, 0:1, lanes]
            grads.append((gmid_s[slot, :, lanes].astype(F32) + rstd * (a - m1 - nhat * m2)).astype(BF16))
        for b in range(BINS):
            rows_s[slot, b] = mm(gg_s[:, bin_lanes(b)], grads[b], NT).astype(BF16)

    store_tiles(
        share,
        meta,
        [(idx_ref, idx_in), (wqkv_ref, wqkv_s)],
        [(nhat1_ref, nhat1_s), (rstd1_ref, rstd1_s), (gq_ref, gq_s), (gmid_ref, gmid_s)],
        sems,
        prepare,
        rows_of,
        rows_s,
        tg_ref,
        seq,
        out_sems,
    )


def store_tiles(share, meta, once, each, sems, prepare, rows_of, rows_s, to_ref, rows, out_sems):
    first, stop = share.start(meta.tiles()), share.stop(meta.tiles())
    done = stop - first

    def constant(act):
        for k, (ref, place) in enumerate(once):
            act(pltpu.make_async_copy(ref, place, sems.at[2, k]))

    def come(tile, slot, act):
        lanes = pl.ds(pl.multiple_of(jnp.bitwise_and(tile, 1) * TILE, TILE), TILE)
        for k, (ref, place) in enumerate(each):
            act(
                pltpu.make_async_copy(
                    ref.at[lax.shift_right_logical(tile, 1), :, lanes], place.at[slot], sems.at[slot, k]
                )
            )

    def leave(i, act):
        departures(meta, first + i, rows_s, jnp.bitwise_and(i, 1), to_ref, rows, out_sems, act)

    constant(lambda c: c.start())
    come(first, 0, lambda c: c.start())
    constant(lambda c: c.wait())
    prepare()

    def step(i, carry):
        slot = jnp.bitwise_and(i, 1)
        come(first + i, slot, lambda c: c.wait())

        @pl.when(i + 1 < done)
        def _():
            come(first + i + 1, 1 - slot, lambda c: c.start())

        @pl.when(i >= 2)
        def _():
            leave(i - 2, lambda c: c.wait())

        rows_of(first + i, slot)
        leave(i, lambda c: c.start())
        return carry

    lax.fori_loop(0, done, step, 0)

    @pl.when(done >= 2)
    def _():
        leave(done - 2, lambda c: c.wait())

    leave(done - 1, lambda c: c.wait())


def output_kernel(share, traj, meta_ref, bdn_ref, wdnt_ref, act_ref, mid_ref, *refs):
    lay_ref, wdnt_s, act_s, mid_s, sems, col_s, y_s, rows_s, out_sems = refs[-9:]
    slots, d = lay_ref.shape[1:]
    meta = Meta(meta_ref, traj)

    def prepare():
        row = jnp.broadcast_to(bdn_ref[...].astype(F32).reshape(1, d), (8, d))
        col_s[...] = jnp.broadcast_to(row.T[:, 0:1], (d, BIN))

    def rows_of(tile, slot):
        for t in range(BINS // 2):
            lanes = pair_lanes(t)
            mlp = mm(wdnt_s[...], act_s[slot, :, lanes])
            y_s[:, lanes] = (mlp + mid_s[slot, :, lanes].astype(F32) + two(col_s[...])).astype(BF16)
        for b in range(BINS):
            _, _, ca, cb = meta.bin(tile * BINS + b)
            rows_s[slot, b] = mm(bin_slots(ca, cb), y_s[:, bin_lanes(b)], NT).astype(BF16)

    store_tiles(
        share,
        meta,
        [(wdnt_ref, wdnt_s)],
        [(act_ref, act_s), (mid_ref, mid_s)],
        sems,
        prepare,
        rows_of,
        rows_s,
        lay_ref,
        slots,
        out_sems,
    )


CORE, Y, X, Z = 0, 1, 2, 3


def row_at(const=0, **bits):
    return const, tuple(({"core": CORE, "y": Y, "x": X, "z": Z}[name], coef) for name, coef in bits.items())


def mine(bit, rows, base=0):
    return base, ((bit, rows),)


def other(bit, rows, base=0):
    return base + rows, ((bit, -rows),)


class Step:
    def __init__(self, inputs, out_rows, parts, sends=()):
        self.inputs, self.out_rows, self.parts, self.sends = list(inputs), list(out_rows), list(parts), dict(sends)


def combine_kernel(step, bits_at, meta_ref, *refs):
    ins, outs = refs[: len(step.inputs)], refs[len(step.inputs) :]

    def row(start):
        if isinstance(start, int):
            return start
        const, bits = start
        for bit, coef in bits:
            const = const + meta_ref[bits_at + bit] * coef
        return const

    def rows(start, n):
        return pl.ds(start if isinstance(start, int) else pl.multiple_of(start, 8), n)

    for n, terms, goes in step.parts:
        for out, start, first, count in goes:
            total = None
            for ref, at in terms:
                term = ins[ref][rows(row(at) + row(first), count), :]
                total = term if total is None else total + term
            outs[out][rows(row(start), count), :] = total


def combine(step, meta, bits_at, width):
    vmem = pl.BlockSpec(memory_space=pltpu.VMEM)
    return pl.pallas_call(
        lambda *refs: combine_kernel(step, bits_at, *refs),
        in_specs=[pl.BlockSpec(memory_space=pltpu.SMEM)] + [vmem] * len(step.inputs),
        out_specs=[vmem] * len(step.out_rows),
        out_shape=[jax.ShapeDtypeStruct((n, width), F32) for n in step.out_rows],
        compiler_params=pltpu.CompilerParams(vmem_limit_bytes=2 * MIB),
        name="combine",
    )(meta, *step.inputs)


def bucket_sum(bits, keep, send, half, halve_z):
    h, e, f = half // 4, half // 8, half // 16
    _, (got,) = yield Step([send], [], [], {0: (CORE,)})

    def part(x, y):
        return (0 if x else 2 * h) + (0 if y else h), ((X, 2 * h if x else -2 * h), (Y, h if y else -h))

    (k, _, _, _), got = yield Step(
        [keep, got],
        [h] * 4,
        [
            (h, [(0, part(x, y)), (1, part(x, y))], [(out, row_at(), 0, h)])
            for out, (x, y) in enumerate(((True, True), (False, True), (True, False), (False, False)))
        ],
        {1: (X,), 2: (Y,), 3: (X, Y)},
    )
    four = [k, *got]
    if halve_z:
        (z, _), (got,) = yield Step(
            four,
            [e, e],
            [
                (
                    e,
                    [(n, row_at(c * e)) for n in range(4)],
                    [(0, row_at(c * f), mine(Z, f), f), (1, row_at(c * f), other(Z, f), f)],
                )
                for c in range(2)
            ],
            {1: (Z,)},
        )
        for bit in [*range(Z + 1, bits), Z]:
            (z,), (got,) = yield Step(
                [z, got], [e], [(e, [(0, row_at()), (1, row_at())], [(0, row_at(), 0, e)])], {0: (bit,)}
            )
        (e0, e1), (g0, g1) = yield Step(
            [z, got],
            [e, e],
            [
                (f, [(ref, row_at(c * f))], [(c, side(Z, f), 0, f)])
                for ref, side in enumerate((mine, other))
                for c in range(2)
            ],
            {0: (Y,), 1: (X,)},
        )
    else:
        (z,), (got,) = yield Step(
            four, [h], [(h, [(n, row_at()) for n in range(4)], [(0, row_at(), 0, h)])], {0: (bits - 1,)}
        )
        for bit in range(bits - 2, Z - 1, -1):
            (z,), (got,) = yield Step(
                [z, got], [h], [(h, [(0, row_at()), (1, row_at())], [(0, row_at(), 0, h)])], {0: (bit,)}
            )
        (e0, e1), (g0, g1) = yield Step(
            [z, got],
            [e, e],
            [(h, [(0, row_at()), (1, row_at())], [(0, row_at(), 0, e), (1, row_at(), e, e)])],
            {0: (Y,), 1: (X,)},
        )
    (f0, f1), (g0, g1) = yield Step(
        [e0, e1, g0, g1],
        [h, h],
        [
            (e, [(0, row_at())], [(0, mine(Y, e), 0, e)]),
            (e, [(2, row_at())], [(0, other(Y, e), 0, e)]),
            (e, [(1, row_at())], [(1, mine(X, e), 0, e)]),
            (e, [(3, row_at())], [(1, other(X, e), 0, e)]),
        ],
        {0: (X,), 1: (Y,)},
    )
    (near,), (far,) = yield Step(
        [f0, f1, g0, g1],
        [half],
        [
            (h, [(0, row_at())], [(0, mine(X, 2 * h, y * h), y * e, e) for y in range(2)]),
            (h, [(2, row_at())], [(0, other(X, 2 * h, y * h), y * e, e) for y in range(2)]),
            (h, [(1, row_at())], [(0, mine(Y, h, x * 2 * h + e), x * e, e) for x in range(2)]),
            (h, [(3, row_at())], [(0, other(Y, h, x * 2 * h + e), x * e, e) for x in range(2)]),
        ],
        {0: (CORE,)},
    )
    return near, far


class Sums:
    def __init__(self, ranks, meta, bits_at, width):
        self.ranks, self.meta, self.bits_at, self.width = ranks, meta, bits_at, width
        self.arrays, self.arrived, self.sent = [], [], []
        self.running, self.results = {}, {}

    def view(self, array):
        self.arrays.append(array)
        return (len(self.arrays) - 1, 0)

    def add(self, name, steps):
        self.running[name] = (steps, next(steps))

    def advance(self, after=None):
        if after is not None and self.arrived:
            tied = lax.optimization_barrier((*[self.arrays[k] for k in self.arrived], after))
            for k, array in zip(self.arrived, tied):
                self.arrays[k] = array
        inputs, out_rows, parts, places, sends = [], [], [], {}, {}
        for name, (_, step) in self.running.items():
            outs = []
            for out, rows in enumerate(step.out_rows):
                bit = step.sends.get(out)
                if bit in sends:
                    at = sends[bit]
                    outs.append((at, out_rows[at]))
                    out_rows[at] += rows
                    continue
                if bit is not None:
                    sends[bit] = len(out_rows)
                outs.append((len(out_rows), 0))
                out_rows.append(rows)
            places[name] = outs
            for rows, terms, goes in step.parts:
                moved = []
                for ref, (const, bits) in terms:
                    k, row = step.inputs[ref]
                    if k not in inputs:
                        inputs.append(k)
                    moved.append((inputs.index(k), (const + row, bits)))
                parts.append(
                    (
                        rows,
                        moved,
                        [(outs[out][0], (const + outs[out][1], bits), *rest) for out, (const, bits), *rest in goes],
                    )
                )
        base = len(self.arrays)
        if out_rows:
            merged = Step([self.arrays[k] for k in inputs], out_rows, parts)
            self.arrays += list(combine(merged, self.meta, self.bits_at, self.width))
        to_send = {bit: base + out for bit, out in sends.items()}
        raw = {name: step for name, (_, step) in self.running.items() if not step.parts}
        for step in raw.values():
            for out, bit in step.sends.items():
                to_send[(bit, id(step))] = step.inputs[out][0]
        self.sent = [self.arrays[k] for k in to_send.values()]
        received = {}
        for key, k in to_send.items():
            mask = sum(1 << bit for bit in (key[0] if isinstance(key[0], tuple) else key))
            perm = [(r, r ^ mask) for r in range(self.ranks)]
            received[key] = self.view(lax.ppermute(self.arrays[k], AXES, perm))[0]
        self.arrived = list(received.values())
        for name, (steps, step) in list(self.running.items()):
            if name in raw:
                outs = []
                got = [(received[(bit, id(step))], 0) for bit in step.sends.values()]
            else:
                outs = [(base + out, row) for out, row in places[name]]
                got = [(received[bit], places[name][out][1]) for out, bit in step.sends.items()]
            try:
                self.running[name] = (steps, steps.send((outs, got)))
            except StopIteration as stop:
                self.results[name] = stop.value
                del self.running[name]

    def ordered(self, value):
        return lax.optimization_barrier((value, *self.sent))[0]


def finish_kernel(
    bits_at, rows_at, meta_ref, late0_ref, late1_ref, first0_ref, first1_ref, g1_ref, c1_ref, wqkv_ref, wup_ref,
    dwn_ref, dup_ref, dwo_ref, dqkv_ref, dg1_ref, dc1_ref, dbq_ref, dbv_ref, dbo_ref, dg2_ref, dc2_ref, dbup_ref, dbdn_ref,
    late_s, first_s, first_sem, late_sem, out_sem,
):
    ff, d = dwn_ref.shape
    core = meta_ref[bits_at + CORE]
    late_near, late_far, first_near, first_far = rows_at
    first, late = [], []
    for to_s, copies, sems, sides in (
        (late_s, late, late_sem, ((late0_ref, late_near, core), (late1_ref, late_far, 1 - core))),
        (first_s, first, first_sem, ((first0_ref, first_near, core), (first1_ref, first_far, 1 - core))),
    ):
        half = to_s.shape[0] // 2
        for k, (ref, row, side) in enumerate(sides):
            to = to_s.at[pl.ds(pl.multiple_of(side * half, 8), half)]
            copies.append(pltpu.make_async_copy(ref.at[pl.ds(row, half)], to, sems.at[k]))
    for copy in late + first:
        copy.start()
    for copy in late:
        copy.wait()
    copies = [
        pltpu.make_async_copy(late_s.at[pl.ds(0, ff)], dwn_ref, out_sem.at[0]),
        pltpu.make_async_copy(late_s.at[pl.ds(2 * ff, d)], dwo_ref, out_sem.at[1]),
    ]
    for copy in copies:
        copy.start()
    for j in range(ff // d):
        dup_ref[:, j * d : (j + 1) * d] = late_s[ff + j * d : ff + (j + 1) * d, :].T
    for copy in first:
        copy.wait()

    def late_row(j):
        return first_s[3 * d + 3 + j : 3 * d + 4 + j, :].reshape(d)

    dg2_ref[...] = late_row(0)
    for j in range(ff // d):
        dbup_ref[j * d : (j + 1) * d] = late_row(1 + j)
    dbdn_ref[...] = late_row(5)
    dbo_ref[...] = late_row(6)

    def times(weight_ref, row, n):
        total = jnp.zeros((8, d), F32)
        for j in range(n):
            left = jnp.broadcast_to(first_s[row + j : row + j + 1, :], (8, d))
            for _ in range(3):
                low = left.astype(BF16)
                left = left - low.astype(F32)
                total = total + mm(low, weight_ref[:, j * d : (j + 1) * d], NT)
        return total[0:1, :]

    dc2_ref[...] = times(wup_ref, 3 * d + 4, ff // d).reshape(d)
    dc1_ref[...] = times(wqkv_ref, 3 * d, 3).reshape(d)

    gain = jnp.broadcast_to(g1_ref[...].astype(F32).reshape(1, d), (8, d)).T[:, 0:1]
    bias = jnp.broadcast_to(c1_ref[...].astype(F32).reshape(1, d), (8, d)).T[:, 0:1]
    gain_grad = jnp.zeros((d, d), F32)
    for j in range(3):
        block = slice(j * d, (j + 1) * d)
        total = first_s[3 * d + j : 3 * d + j + 1, :]
        product = first_s[block, :].T
        weight = wqkv_ref[:, block].astype(F32)
        dqkv_ref[:, block] = gain * product + bias * total
        gain_grad += weight * product
    dg1_ref[...] = jnp.sum(gain_grad.T, axis=0, keepdims=True).reshape(d)
    dbq_ref[...] = first_s[3 * d : 3 * d + 1, :].reshape(d)
    dbv_ref[...] = first_s[3 * d + 2 : 3 * d + 3, :].reshape(d)
    for copy in copies:
        copy.wait()


def doubled(shape):
    if len(shape) == 3:
        return (2 * shape[0],) + shape[1:]
    return shape[:-1] + (2 * shape[-1],)


SHARES_C = shares(0, 8, 11, 16)
SHARES_D = shares(0, 6, 9, 16)


def body(
    ranks,
    tokens,
    visible_index,
    visible_count,
    ln1_gain,
    ln1_bias,
    qkv_weight,
    query_bias,
    value_bias,
    out_weight,
    out_bias,
    ln2_gain,
    ln2_bias,
    up_weight,
    up_bias,
    down_weight,
    down_bias,
    out_grad,
):
    traj, slots = visible_index.shape
    seq, d = tokens.shape[1:]
    ff = up_weight.shape[1]
    hs = d // HEADS
    steps_a = -(-traj // BINS_A)
    tiles = 2 * steps_a
    tiles_at = Meta.size(traj) - 16
    bits = ranks.bit_length() - 1
    rank = lax.axis_index(AXES).astype(jnp.int32).reshape(1)
    meta = make_plan(visible_count, rank, slots)
    sums = Sums(ranks, meta, tiles_at + 1, d)

    shapes = dict(
        nhat=((d, TILE), BF16),
        rstd=((8, TILE), F32),
        qkv=((3 * d, TILE), BF16),
        prob=((BINS, BIN, HEADS * BIN), BF16),
        gatt=((d, TILE), BF16),
        gmid=((d, TILE), BF16),
        act=((ff, TILE), BF16),
        mid=((d, TILE), BF16),
    )

    def stored(name):
        shape, kind = shapes[name]
        return jax.ShapeDtypeStruct((steps_a,) + doubled(shape), kind)

    smem, vmem = (pl.BlockSpec(memory_space=m) for m in (pltpu.SMEM, pltpu.VMEM))

    def step_places(*names):
        return [pltpu.VMEM((2,) + doubled(shapes[n][0]), shapes[n][1]) for n in names]

    late_shape = (2 * ff + d, d)
    vectors = [ln1_gain, ln1_bias, query_bias, value_bias, out_bias, ln2_gain, ln2_bias, up_bias]
    weights = [qkv_weight, out_weight, up_weight, down_weight]
    down_weight_t, nhat, rstd, qkv, prob, gatt, gmid, act, mid, late_keep, late_send, late_vectors = pl.pallas_call(
        late_kernel,
        in_specs=[smem, vmem, HBM, HBM] + [vmem] * len(vectors + weights),
        out_specs=[vmem] + [HBM] * len(shapes) + [vmem] * 3,
        scratch_shapes=[
            pltpu.VMEM((2, BINS_A, 2 * seq, d), BF16),
            pltpu.VMEM((2, BINS_A, 2 * BIN, d), BF16),
            pltpu.SemaphoreType.DMA((2, BINS_A, 2, 2)),
            *step_places(*shapes),
            pltpu.SemaphoreType.DMA((2, 8)),
            pltpu.VMEM((traj, BIN), jnp.int32),
            pltpu.VMEM((16, d), F32),
            pltpu.VMEM((12 * d, BIN), F32),
            pltpu.VMEM((3 * d, d), BF16),
            pltpu.VMEM((d, d), BF16),
            pltpu.VMEM((ff, d), BF16),
            pltpu.VMEM((d, TILE_A), F32),
            pltpu.VMEM((d, TILE_A), BF16),
            pltpu.VMEM((BINS_A * HEADS // 2, 2 * hs, PAIR), BF16),
            pltpu.VMEM((BINS_A * HEADS // 2, BIN, PAIR), F32),
            pltpu.VMEM((d, TILE_A), BF16),
            pltpu.VMEM((d, TILE_A), F32),
            pltpu.VMEM((d, TILE_A), BF16),
            pltpu.VMEM((d, TILE_A), BF16),
            pltpu.VMEM((ff, TILE_A), BF16),
            pltpu.VMEM((ff, TILE_A), BF16),
            pltpu.VMEM((ff, TILE_A), BF16),
            pltpu.VMEM((d, TILE_A), F32),
            pltpu.VMEM((d, TILE_A), F32),
            pltpu.VMEM(late_shape, F32),
            pltpu.VMEM((3 * d + ff, BIN), F32),
        ],
        out_shape=[jax.ShapeDtypeStruct((d, ff), BF16)]
        + [stored(n) for n in shapes]
        + [jax.ShapeDtypeStruct(n, F32) for n in ((late_shape[0] // 2, d), (late_shape[0] // 2, d), (8, d))],
        compiler_params=pltpu.CompilerParams(vmem_limit_bytes=58 * MIB),
        name="forward_mlp",
    )(meta, visible_index, tokens, out_grad, *vectors, *weights)
    late = bucket_sum(bits, sums.view(late_keep), sums.view(late_send), late_shape[0] // 2, True)
    sums.add("late", late)
    sums.advance()

    acc_shape = (-(-(3 * d + 11) // 128) * 128, d)
    send_shape = (acc_shape[0] // 2, d)
    grad_qkv, first_keep, first_send = pl.pallas_call(
        lambda *refs: attention_kernel(traj, *refs),
        in_specs=[smem] + [HBM] * 4 + [vmem],
        out_specs=[HBM, vmem, vmem],
        scratch_shapes=step_places("nhat", "qkv", "prob", "gatt")
        + [pltpu.VMEM((2, 3 * d, TILE_A), BF16), pltpu.SemaphoreType.DMA((2, 4)), pltpu.SemaphoreType.DMA((2,))]
        + [pltpu.VMEM((BINS_A * HEADS // 2, 2 * hs, PAIR), BF16)] * 2
        + [
            pltpu.VMEM((BINS_A * HEADS // 2, BIN, PAIR), F32),
            pltpu.VMEM((BINS_A * HEADS // 2, BIN, PAIR), BF16),
            pltpu.VMEM((3 * d, BIN), F32),
            pltpu.VMEM(acc_shape, F32),
        ],
        out_shape=[jax.ShapeDtypeStruct((steps_a, 3 * d, TILE_A), BF16)] + [jax.ShapeDtypeStruct(send_shape, F32)] * 2,
        compiler_params=pltpu.CompilerParams(vmem_limit_bytes=56 * MIB),
        cost_estimate=pl.CostEstimate(flops=5 * 10**9, bytes_accessed=16 * 10**6, transcendentals=0),
        name="attention_backward",
    )(sums.ordered(meta), nhat, qkv, prob, gatt, late_vectors)
    first = bucket_sum(bits, sums.view(first_keep), sums.view(first_send), send_shape[0], False)
    sums.add("first", first)
    sums.advance(first_keep)

    def tile_places(*names):
        shapes_of = dict(shapes, gq=((3 * d, TILE), BF16))
        return [pltpu.VMEM((2,) + shapes_of[n][0], shapes_of[n][1]) for n in names]

    def stores(kernel, name, vector, inputs, rows, scratch, earlier):
        given = [] if earlier is None else [earlier]
        return pl.pallas_call(
            kernel,
            in_specs=[smem, vmem] + [HBM] * (len(inputs) + len(given)),
            out_specs=HBM,
            scratch_shapes=scratch
            + [pltpu.VMEM((2, BINS, 2 * BIN, d), BF16), pltpu.SemaphoreType.DMA((2, BINS, 2))],
            out_shape=jax.ShapeDtypeStruct((traj, rows, d), BF16),
            input_output_aliases={2 + len(inputs): 0} if given else {},
            compiler_params=pltpu.CompilerParams(vmem_limit_bytes=56 * MIB),
            cost_estimate=pl.CostEstimate(flops=2 * 10**9, bytes_accessed=8 * 10**6, transcendentals=0),
            name=name,
        )(sums.ordered(meta), vector, *inputs, *given)

    tokens_grad = None
    for share in SHARES_C:
        tokens_grad = stores(
            lambda *refs, share=share: token_kernel(share, *refs),
            "tokens_backward",
            ln1_gain,
            [visible_index, qkv_weight, nhat, rstd, grad_qkv, gmid],
            seq,
            [pltpu.VMEM((traj, slots), jnp.int32), pltpu.VMEM((d, 3 * d), BF16)]
            + tile_places("nhat", "rstd", "gq", "gmid")
            + [pltpu.SemaphoreType.DMA((3, 4))]
            + [pltpu.VMEM((traj, BIN), jnp.int32), pltpu.VMEM((d, BIN), F32), pltpu.VMEM((d, TILE), BF16)],
            tokens_grad,
        )
        sums.advance(tokens_grad)
    layer_out = None
    for share in SHARES_D:
        layer_out = stores(
            lambda *refs, share=share: output_kernel(share, traj, *refs),
            "layer_output",
            down_bias,
            [down_weight_t, act, mid],
            slots,
            [pltpu.VMEM((d, ff), BF16)]
            + tile_places("act", "mid")
            + [pltpu.SemaphoreType.DMA((3, 4))]
            + [pltpu.VMEM((d, BIN), F32), pltpu.VMEM((d, TILE), BF16)],
            layer_out,
        )
        sums.advance(layer_out)
    while sums.running:
        sums.advance()
    views = sums.results["late"] + sums.results["first"]
    near_far = [sums.arrays[k] for k, _ in views]
    rows_at = tuple(row for _, row in views)

    vmem = pl.BlockSpec(memory_space=pltpu.VMEM)
    vector = jax.ShapeDtypeStruct((d,), F32)
    dwn, dup, dwo, dqkv, dg1, dc1, dbq, dbv, dbo, dg2, dc2, dbup, dbdn = pl.pallas_call(
        lambda *refs: finish_kernel(tiles_at + 1, rows_at, *refs),
        in_specs=[pl.BlockSpec(memory_space=pltpu.SMEM)] + [HBM] * 4 + [vmem] * 4,
        out_specs=[HBM, vmem, HBM] + [vmem] * 10,
        out_shape=[
            jax.ShapeDtypeStruct((ff, d), F32),
            jax.ShapeDtypeStruct((d, ff), F32),
            jax.ShapeDtypeStruct((d, d), F32),
            jax.ShapeDtypeStruct((d, 3 * d), F32),
        ]
        + [vector] * 7
        + [jax.ShapeDtypeStruct((ff,), F32), vector],
        scratch_shapes=[
            pltpu.VMEM(late_shape, F32),
            pltpu.VMEM(acc_shape, F32),
            pltpu.SemaphoreType.DMA((2,)),
            pltpu.SemaphoreType.DMA((2,)),
            pltpu.SemaphoreType.DMA((2,)),
        ],
        compiler_params=pltpu.CompilerParams(vmem_limit_bytes=24 * MIB),
        name="finish",
    )(meta, *near_far, ln1_gain, ln1_bias, qkv_weight, up_weight)
    return layer_out, tokens_grad, dg1, dc1, dqkv, dbq, dbv, dwo, dbo, dg2, dc2, dup, dbup, dwn, dbdn


def solution(mesh):
    devices = mesh.devices
    ranks = devices.size
    mesh = Mesh(devices.reshape(devices.shape[0], devices.shape[1] // 2, 2), AXES)
    rows = P(AXES)
    placed = (rows, rows, rows) + (P(),) * 13 + (rows,)
    return jax.shard_map(
        lambda *args: body(ranks, *args),
        mesh=mesh,
        in_specs=placed,
        out_specs=(rows, rows) + (P(),) * 13,
        check_vma=False,
    )
```

```python
import jax
import jax.numpy as jnp
from jax import lax
from jax.experimental import pallas as pl
from jax.experimental.pallas import tpu as pltpu
from jax.sharding import Mesh, PartitionSpec as P

AXES = ("wide", "square", "core")
HEADS = 4
EPS = 1e-05
BIN = 128
PAIR = 2 * BIN
BINS = 4
TILE = BINS * BIN
BINS_A = 8
TILE_A = BINS_A * BIN
F32 = jnp.float32
BF16 = jnp.bfloat16
GELU_A = 0.7978845608028654
GELU_B = 0.044715 * GELU_A

NN = (((1,), (0,)), ((), ()))
NT = (((1,), (1,)), ((), ()))
TN = (((0,), (0,)), ((), ()))

MIB = 1024 * 1024
HBM = pl.BlockSpec(memory_space=pl.ANY)


def mm(left, right, dims=NN):
    return lax.dot_general(left, right, dims, preferred_element_type=F32)


class Meta:
    def __init__(self, ref, traj):
        self.ref = ref
        self.width = traj + 8

    @staticmethod
    def size(traj):
        return 4 * (traj + 8) + 16

    def bin(self, b):
        return tuple(self.ref[j * self.width + b] for j in range(4))

    def put(self, b, *values):
        for j, value in enumerate(values):
            self.ref[j * self.width + b] = value

    @property
    def tiles_at(self):
        return 4 * self.width

    def tiles(self):
        return self.ref[self.tiles_at]

    def bins(self):
        return self.ref[self.tiles_at + 15]

    def bit(self, b):
        return self.ref[self.tiles_at + 1 + b]


def plan_kernel(count_ref, rank_ref, meta_ref, first_ref, order_ref):
    traj = count_ref.shape[0]
    top = first_ref.shape[0]
    meta = Meta(meta_ref, traj)

    def clear(v, carry):
        first_ref[v] = 0
        return carry

    lax.fori_loop(0, top, clear, 0, unroll=16)

    def tally(t, carry):
        c = count_ref[t]
        first_ref[c] = first_ref[c] + 1
        return carry

    lax.fori_loop(0, traj, tally, 0, unroll=8)

    def starts(i, run):
        v = top - 1 - i
        n = first_ref[v]
        first_ref[v] = run
        return run + n

    lax.fori_loop(0, top, starts, 0, unroll=16)

    def place(t, carry):
        c = count_ref[t]
        at = first_ref[c]
        order_ref[at] = t
        first_ref[c] = at + 1
        return carry

    lax.fori_loop(0, traj, place, 0, unroll=8)

    def pair(carry):
        hi, lo, n = carry
        t_hi = order_ref[hi]
        t_lo = order_ref[lo]
        c_hi = count_ref[t_hi]
        c_lo = count_ref[t_lo]
        fits = jnp.logical_and(hi < lo, c_hi + c_lo <= BIN)
        meta.put(n, t_hi, jnp.where(fits, t_lo, t_hi), c_hi, jnp.where(fits, c_lo, 0))
        return hi + 1, jnp.where(fits, lo - 1, lo), n + 1

    _, _, n = lax.while_loop(lambda c: c[0] <= c[1], pair, (jnp.int32(0), jnp.int32(traj - 1), jnp.int32(0)))
    last = meta_ref[n - 1]
    for j in range(BINS_A - 1):
        meta.put(n + j, last, last, 0, 0)
    meta_ref[meta.tiles_at] = lax.shift_right_logical(n + BINS - 1, BINS.bit_length() - 1)
    meta_ref[meta.tiles_at + 15] = n
    for b in range(14):
        meta_ref[meta.tiles_at + 1 + b] = jnp.bitwise_and(lax.shift_right_logical(rank_ref[0], b), 1)


def make_plan(counts, rank, slots):
    traj = counts.shape[0]
    smem = pl.BlockSpec(memory_space=pltpu.SMEM)
    return pl.pallas_call(
        plan_kernel,
        in_specs=[smem, smem],
        out_specs=smem,
        out_shape=jax.ShapeDtypeStruct((Meta.size(traj),), jnp.int32),
        scratch_shapes=[pltpu.SMEM((-(-(slots + 1) // 16) * 16,), jnp.int32), pltpu.SMEM((traj,), jnp.int32)],
        name="plan",
    )(counts, rank)


def bin_onehot(idx_ref, ta, tb, ca, cb, seq):
    lane = lax.broadcasted_iota(jnp.int32, (8, BIN), 1)
    ia = jnp.broadcast_to(idx_ref[pl.ds(ta, 1), :], (8, BIN))
    ib = jnp.broadcast_to(idx_ref[pl.ds(tb, 1), :], (8, BIN))
    ib = pltpu.roll(ib, ca, 1)
    code = jnp.where(lane < ca, ia, jnp.where(lane < ca + cb, ib + seq, -1))[0:1, :]
    pos = lax.broadcasted_iota(jnp.int32, (2 * seq, BIN), 0)
    return jnp.where(pos == code, 1.0, 0.0).astype(BF16)


def bin_slots(ca, cb):
    row = lax.broadcasted_iota(jnp.int32, (BIN, BIN), 0)
    lane = lax.broadcasted_iota(jnp.int32, (BIN, BIN), 1)
    first = jnp.logical_and(lane == row, row < ca)
    second = jnp.logical_and(lane == row + ca, row < cb)
    return jnp.concatenate([jnp.where(x, 1.0, 0.0).astype(BF16) for x in (first, second)], axis=0)


def bin_mask(ca, cb):
    row = lax.broadcasted_iota(jnp.int32, (BIN, BIN), 0)
    lane = lax.broadcasted_iota(jnp.int32, (BIN, BIN), 1)
    key = jnp.where(row < ca, 0, jnp.where(row < ca + cb, 1, 2))
    query = jnp.where(lane < ca, 0, jnp.where(lane < ca + cb, 1, 3))
    return jnp.where(key == query, 0.0, -1e30)


def center(x):
    mean = jnp.mean(x, axis=0, keepdims=True)
    xc = x - mean
    var = jnp.mean(xc * xc, axis=0, keepdims=True)
    rstd = lax.rsqrt(var + EPS)
    return xc * rstd, rstd


def lanes_into_rows(acc):
    return jnp.sum(acc.T, axis=0, keepdims=True)


def two(x):
    return jnp.concatenate([x, x], axis=1)


def bin_lanes(b):
    return slice(b * BIN, (b + 1) * BIN)


def pair_lanes(t):
    return slice(t * PAIR, (t + 1) * PAIR)


def departures(meta, tile, rows_s, slot, to_ref, rows, sems, act):
    half = rows_s.shape[2] // 2
    last = jnp.bitwise_and(meta.bins() - 1, BINS - 1)
    for b in range(BINS):
        ta, tb, ca, cb = meta.bin(tile * BINS + b)
        source = jnp.where(ca > 0, b, last)
        for part, (t, row) in enumerate(((ta, 0), (tb, jnp.where(cb > 0, half, 0)))):
            rows_of_t = pl.ds(pl.multiple_of(row, half) if part else 0, rows)
            act(pltpu.make_async_copy(rows_s.at[slot, source, rows_of_t], to_ref.at[t], sems.at[slot, b, part]))


class Share:
    def __init__(self, first, last):
        self.first, self.last = first, last

    def start(self, tiles):
        return lax.shift_right_logical(tiles * self.first, 4)

    def stop(self, tiles):
        return lax.shift_right_logical(tiles * self.last, 4)


def shares(*cuts):
    return [Share(a, b) for a, b in zip(cuts[:-1], cuts[1:])]


def keep_half(meta, acc_s, keep_ref, send_ref):
    half = keep_ref.shape[0]
    core = meta.bit(CORE)
    keep_ref[...] = acc_s[pl.ds(pl.multiple_of(core * half, 8), half), :]
    send_ref[...] = acc_s[pl.ds(pl.multiple_of((1 - core) * half, 8), half), :]


def late_kernel(
    meta_ref,
    idx_ref,
    tok_ref,
    og_ref,
    g1_ref,
    c1_ref,
    bq_ref,
    bv_ref,
    bo_ref,
    g2_ref,
    c2_ref,
    bup_ref,
    wqkv_ref,
    wo_ref,
    wup_ref,
    wdn_ref,
    wdnt_s,
    nhat1_hbm,
    rstd1_hbm,
    qkv_hbm,
    prob_hbm,
    gatt_hbm,
    gmid_hbm,
    act_hbm,
    mid_hbm,
    keep_ref,
    send_ref,
    dvec_ref,
    tok_s,
    og_s,
    in_sem,
    nhat1_b,
    rstd1_b,
    qkv_b,
    prob_b,
    gatt_b,
    gmid_b,
    act_b,
    mid_b,
    out_sem,
    idx_s,
    vec_s,
    col_s,
    wqkvt_s,
    wot_s,
    wupt_s,
    gath_s,
    first_s,
    bd_s,
    score_s,
    att_s,
    nhat_s,
    sec_s,
    gm_s,
    u_s,
    ga_s,
    gp_s,
    mid_s,
    gs_s,
    acc_s,
    bacc_s,
):
    traj, seq, d = tok_ref.shape
    slots = og_ref.shape[1]
    ff = wup_ref.shape[1]
    hs = d // HEADS
    scale = hs**-0.5
    meta = Meta(meta_ref, traj)
    steps = lax.shift_right_logical(meta.tiles() + 1, 1)

    def arrivals(i, slot, act):
        for b in range(BINS_A):
            for part, t in enumerate(meta.bin(i * BINS_A + b)[0:2]):
                sems = in_sem.at[slot, b, part]
                act(pltpu.make_async_copy(tok_ref.at[t], tok_s.at[slot, b, pl.ds(part * seq, seq)], sems.at[0]))
                act(pltpu.make_async_copy(og_ref.at[t], og_s.at[slot, b, pl.ds(part * BIN, slots)], sems.at[1]))

    saved = (
        (nhat1_b, nhat1_hbm), (rstd1_b, rstd1_hbm), (qkv_b, qkv_hbm), (prob_b, prob_hbm),
        (act_b, act_hbm), (mid_b, mid_hbm), (gatt_b, gatt_hbm), (gmid_b, gmid_hbm),
    )

    def departures(i, which, act):
        slot = jnp.bitwise_and(i, 1)
        for k in which:
            place, ref = saved[k]
            act(pltpu.make_async_copy(place.at[slot], ref.at[i], out_sem.at[slot, k]))

    for part in range(2):
        og_s[:, :, part * BIN + slots : (part + 1) * BIN, :] = jnp.zeros((2, BINS_A, BIN - slots, d), BF16)
    arrivals(0, 0, lambda c: c.start())
    idx_s[...] = jnp.zeros_like(idx_s)
    idx_s[:, 0:slots] = idx_ref[...]
    vec_s[...] = jnp.zeros_like(vec_s)
    rows = [(0, g1_ref), (1, c1_ref), (2, bq_ref), (4, bv_ref), (5, bo_ref), (6, g2_ref), (7, c2_ref)]
    for j, ref in rows:
        vec_s[j : j + 1, :] = ref[...].astype(F32).reshape(1, d)
    for j in range(ff // d):
        vec_s[8 + j : 9 + j, :] = bup_ref[j * d : (j + 1) * d].astype(F32).reshape(1, d)
    vec_s[2:3, :] = vec_s[2:3, :] * scale
    cols = vec_s[...].T
    for j in range(12):
        col_s[j * d : (j + 1) * d, :] = jnp.broadcast_to(cols[:, j : j + 1], (d, BIN))
    wqkvt_s[...] = wqkv_ref[...].T
    wqkvt_s[0:d, :] = (wqkvt_s[0:d, :].astype(F32) * scale).astype(BF16)
    wot_s[...] = wo_ref[...].T
    wupt_s[...] = wup_ref[...].T
    wdnt_s[...] = wdn_ref[...].T
    bd_s[...] = jnp.zeros_like(bd_s)
    bacc_s[...] = jnp.zeros_like(bacc_s)
    acc_s[...] = jnp.zeros_like(acc_s)

    def col(j, n=1):
        return col_s[j * d : (j + n) * d, :]

    def work_on(step, carry):
        slot = jnp.bitwise_and(step, 1)
        arrivals(step, slot, lambda c: c.wait())

        @pl.when(step >= 2)
        def _():
            departures(step - 2, range(8), lambda c: c.wait())

        nhat1_ref, rstd1_ref, qkv_ref, prob_ref, act_ref, mid_ref, gatt_ref, gmid_ref = (
            place.at[pl.ds(slot, 1)] for place, _ in saved
        )
        metas = [meta.bin(step * BINS_A + b) for b in range(BINS_A)]
        rstds = {}

        def gather(b):
            lanes = bin_lanes(b)
            gath_s[:, lanes] = mm(tok_s[slot, b], bin_onehot(idx_s, *metas[b], seq), TN)

        def first_norm(b):
            lanes = bin_lanes(b)
            nhat, rstd = center(gath_s[:, lanes])
            nhat1_ref[0, :, lanes] = nhat.astype(BF16)
            rstd1_ref[0, :, lanes] = jnp.broadcast_to(rstd, (8, BIN))
            first_s[:, lanes] = (nhat * col(0) + col(1)).astype(BF16)

        def cotangent(b):
            gm_s[:, bin_lanes(b)] = mm(og_s[slot, b], bin_slots(*metas[b][2:]), TN).astype(BF16)

        def project(t):
            lanes = pair_lanes(t)
            qkv_ref[0, :, lanes] = (mm(wqkvt_s[...], first_s[:, lanes]) + two(col(2, 3))).astype(BF16)

        def scores(b, p):
            lanes = bin_lanes(b)
            f0 = p * 2 * hs
            at = b * (HEADS // 2) + p
            bd_s[at, 0:hs, 0:BIN] = qkv_ref[0, f0 : f0 + hs, lanes]
            bd_s[at, hs : 2 * hs, BIN:PAIR] = qkv_ref[0, f0 + hs : f0 + 2 * hs, lanes]
            score_s[at] = mm(qkv_ref[0, d + f0 : d + f0 + 2 * hs, lanes], bd_s[at], TN)

        def softmax(b):
            mask = two(bin_mask(*metas[b][2:]))
            for p in range(HEADS // 2):
                s = score_s[b * (HEADS // 2) + p] + mask
                e = jnp.exp(s - jnp.max(s, axis=0, keepdims=True))
                prob_ref[0, b, :, pair_lanes(p)] = (e * (1.0 / jnp.sum(e, axis=0, keepdims=True))).astype(BF16)

        def attend(b, p):
            lanes = bin_lanes(b)
            f0 = p * 2 * hs
            both = mm(qkv_ref[0, 2 * d + f0 : 2 * d + f0 + 2 * hs, lanes], prob_ref[0, b, :, pair_lanes(p)])
            for h in range(2):
                att_s[f0 + h * hs : f0 + (h + 1) * hs, lanes] = both[h * hs : (h + 1) * hs, bin_lanes(h)].astype(BF16)

        def residual(t):
            lanes = pair_lanes(t)
            mid_s[:, lanes] = mm(wot_s[...], att_s[:, lanes])

        def second_norm(b):
            lanes = bin_lanes(b)
            mid = mid_s[:, lanes] + gath_s[:, lanes] + col(5)
            mid_ref[0, :, lanes] = mid.astype(BF16)
            nhat, rstds[b] = center(mid)
            nhat_s[:, lanes] = nhat
            sec_s[:, lanes] = (nhat * col(6) + col(7)).astype(BF16)

        def up(t):
            lanes = pair_lanes(t)
            u_s[:, lanes] = (mm(wupt_s[...], sec_s[:, lanes]) + two(col_s[8 * d : 8 * d + ff, :])).astype(BF16)
            ga_s[:, lanes] = mm(wdn_ref[...], gm_s[:, lanes]).astype(BF16)

        def gelu(t, rows):
            lanes = pair_lanes(t)
            u = u_s[rows, lanes]
            u2 = u * u
            sg = 0.5 * jnp.tanh(u * (u2 * GELU_B + GELU_A)) + 0.5
            act = u * sg
            gp = (act * (1.0 - sg) * (u2 * (6.0 * GELU_B) + 2.0 * GELU_A) + sg) * ga_s[rows, lanes]
            act_ref[0, rows, lanes] = act
            gp_s[rows, lanes] = gp
            bacc_s[d + rows.start : d + rows.stop, :] += (gp[:, 0:BIN] + gp[:, BIN:PAIR]).astype(F32)

        def grad_second(t):
            lanes = pair_lanes(t)
            gs_s[:, lanes] = mm(wup_ref[...], gp_s[:, lanes])

        def second_norm_back(b):
            lanes = bin_lanes(b)
            gs = gs_s[:, lanes]
            nhat = nhat_s[:, lanes]
            bacc_s[0:d, :] += gs * nhat
            a = gs * col(6)
            m1 = jnp.mean(a, axis=0, keepdims=True)
            m2 = jnp.mean(a * nhat, axis=0, keepdims=True)
            gm = gm_s[:, lanes].astype(F32)
            gmid = gm + rstds[b] * (a - m1 - nhat * m2)
            gmid_ref[0, :, lanes] = gmid.astype(BF16)
            bacc_s[d + ff : 2 * d + ff, :] += gm
            bacc_s[2 * d + ff : 3 * d + ff, :] += gmid

        def grad_attended(t):
            lanes = pair_lanes(t)
            gatt_ref[0, :, lanes] = mm(wo_ref[...], gmid_ref[0, :, lanes]).astype(BF16)

        def work(count):
            bins, tiles, chunk, lanes = range(count), range(count // 2), 64, slice(0, count * BIN)
            pairs = [[(b, p) for b in (2 * t, 2 * t + 1) for p in range(HEADS // 2)] for t in tiles]
            stages = dict(
                cotangent=lambda t: [cotangent(b) for b in (2 * t, 2 * t + 1)],
                first_norm=lambda t: [first_norm(b) for b in (2 * t, 2 * t + 1)],
                project=project,
                scores=lambda t: [scores(b, p) for b, p in pairs[t]],
                softmax=lambda t: [softmax(b) for b in (2 * t, 2 * t + 1)],
                attend=lambda t: [attend(b, p) for b, p in pairs[t]],
                residual=residual,
                second_norm=lambda t: [second_norm(b) for b in (2 * t, 2 * t + 1)],
                up=up,
                gelu=lambda t: [gelu(t, slice(j, j + chunk)) for j in range(0, ff, chunk)],
                grad_second=grad_second,
            )
            arrivals(jnp.minimum(step + 1, steps - 1), 1 - slot, lambda c: c.start())
            for b in bins:
                gather(b)
            for when in range(len(tiles) + len(stages) - 1):
                for n, stage in enumerate(stages.values()):
                    if 0 <= when - n < len(tiles):
                        stage(when - n)
            departures(step, range(6), lambda c: c.start())
            acc_s[0:ff, :] += mm(act_ref[0, :, lanes], gm_s[:, lanes], NT)
            for b in bins[: count // 2]:
                second_norm_back(b)
            acc_s[ff : 2 * ff, :] += mm(gp_s[:, lanes], sec_s[:, lanes], NT)
            for b in bins[count // 2 :]:
                second_norm_back(b)
            acc_s[2 * ff : 2 * ff + d, :] += mm(att_s[:, lanes], gmid_ref[0, :, lanes], NT)
            for t in tiles:
                grad_attended(t)

        full = 2 * step + 1 < meta.tiles()

        @pl.when(full)
        def _():
            work(BINS_A)

        @pl.when(jnp.logical_not(full))
        def _():
            work(BINS)

        departures(step, range(6, 8), lambda c: c.start())
        return carry

    lax.fori_loop(0, steps, work_on, 0)
    keep_half(meta, acc_s, keep_ref, send_ref)
    for j in range(7):
        dvec_ref[j : j + 1, :] = lanes_into_rows(bacc_s[j * d : (j + 1) * d, :])
    dvec_ref[7:8, :] = jnp.zeros((1, d), F32)
    arrivals(steps - 1, jnp.bitwise_and(steps, 1), lambda c: c.wait())

    @pl.when(steps >= 2)
    def _():
        departures(steps - 2, range(8), lambda c: c.wait())

    departures(steps - 1, range(8), lambda c: c.wait())


def attention_kernel(
    traj,
    meta_ref,
    nhat1_hbm,
    qkv_hbm,
    prob_hbm,
    gatt_hbm,
    dvec_ref,
    gq_hbm,
    keep_ref,
    send_ref,
    nhat1_s,
    qkv_s,
    prob_s,
    gatt_s,
    gq_s,
    in_sem,
    out_sem,
    bd_s,
    bdq_s,
    dp_s,
    ds_s,
    bacc_s,
    acc_s,
):
    d = nhat1_hbm.shape[1]
    hs = d // HEADS
    scale = hs**-0.5
    meta = Meta(meta_ref, traj)
    steps = lax.shift_right_logical(meta.tiles() + 1, 1)

    def come(i, act):
        slot = jnp.bitwise_and(i, 1)
        for k, (ref, place) in enumerate(
            ((gatt_hbm, gatt_s), (qkv_hbm, qkv_s), (prob_hbm, prob_s), (nhat1_hbm, nhat1_s))
        ):
            act(pltpu.make_async_copy(ref.at[i], place.at[slot], in_sem.at[slot, k]))

    def leave(i, act):
        slot = jnp.bitwise_and(i, 1)
        act(pltpu.make_async_copy(gq_s.at[slot], gq_hbm.at[i], out_sem.at[slot]))

    come(0, lambda c: c.start())
    bd_s[...] = jnp.zeros_like(bd_s)
    bdq_s[...] = jnp.zeros_like(bdq_s)
    bacc_s[...] = jnp.zeros_like(bacc_s)
    acc_s[...] = jnp.zeros_like(acc_s)

    def step(i, carry):
        slot = jnp.bitwise_and(i, 1)
        come(i, lambda c: c.wait())

        @pl.when(i + 1 < steps)
        def _():
            come(i + 1, lambda c: c.start())

        @pl.when(i >= 2)
        def _():
            leave(i - 2, lambda c: c.wait())

        refs = [ref.at[pl.ds(slot, 1)] for ref in (nhat1_s, qkv_s, prob_s, gatt_s, gq_s)]

        @pl.when(2 * i + 1 < meta.tiles())
        def _():
            work(BINS_A, *refs)

        @pl.when(2 * i + 1 == meta.tiles())
        def _():
            work(BINS, *refs)

        leave(i, lambda c: c.start())
        return carry

    def work(count, nhat1_ref, qkv_ref, prob_ref, gatt_ref, gq_ref):
        pairs = [(b, p * 2 * hs, b * (HEADS // 2) + p, p) for b in range(count) for p in range(HEADS // 2)]
        for b, f0, at, _ in pairs:
            lanes = bin_lanes(b)
            bd_s[at, 0:hs, 0:BIN] = gatt_ref[0, f0 : f0 + hs, lanes]
            bd_s[at, hs : 2 * hs, BIN:PAIR] = gatt_ref[0, f0 + hs : f0 + 2 * hs, lanes]
            bdq_s[at, 0:hs, 0:BIN] = qkv_ref[0, f0 : f0 + hs, lanes]
            bdq_s[at, hs : 2 * hs, BIN:PAIR] = qkv_ref[0, f0 + hs : f0 + 2 * hs, lanes]
        for b, f0, at, _ in pairs:
            dp_s[at] = mm(qkv_ref[0, 2 * d + f0 : 2 * d + f0 + 2 * hs, bin_lanes(b)], bd_s[at], TN)
        for b, f0, at, p in pairs:
            pr = prob_ref[0, b, :, pair_lanes(p)].astype(F32)
            t = pr * dp_s[at]
            ds_s[at] = (t - pr * jnp.sum(t, axis=0, keepdims=True)).astype(BF16)

        def put(b, row, part):
            gq_ref[0, row : row + 2 * hs, bin_lanes(b)] = part.astype(BF16)
            bacc_s[row : row + 2 * hs, :] += part

        for b, f0, at, _ in pairs:
            both = mm(qkv_ref[0, d + f0 : d + f0 + 2 * hs, bin_lanes(b)], ds_s[at]) * scale
            put(b, f0, jnp.concatenate([both[0:hs, 0:BIN], both[hs : 2 * hs, BIN:PAIR]], axis=0))
        for b, f0, at, _ in pairs:
            put(b, d + f0, mm(bdq_s[at], ds_s[at], NT))
        for b, f0, at, p in pairs:
            put(b, 2 * d + f0, mm(bd_s[at], prob_ref[0, b, :, pair_lanes(p)], NT))
        lanes = slice(0, count * BIN)
        acc_s[0 : 3 * d, :] += mm(gq_ref[0, :, lanes], nhat1_ref[0, :, lanes], NT)

    lax.fori_loop(0, steps, step, 0)
    for j in range(3):
        acc_s[3 * d + j : 3 * d + j + 1, :] = lanes_into_rows(bacc_s[j * d : (j + 1) * d, :])
    acc_s[3 * d + 3 : 3 * d + 11, :] = dvec_ref[...]
    keep_half(meta, acc_s, keep_ref, send_ref)

    @pl.when(steps >= 2)
    def _():
        leave(steps - 2, lambda c: c.wait())

    leave(steps - 1, lambda c: c.wait())


def token_kernel(share, meta_ref, g1_ref, idx_ref, wqkv_ref, nhat1_ref, rstd1_ref, gq_ref, gmid_ref, *refs):
    tg_ref, idx_in, wqkv_s, nhat1_s, rstd1_s, gq_s, gmid_s, sems, idx_s, col_s, gg_s, rows_s, out_sems = refs[-13:]
    traj, slots = idx_ref.shape
    seq, d = tg_ref.shape[1:]
    meta = Meta(meta_ref, traj)

    def prepare():
        idx_s[...] = jnp.zeros_like(idx_s)
        idx_s[:, 0:slots] = idx_in[...]
        row = jnp.broadcast_to(g1_ref[...].astype(F32).reshape(1, d), (8, d))
        col_s[...] = jnp.broadcast_to(row.T[:, 0:1], (d, BIN))

    def rows_of(tile, slot):
        for b in range(BINS):
            gg_s[:, bin_lanes(b)] = bin_onehot(idx_s, *meta.bin(tile * BINS + b), seq)
        gfs = [mm(wqkv_s[...], gq_s[slot, :, pair_lanes(t)]) for t in range(BINS // 2)]
        grads = []
        for b in range(BINS):
            lanes = bin_lanes(b)
            nhat = nhat1_s[slot, :, lanes].astype(F32)
            a = gfs[b // 2][:, bin_lanes(b % 2)] * col_s[...]
            m1 = jnp.mean(a, axis=0, keepdims=True)
            m2 = jnp.mean(a * nhat, axis=0, keepdims=True)
            rstd = rstd1_s[slot, 0:1, lanes]
            grads.append((gmid_s[slot, :, lanes].astype(F32) + rstd * (a - m1 - nhat * m2)).astype(BF16))
        for b in range(BINS):
            rows_s[slot, b] = mm(gg_s[:, bin_lanes(b)], grads[b], NT).astype(BF16)

    store_tiles(
        share,
        meta,
        [(idx_ref, idx_in), (wqkv_ref, wqkv_s)],
        [(nhat1_ref, nhat1_s), (rstd1_ref, rstd1_s), (gq_ref, gq_s), (gmid_ref, gmid_s)],
        sems,
        prepare,
        rows_of,
        rows_s,
        tg_ref,
        seq,
        out_sems,
    )


def store_tiles(share, meta, once, each, sems, prepare, rows_of, rows_s, to_ref, rows, out_sems):
    first, stop = share.start(meta.tiles()), share.stop(meta.tiles())
    done = stop - first

    def constant(act):
        for k, (ref, place) in enumerate(once):
            act(pltpu.make_async_copy(ref, place, sems.at[2, k]))

    def come(tile, slot, act):
        lanes = pl.ds(pl.multiple_of(jnp.bitwise_and(tile, 1) * TILE, TILE), TILE)
        for k, (ref, place) in enumerate(each):
            act(
                pltpu.make_async_copy(
                    ref.at[lax.shift_right_logical(tile, 1), :, lanes], place.at[slot], sems.at[slot, k]
                )
            )

    def leave(i, act):
        departures(meta, first + i, rows_s, jnp.bitwise_and(i, 1), to_ref, rows, out_sems, act)

    constant(lambda c: c.start())
    come(first, 0, lambda c: c.start())
    constant(lambda c: c.wait())
    prepare()

    def step(i, carry):
        slot = jnp.bitwise_and(i, 1)
        come(first + i, slot, lambda c: c.wait())

        @pl.when(i + 1 < done)
        def _():
            come(first + i + 1, 1 - slot, lambda c: c.start())

        @pl.when(i >= 2)
        def _():
            leave(i - 2, lambda c: c.wait())

        rows_of(first + i, slot)
        leave(i, lambda c: c.start())
        return carry

    lax.fori_loop(0, done, step, 0)

    @pl.when(done >= 2)
    def _():
        leave(done - 2, lambda c: c.wait())

    leave(done - 1, lambda c: c.wait())


def output_kernel(share, traj, meta_ref, bdn_ref, wdnt_ref, act_ref, mid_ref, *refs):
    lay_ref, wdnt_s, act_s, mid_s, sems, col_s, y_s, sel_s, rows_s, out_sems = refs[-10:]
    slots, d = lay_ref.shape[1:]
    meta = Meta(meta_ref, traj)

    def prepare():
        row = jnp.broadcast_to(bdn_ref[...].astype(F32).reshape(1, d), (8, d))
        col_s[...] = jnp.broadcast_to(row.T[:, 0:1], (d, BIN))

    def rows_of(tile, slot):
        mlps = [mm(wdnt_s[...], act_s[slot, :, pair_lanes(t)]) for t in range(BINS // 2)]
        for b in range(BINS):
            sel_s[b] = bin_slots(*meta.bin(tile * BINS + b)[2:])
        for t in range(BINS // 2):
            lanes = pair_lanes(t)
            y_s[:, lanes] = (mlps[t] + mid_s[slot, :, lanes].astype(F32) + two(col_s[...])).astype(BF16)
        for b in range(BINS):
            rows_s[slot, b] = mm(sel_s[b], y_s[:, bin_lanes(b)], NT).astype(BF16)

    store_tiles(
        share,
        meta,
        [(wdnt_ref, wdnt_s)],
        [(act_ref, act_s), (mid_ref, mid_s)],
        sems,
        prepare,
        rows_of,
        rows_s,
        lay_ref,
        slots,
        out_sems,
    )


CORE, Y, X, Z = 0, 1, 2, 3


def row_at(const=0, **bits):
    return const, tuple(({"core": CORE, "y": Y, "x": X, "z": Z}[name], coef) for name, coef in bits.items())


def mine(bit, rows, base=0):
    return base, ((bit, rows),)


def other(bit, rows, base=0):
    return base + rows, ((bit, -rows),)


class Step:
    def __init__(self, inputs, out_rows, parts, sends=()):
        self.inputs, self.out_rows, self.parts, self.sends = list(inputs), list(out_rows), list(parts), dict(sends)


def combine_kernel(step, bits_at, meta_ref, *refs):
    ins, outs = refs[: len(step.inputs)], refs[len(step.inputs) :]

    def row(start):
        if isinstance(start, int):
            return start
        const, bits = start
        for bit, coef in bits:
            const = const + meta_ref[bits_at + bit] * coef
        return const

    def rows(start, n):
        return pl.ds(start if isinstance(start, int) else pl.multiple_of(start, 8), n)

    for n, terms, goes in step.parts:
        for out, start, first, count in goes:
            total = None
            for ref, at in terms:
                term = ins[ref][rows(row(at) + row(first), count), :]
                total = term if total is None else total + term
            outs[out][rows(row(start), count), :] = total


def combine(step, meta, bits_at, width):
    vmem = pl.BlockSpec(memory_space=pltpu.VMEM)
    return pl.pallas_call(
        lambda *refs: combine_kernel(step, bits_at, *refs),
        in_specs=[pl.BlockSpec(memory_space=pltpu.SMEM)] + [vmem] * len(step.inputs),
        out_specs=[vmem] * len(step.out_rows),
        out_shape=[jax.ShapeDtypeStruct((n, width), F32) for n in step.out_rows],
        compiler_params=pltpu.CompilerParams(vmem_limit_bytes=2 * MIB),
        name="combine",
    )(meta, *step.inputs)


def bucket_sum(bits, keep, send, half, halve_z):
    h, e, f = half // 4, half // 8, half // 16
    _, (got,) = yield Step([send], [], [], {0: (CORE,)})

    def part(x, y):
        return (0 if x else 2 * h) + (0 if y else h), ((X, 2 * h if x else -2 * h), (Y, h if y else -h))

    (k, _, _, _), got = yield Step(
        [keep, got],
        [h] * 4,
        [
            (h, [(0, part(x, y)), (1, part(x, y))], [(out, row_at(), 0, h)])
            for out, (x, y) in enumerate(((True, True), (False, True), (True, False), (False, False)))
        ],
        {1: (X,), 2: (Y,), 3: (X, Y)},
    )
    four = [k, *got]
    if halve_z:
        (z, _), (got,) = yield Step(
            four,
            [e, e],
            [
                (
                    e,
                    [(n, row_at(c * e)) for n in range(4)],
                    [(0, row_at(c * f), mine(Z, f), f), (1, row_at(c * f), other(Z, f), f)],
                )
                for c in range(2)
            ],
            {1: (Z,)},
        )
        for bit in [*range(Z + 1, bits), Z]:
            (z,), (got,) = yield Step(
                [z, got], [e], [(e, [(0, row_at()), (1, row_at())], [(0, row_at(), 0, e)])], {0: (bit,)}
            )
        (e0, e1), (g0, g1) = yield Step(
            [z, got],
            [e, e],
            [
                (f, [(ref, row_at(c * f))], [(c, side(Z, f), 0, f)])
                for ref, side in enumerate((mine, other))
                for c in range(2)
            ],
            {0: (Y,), 1: (X,)},
        )
    else:
        (z,), (got,) = yield Step(
            four, [h], [(h, [(n, row_at()) for n in range(4)], [(0, row_at(), 0, h)])], {0: (bits - 1,)}
        )
        for bit in range(bits - 2, Z - 1, -1):
            (z,), (got,) = yield Step(
                [z, got], [h], [(h, [(0, row_at()), (1, row_at())], [(0, row_at(), 0, h)])], {0: (bit,)}
            )
        (e0, e1), (g0, g1) = yield Step(
            [z, got],
            [e, e],
            [(h, [(0, row_at()), (1, row_at())], [(0, row_at(), 0, e), (1, row_at(), e, e)])],
            {0: (Y,), 1: (X,)},
        )
    (f0, f1), (g0, g1) = yield Step(
        [e0, e1, g0, g1],
        [h, h],
        [
            (e, [(0, row_at())], [(0, mine(Y, e), 0, e)]),
            (e, [(2, row_at())], [(0, other(Y, e), 0, e)]),
            (e, [(1, row_at())], [(1, mine(X, e), 0, e)]),
            (e, [(3, row_at())], [(1, other(X, e), 0, e)]),
        ],
        {0: (X,), 1: (Y,)},
    )
    (near,), (far,) = yield Step(
        [f0, f1, g0, g1],
        [half],
        [
            (h, [(0, row_at())], [(0, mine(X, 2 * h, y * h), y * e, e) for y in range(2)]),
            (h, [(2, row_at())], [(0, other(X, 2 * h, y * h), y * e, e) for y in range(2)]),
            (h, [(1, row_at())], [(0, mine(Y, h, x * 2 * h + e), x * e, e) for x in range(2)]),
            (h, [(3, row_at())], [(0, other(Y, h, x * 2 * h + e), x * e, e) for x in range(2)]),
        ],
        {0: (CORE,)},
    )
    return near, far


class Sums:
    def __init__(self, ranks, meta, bits_at, width):
        self.ranks, self.meta, self.bits_at, self.width = ranks, meta, bits_at, width
        self.arrays, self.arrived, self.sent = [], [], []
        self.running, self.results = {}, {}

    def view(self, array):
        self.arrays.append(array)
        return (len(self.arrays) - 1, 0)

    def add(self, name, steps):
        self.running[name] = (steps, next(steps))

    def advance(self, after=None):
        if after is not None and self.arrived:
            tied = lax.optimization_barrier((*[self.arrays[k] for k in self.arrived], after))
            for k, array in zip(self.arrived, tied):
                self.arrays[k] = array
        inputs, out_rows, parts, places, sends = [], [], [], {}, {}
        for name, (_, step) in self.running.items():
            outs = []
            for out, rows in enumerate(step.out_rows):
                bit = step.sends.get(out)
                if bit in sends:
                    at = sends[bit]
                    outs.append((at, out_rows[at]))
                    out_rows[at] += rows
                    continue
                if bit is not None:
                    sends[bit] = len(out_rows)
                outs.append((len(out_rows), 0))
                out_rows.append(rows)
            places[name] = outs
            for rows, terms, goes in step.parts:
                moved = []
                for ref, (const, bits) in terms:
                    k, row = step.inputs[ref]
                    if k not in inputs:
                        inputs.append(k)
                    moved.append((inputs.index(k), (const + row, bits)))
                parts.append(
                    (
                        rows,
                        moved,
                        [(outs[out][0], (const + outs[out][1], bits), *rest) for out, (const, bits), *rest in goes],
                    )
                )
        base = len(self.arrays)
        if out_rows:
            merged = Step([self.arrays[k] for k in inputs], out_rows, parts)
            self.arrays += list(combine(merged, self.meta, self.bits_at, self.width))
        to_send = {bit: base + out for bit, out in sends.items()}
        raw = {name: step for name, (_, step) in self.running.items() if not step.parts}
        for step in raw.values():
            for out, bit in step.sends.items():
                to_send[(bit, id(step))] = step.inputs[out][0]
        self.sent = [self.arrays[k] for k in to_send.values()]
        received = {}
        for key, k in to_send.items():
            mask = sum(1 << bit for bit in (key[0] if isinstance(key[0], tuple) else key))
            perm = [(r, r ^ mask) for r in range(self.ranks)]
            received[key] = self.view(lax.ppermute(self.arrays[k], AXES, perm))[0]
        self.arrived = list(received.values())
        for name, (steps, step) in list(self.running.items()):
            if name in raw:
                outs = []
                got = [(received[(bit, id(step))], 0) for bit in step.sends.values()]
            else:
                outs = [(base + out, row) for out, row in places[name]]
                got = [(received[bit], places[name][out][1]) for out, bit in step.sends.items()]
            try:
                self.running[name] = (steps, steps.send((outs, got)))
            except StopIteration as stop:
                self.results[name] = stop.value
                del self.running[name]

    def ordered(self, value):
        return lax.optimization_barrier((value, *self.sent))[0]


def finish_kernel(
    bits_at, rows_at, meta_ref, late0_ref, late1_ref, first0_ref, first1_ref, g1_ref, c1_ref, wqkv_ref, wup_ref,
    dwn_ref, dup_ref, dwo_ref, dqkv_ref, dg1_ref, dc1_ref, dbq_ref, dbv_ref, dbo_ref, dg2_ref, dc2_ref, dbup_ref, dbdn_ref,
    late_s, first_s, first_sem, late_sem, out_sem,
):
    ff, d = dwn_ref.shape
    core = meta_ref[bits_at + CORE]
    late_near, late_far, first_near, first_far = rows_at
    first, late = [], []
    for to_s, copies, sems, sides in (
        (late_s, late, late_sem, ((late0_ref, late_near, core), (late1_ref, late_far, 1 - core))),
        (first_s, first, first_sem, ((first0_ref, first_near, core), (first1_ref, first_far, 1 - core))),
    ):
        half = to_s.shape[0] // 2
        for k, (ref, row, side) in enumerate(sides):
            to = to_s.at[pl.ds(pl.multiple_of(side * half, 8), half)]
            copies.append(pltpu.make_async_copy(ref.at[pl.ds(row, half)], to, sems.at[k]))
    for copy in late + first:
        copy.start()
    for copy in late:
        copy.wait()
    copies = [
        pltpu.make_async_copy(late_s.at[pl.ds(0, ff)], dwn_ref, out_sem.at[0]),
        pltpu.make_async_copy(late_s.at[pl.ds(2 * ff, d)], dwo_ref, out_sem.at[1]),
    ]
    for copy in copies:
        copy.start()
    for j in range(ff // d):
        dup_ref[:, j * d : (j + 1) * d] = late_s[ff + j * d : ff + (j + 1) * d, :].T
    for copy in first:
        copy.wait()

    def late_row(j):
        return first_s[3 * d + 3 + j : 3 * d + 4 + j, :].reshape(d)

    dg2_ref[...] = late_row(0)
    for j in range(ff // d):
        dbup_ref[j * d : (j + 1) * d] = late_row(1 + j)
    dbdn_ref[...] = late_row(5)
    dbo_ref[...] = late_row(6)

    def times(weight_ref, row, n):
        total = jnp.zeros((8, d), F32)
        for j in range(n):
            left = jnp.broadcast_to(first_s[row + j : row + j + 1, :], (8, d))
            for _ in range(3):
                low = left.astype(BF16)
                left = left - low.astype(F32)
                total = total + mm(low, weight_ref[:, j * d : (j + 1) * d], NT)
        return total[0:1, :]

    dc2_ref[...] = times(wup_ref, 3 * d + 4, ff // d).reshape(d)
    dc1_ref[...] = times(wqkv_ref, 3 * d, 3).reshape(d)

    gain = jnp.broadcast_to(g1_ref[...].astype(F32).reshape(1, d), (8, d)).T[:, 0:1]
    bias = jnp.broadcast_to(c1_ref[...].astype(F32).reshape(1, d), (8, d)).T[:, 0:1]
    gain_grad = jnp.zeros((d, d), F32)
    for j in range(3):
        block = slice(j * d, (j + 1) * d)
        total = first_s[3 * d + j : 3 * d + j + 1, :]
        product = first_s[block, :].T
        weight = wqkv_ref[:, block].astype(F32)
        dqkv_ref[:, block] = gain * product + bias * total
        gain_grad += weight * product
    dg1_ref[...] = jnp.sum(gain_grad.T, axis=0, keepdims=True).reshape(d)
    dbq_ref[...] = first_s[3 * d : 3 * d + 1, :].reshape(d)
    dbv_ref[...] = first_s[3 * d + 2 : 3 * d + 3, :].reshape(d)
    for copy in copies:
        copy.wait()


def doubled(shape):
    if len(shape) == 3:
        return (2 * shape[0],) + shape[1:]
    return shape[:-1] + (2 * shape[-1],)


SHARES_C = shares(0, 10, 16)
SHARES_D = shares(0, 5, 8, 16)


def body(
    ranks,
    tokens,
    visible_index,
    visible_count,
    ln1_gain,
    ln1_bias,
    qkv_weight,
    query_bias,
    value_bias,
    out_weight,
    out_bias,
    ln2_gain,
    ln2_bias,
    up_weight,
    up_bias,
    down_weight,
    down_bias,
    out_grad,
):
    traj, slots = visible_index.shape
    seq, d = tokens.shape[1:]
    ff = up_weight.shape[1]
    hs = d // HEADS
    steps_a = -(-traj // BINS_A)
    tiles = 2 * steps_a
    tiles_at = Meta.size(traj) - 16
    bits = ranks.bit_length() - 1
    rank = lax.axis_index(AXES).astype(jnp.int32).reshape(1)
    meta = make_plan(visible_count, rank, slots)
    sums = Sums(ranks, meta, tiles_at + 1, d)

    shapes = dict(
        nhat=((d, TILE), BF16),
        rstd=((8, TILE), F32),
        qkv=((3 * d, TILE), BF16),
        prob=((BINS, BIN, HEADS * BIN), BF16),
        gatt=((d, TILE), BF16),
        gmid=((d, TILE), BF16),
        act=((ff, TILE), BF16),
        mid=((d, TILE), BF16),
    )

    def stored(name):
        shape, kind = shapes[name]
        return jax.ShapeDtypeStruct((steps_a,) + doubled(shape), kind)

    smem, vmem = (pl.BlockSpec(memory_space=m) for m in (pltpu.SMEM, pltpu.VMEM))

    def step_places(*names):
        return [pltpu.VMEM((2,) + doubled(shapes[n][0]), shapes[n][1]) for n in names]

    late_shape = (2 * ff + d, d)
    vectors = [ln1_gain, ln1_bias, query_bias, value_bias, out_bias, ln2_gain, ln2_bias, up_bias]
    weights = [qkv_weight, out_weight, up_weight, down_weight]
    down_weight_t, nhat, rstd, qkv, prob, gatt, gmid, act, mid, late_keep, late_send, late_vectors = pl.pallas_call(
        late_kernel,
        in_specs=[smem, vmem, HBM, HBM] + [vmem] * len(vectors + weights),
        out_specs=[vmem] + [HBM] * len(shapes) + [vmem] * 3,
        scratch_shapes=[
            pltpu.VMEM((2, BINS_A, 2 * seq, d), BF16),
            pltpu.VMEM((2, BINS_A, 2 * BIN, d), BF16),
            pltpu.SemaphoreType.DMA((2, BINS_A, 2, 2)),
            *step_places(*shapes),
            pltpu.SemaphoreType.DMA((2, 8)),
            pltpu.VMEM((traj, BIN), jnp.int32),
            pltpu.VMEM((16, d), F32),
            pltpu.VMEM((12 * d, BIN), F32),
            pltpu.VMEM((3 * d, d), BF16),
            pltpu.VMEM((d, d), BF16),
            pltpu.VMEM((ff, d), BF16),
            pltpu.VMEM((d, TILE_A), F32),
            pltpu.VMEM((d, TILE_A), BF16),
            pltpu.VMEM((BINS_A * HEADS // 2, 2 * hs, PAIR), BF16),
            pltpu.VMEM((BINS_A * HEADS // 2, BIN, PAIR), F32),
            pltpu.VMEM((d, TILE_A), BF16),
            pltpu.VMEM((d, TILE_A), F32),
            pltpu.VMEM((d, TILE_A), BF16),
            pltpu.VMEM((d, TILE_A), BF16),
            pltpu.VMEM((ff, TILE_A), BF16),
            pltpu.VMEM((ff, TILE_A), BF16),
            pltpu.VMEM((ff, TILE_A), BF16),
            pltpu.VMEM((d, TILE_A), F32),
            pltpu.VMEM((d, TILE_A), F32),
            pltpu.VMEM(late_shape, F32),
            pltpu.VMEM((3 * d + ff, BIN), F32),
        ],
        out_shape=[jax.ShapeDtypeStruct((d, ff), BF16)]
        + [stored(n) for n in shapes]
        + [jax.ShapeDtypeStruct(n, F32) for n in ((late_shape[0] // 2, d), (late_shape[0] // 2, d), (8, d))],
        compiler_params=pltpu.CompilerParams(vmem_limit_bytes=58 * MIB),
        name="forward_mlp",
    )(meta, visible_index, tokens, out_grad, *vectors, *weights)
    late = bucket_sum(bits, sums.view(late_keep), sums.view(late_send), late_shape[0] // 2, True)
    sums.add("late", late)
    sums.advance()

    acc_shape = (-(-(3 * d + 11) // 128) * 128, d)
    send_shape = (acc_shape[0] // 2, d)
    grad_qkv, first_keep, first_send = pl.pallas_call(
        lambda *refs: attention_kernel(traj, *refs),
        in_specs=[smem] + [HBM] * 4 + [vmem],
        out_specs=[HBM, vmem, vmem],
        scratch_shapes=step_places("nhat", "qkv", "prob", "gatt")
        + [pltpu.VMEM((2, 3 * d, TILE_A), BF16), pltpu.SemaphoreType.DMA((2, 4)), pltpu.SemaphoreType.DMA((2,))]
        + [pltpu.VMEM((BINS_A * HEADS // 2, 2 * hs, PAIR), BF16)] * 2
        + [
            pltpu.VMEM((BINS_A * HEADS // 2, BIN, PAIR), F32),
            pltpu.VMEM((BINS_A * HEADS // 2, BIN, PAIR), BF16),
            pltpu.VMEM((3 * d, BIN), F32),
            pltpu.VMEM(acc_shape, F32),
        ],
        out_shape=[jax.ShapeDtypeStruct((steps_a, 3 * d, TILE_A), BF16)] + [jax.ShapeDtypeStruct(send_shape, F32)] * 2,
        compiler_params=pltpu.CompilerParams(vmem_limit_bytes=56 * MIB),
        cost_estimate=pl.CostEstimate(flops=5 * 10**9, bytes_accessed=16 * 10**6, transcendentals=0),
        name="attention_backward",
    )(sums.ordered(meta), nhat, qkv, prob, gatt, late_vectors)
    first = bucket_sum(bits, sums.view(first_keep), sums.view(first_send), send_shape[0], False)
    sums.add("first", first)
    sums.advance(first_keep)

    def tile_places(*names):
        shapes_of = dict(shapes, gq=((3 * d, TILE), BF16))
        return [pltpu.VMEM((2,) + shapes_of[n][0], shapes_of[n][1]) for n in names]

    def stores(kernel, name, vector, inputs, rows, scratch, earlier):
        given = [] if earlier is None else [earlier]
        return pl.pallas_call(
            kernel,
            in_specs=[smem, vmem] + [HBM] * (len(inputs) + len(given)),
            out_specs=HBM,
            scratch_shapes=scratch
            + [pltpu.VMEM((2, BINS, 2 * BIN, d), BF16), pltpu.SemaphoreType.DMA((2, BINS, 2))],
            out_shape=jax.ShapeDtypeStruct((traj, rows, d), BF16),
            input_output_aliases={2 + len(inputs): 0} if given else {},
            compiler_params=pltpu.CompilerParams(vmem_limit_bytes=56 * MIB),
            cost_estimate=pl.CostEstimate(flops=2 * 10**9, bytes_accessed=8 * 10**6, transcendentals=0),
            name=name,
        )(sums.ordered(meta), vector, *inputs, *given)

    tokens_grad = None
    for share in SHARES_C:
        tokens_grad = stores(
            lambda *refs, share=share: token_kernel(share, *refs),
            "tokens_backward",
            ln1_gain,
            [visible_index, qkv_weight, nhat, rstd, grad_qkv, gmid],
            seq,
            [pltpu.VMEM((traj, slots), jnp.int32), pltpu.VMEM((d, 3 * d), BF16)]
            + tile_places("nhat", "rstd", "gq", "gmid")
            + [pltpu.SemaphoreType.DMA((3, 4))]
            + [pltpu.VMEM((traj, BIN), jnp.int32), pltpu.VMEM((d, BIN), F32), pltpu.VMEM((d, TILE), BF16)],
            tokens_grad,
        )
        sums.advance(tokens_grad)
        if share is SHARES_C[0]:
            sums.advance()
    layer_out = None
    for share in SHARES_D:
        layer_out = stores(
            lambda *refs, share=share: output_kernel(share, traj, *refs),
            "layer_output",
            down_bias,
            [down_weight_t, act, mid],
            slots,
            [pltpu.VMEM((d, ff), BF16)]
            + tile_places("act", "mid")
            + [pltpu.SemaphoreType.DMA((3, 4))]
            + [pltpu.VMEM((d, BIN), F32), pltpu.VMEM((d, TILE), BF16), pltpu.VMEM((BINS, 2 * BIN, BIN), BF16)],
            layer_out,
        )
        sums.advance(layer_out)
    while sums.running:
        sums.advance()
    views = sums.results["late"] + sums.results["first"]
    near_far = [sums.arrays[k] for k, _ in views]
    rows_at = tuple(row for _, row in views)

    vmem = pl.BlockSpec(memory_space=pltpu.VMEM)
    vector = jax.ShapeDtypeStruct((d,), F32)
    dwn, dup, dwo, dqkv, dg1, dc1, dbq, dbv, dbo, dg2, dc2, dbup, dbdn = pl.pallas_call(
        lambda *refs: finish_kernel(tiles_at + 1, rows_at, *refs),
        in_specs=[pl.BlockSpec(memory_space=pltpu.SMEM)] + [HBM] * 4 + [vmem] * 4,
        out_specs=[HBM, vmem, HBM] + [vmem] * 10,
        out_shape=[
            jax.ShapeDtypeStruct((ff, d), F32),
            jax.ShapeDtypeStruct((d, ff), F32),
            jax.ShapeDtypeStruct((d, d), F32),
            jax.ShapeDtypeStruct((d, 3 * d), F32),
        ]
        + [vector] * 7
        + [jax.ShapeDtypeStruct((ff,), F32), vector],
        scratch_shapes=[
            pltpu.VMEM(late_shape, F32),
            pltpu.VMEM(acc_shape, F32),
            pltpu.SemaphoreType.DMA((2,)),
            pltpu.SemaphoreType.DMA((2,)),
            pltpu.SemaphoreType.DMA((2,)),
        ],
        compiler_params=pltpu.CompilerParams(vmem_limit_bytes=24 * MIB),
        name="finish",
    )(meta, *near_far, ln1_gain, ln1_bias, qkv_weight, up_weight)
    return layer_out, tokens_grad, dg1, dc1, dqkv, dbq, dbv, dwo, dbo, dg2, dc2, dup, dbup, dwn, dbdn


def solution(mesh):
    devices = mesh.devices
    ranks = devices.size
    mesh = Mesh(devices.reshape(devices.shape[0], devices.shape[1] // 2, 2), AXES)
    rows = P(AXES)
    placed = (rows, rows, rows) + (P(),) * 13 + (rows,)
    return jax.shard_map(
        lambda *args: body(ranks, *args),
        mesh=mesh,
        in_specs=placed,
        out_specs=(rows, rows) + (P(),) * 13,
        check_vma=False,
    )
```

```python
import jax
import jax.numpy as jnp
from jax import lax
from jax.experimental import pallas as pl
from jax.experimental.pallas import tpu as pltpu
from jax.sharding import Mesh, PartitionSpec as P

AXES = ("wide", "square", "core")
HEADS = 4
EPS = 1e-05
BIN = 128
PAIR = 2 * BIN
BINS = 4
TILE = BINS * BIN
BINS_A = 8
TILE_A = BINS_A * BIN
F32 = jnp.float32
BF16 = jnp.bfloat16
GELU_A = 0.7978845608028654
GELU_B = 0.044715 * GELU_A

NN = (((1,), (0,)), ((), ()))
NT = (((1,), (1,)), ((), ()))
TN = (((0,), (0,)), ((), ()))

MIB = 1024 * 1024
HBM = pl.BlockSpec(memory_space=pl.ANY)


def mm(left, right, dims=NN):
    return lax.dot_general(left, right, dims, preferred_element_type=F32)


class Meta:
    def __init__(self, ref, traj):
        self.ref = ref
        self.width = traj + 8

    @staticmethod
    def size(traj):
        return 4 * (traj + 8) + 16

    def bin(self, b):
        return tuple(self.ref[j * self.width + b] for j in range(4))

    def put(self, b, *values):
        for j, value in enumerate(values):
            self.ref[j * self.width + b] = value

    @property
    def tiles_at(self):
        return 4 * self.width

    def tiles(self):
        return self.ref[self.tiles_at]

    def bins(self):
        return self.ref[self.tiles_at + 15]

    def bit(self, b):
        return self.ref[self.tiles_at + 1 + b]


def plan_kernel(count_ref, rank_ref, meta_ref, first_ref, order_ref):
    traj = count_ref.shape[0]
    top = first_ref.shape[0]
    meta = Meta(meta_ref, traj)

    def clear(v, carry):
        first_ref[v] = 0
        return carry

    lax.fori_loop(0, top, clear, 0, unroll=16)

    def tally(t, carry):
        c = count_ref[t]
        first_ref[c] = first_ref[c] + 1
        return carry

    lax.fori_loop(0, traj, tally, 0, unroll=8)

    def starts(i, run):
        v = top - 1 - i
        n = first_ref[v]
        first_ref[v] = run
        return run + n

    lax.fori_loop(0, top, starts, 0, unroll=16)

    def place(t, carry):
        c = count_ref[t]
        at = first_ref[c]
        order_ref[at] = t
        first_ref[c] = at + 1
        return carry

    lax.fori_loop(0, traj, place, 0, unroll=8)

    def pair(carry):
        hi, lo, n = carry
        t_hi = order_ref[hi]
        t_lo = order_ref[lo]
        c_hi = count_ref[t_hi]
        c_lo = count_ref[t_lo]
        fits = jnp.logical_and(hi < lo, c_hi + c_lo <= BIN)
        meta.put(n, t_hi, jnp.where(fits, t_lo, t_hi), c_hi, jnp.where(fits, c_lo, 0))
        return hi + 1, jnp.where(fits, lo - 1, lo), n + 1

    _, _, n = lax.while_loop(lambda c: c[0] <= c[1], pair, (jnp.int32(0), jnp.int32(traj - 1), jnp.int32(0)))
    last = meta_ref[n - 1]
    for j in range(BINS_A - 1):
        meta.put(n + j, last, last, 0, 0)
    meta_ref[meta.tiles_at] = lax.shift_right_logical(n + BINS - 1, BINS.bit_length() - 1)
    meta_ref[meta.tiles_at + 15] = n
    for b in range(14):
        meta_ref[meta.tiles_at + 1 + b] = jnp.bitwise_and(lax.shift_right_logical(rank_ref[0], b), 1)


def make_plan(counts, rank, slots):
    traj = counts.shape[0]
    smem = pl.BlockSpec(memory_space=pltpu.SMEM)
    return pl.pallas_call(
        plan_kernel,
        in_specs=[smem, smem],
        out_specs=smem,
        out_shape=jax.ShapeDtypeStruct((Meta.size(traj),), jnp.int32),
        scratch_shapes=[pltpu.SMEM((-(-(slots + 1) // 16) * 16,), jnp.int32), pltpu.SMEM((traj,), jnp.int32)],
        name="plan",
    )(counts, rank)


def bin_onehot(idx_ref, ta, tb, ca, cb, seq):
    lane = lax.broadcasted_iota(jnp.int32, (8, BIN), 1)
    ia = jnp.broadcast_to(idx_ref[pl.ds(ta, 1), :], (8, BIN))
    ib = jnp.broadcast_to(idx_ref[pl.ds(tb, 1), :], (8, BIN))
    ib = pltpu.roll(ib, ca, 1)
    code = jnp.where(lane < ca, ia, jnp.where(lane < ca + cb, ib + seq, -1))[0:1, :]
    pos = lax.broadcasted_iota(jnp.int32, (2 * seq, BIN), 0)
    return jnp.where(pos == code, 1.0, 0.0).astype(BF16)


def bin_slots(ca, cb):
    row = lax.broadcasted_iota(jnp.int32, (BIN, BIN), 0)
    lane = lax.broadcasted_iota(jnp.int32, (BIN, BIN), 1)
    first = jnp.logical_and(lane == row, row < ca)
    second = jnp.logical_and(lane == row + ca, row < cb)
    return jnp.concatenate([jnp.where(x, 1.0, 0.0).astype(BF16) for x in (first, second)], axis=0)


def bin_mask(ca, cb):
    row = lax.broadcasted_iota(jnp.int32, (BIN, BIN), 0)
    lane = lax.broadcasted_iota(jnp.int32, (BIN, BIN), 1)
    key = jnp.where(row < ca, 0, jnp.where(row < ca + cb, 1, 2))
    query = jnp.where(lane < ca, 0, jnp.where(lane < ca + cb, 1, 3))
    return jnp.where(key == query, 0.0, -1e30)


def center(x):
    mean = jnp.mean(x, axis=0, keepdims=True)
    xc = x - mean
    var = jnp.mean(xc * xc, axis=0, keepdims=True)
    rstd = lax.rsqrt(var + EPS)
    return xc * rstd, rstd


def lanes_into_rows(acc):
    return jnp.sum(acc.T, axis=0, keepdims=True)


def two(x):
    return jnp.concatenate([x, x], axis=1)


def bin_lanes(b):
    return slice(b * BIN, (b + 1) * BIN)


def pair_lanes(t):
    return slice(t * PAIR, (t + 1) * PAIR)


def wait_rows(place, rows, sem):
    _, m, _ = place.shape
    parts = [place.at[pl.ds(0, rows // m)]] if rows >= m else []
    if rows % m:
        parts.append(place.at[pl.ds(0, 1), pl.ds(0, rows % m)])
    for part in parts:
        pltpu.make_async_copy(part, part, sem).wait()


def departures(meta, tile, rows_s, slot, to_ref, rows, sems):
    half = rows_s.shape[2] // 2
    last = jnp.bitwise_and(meta.bins() - 1, BINS - 1)
    for b in range(BINS):
        ta, tb, ca, cb = meta.bin(tile * BINS + b)
        source = jnp.where(ca > 0, b, last)
        for part, (t, row) in enumerate(((ta, 0), (tb, jnp.where(cb > 0, half, 0)))):
            rows_of_t = pl.ds(pl.multiple_of(row, half) if part else 0, rows)
            pltpu.make_async_copy(rows_s.at[slot, source, rows_of_t], to_ref.at[t], sems.at[slot]).start()


class Share:
    def __init__(self, first, last):
        self.first, self.last = first, last

    def start(self, tiles):
        return lax.shift_right_logical(tiles * self.first, 4)

    def stop(self, tiles):
        return lax.shift_right_logical(tiles * self.last, 4)


def shares(*cuts):
    return [Share(a, b) for a, b in zip(cuts[:-1], cuts[1:])]


def keep_half(meta, acc_s, keep_ref, send_ref):
    half = keep_ref.shape[0]
    core = meta.bit(CORE)
    keep_ref[...] = acc_s[pl.ds(pl.multiple_of(core * half, 8), half), :]
    send_ref[...] = acc_s[pl.ds(pl.multiple_of((1 - core) * half, 8), half), :]


def late_kernel(
    meta_ref,
    idx_ref,
    tok_ref,
    og_ref,
    g1_ref,
    c1_ref,
    bq_ref,
    bv_ref,
    bo_ref,
    g2_ref,
    c2_ref,
    bup_ref,
    wqkv_ref,
    wo_ref,
    wup_ref,
    wdn_ref,
    wdnt_s,
    nhat1_hbm,
    rstd1_hbm,
    qkv_hbm,
    prob_hbm,
    gatt_hbm,
    gmid_hbm,
    act_hbm,
    mid_hbm,
    keep_ref,
    send_ref,
    dvec_ref,
    tok_s,
    og_s,
    in_sem,
    nhat1_b,
    rstd1_b,
    qkv_b,
    prob_b,
    gatt_b,
    gmid_b,
    act_b,
    mid_b,
    out_sem,
    idx_s,
    vec_s,
    col_s,
    wqkvt_s,
    wot_s,
    wupt_s,
    gath_s,
    first_s,
    bd_s,
    score_s,
    att_s,
    nhat_s,
    sec_s,
    gm_s,
    u_s,
    ga_s,
    gp_s,
    mid_s,
    gs_s,
    acc_s,
    bacc_s,
):
    traj, seq, d = tok_ref.shape
    slots = og_ref.shape[1]
    ff = wup_ref.shape[1]
    hs = d // HEADS
    scale = hs**-0.5
    meta = Meta(meta_ref, traj)
    steps = lax.shift_right_logical(meta.tiles() + 1, 1)

    def arrivals(i, slot):
        for b in range(BINS_A):
            for part, t in enumerate(meta.bin(i * BINS_A + b)[0:2]):
                to_tok = tok_s.at[slot, b, pl.ds(part * seq, seq)]
                to_og = og_s.at[slot, b, pl.ds(part * BIN, slots)]
                pltpu.make_async_copy(tok_ref.at[t], to_tok, in_sem.at[slot, 0]).start()
                pltpu.make_async_copy(og_ref.at[t], to_og, in_sem.at[slot, 1]).start()

    def wait_arrivals(slot):
        wait_rows(tok_s.at[slot], 2 * BINS_A * seq, in_sem.at[slot, 0])
        wait_rows(og_s.at[slot], 2 * BINS_A * slots, in_sem.at[slot, 1])

    saved = (
        (nhat1_b, nhat1_hbm), (rstd1_b, rstd1_hbm), (qkv_b, qkv_hbm), (prob_b, prob_hbm),
        (act_b, act_hbm), (mid_b, mid_hbm), (gatt_b, gatt_hbm), (gmid_b, gmid_hbm),
    )

    def departures(i, which, act):
        slot = jnp.bitwise_and(i, 1)
        for k in which:
            place, ref = saved[k]
            act(pltpu.make_async_copy(place.at[slot], ref.at[i], out_sem.at[slot, k]))

    for part in range(2):
        og_s[:, :, part * BIN + slots : (part + 1) * BIN, :] = jnp.zeros((2, BINS_A, BIN - slots, d), BF16)
    arrivals(0, 0)
    idx_s[...] = jnp.zeros_like(idx_s)
    idx_s[:, 0:slots] = idx_ref[...]
    vec_s[...] = jnp.zeros_like(vec_s)
    rows = [(0, g1_ref), (1, c1_ref), (2, bq_ref), (4, bv_ref), (5, bo_ref), (6, g2_ref), (7, c2_ref)]
    for j, ref in rows:
        vec_s[j : j + 1, :] = ref[...].astype(F32).reshape(1, d)
    for j in range(ff // d):
        vec_s[8 + j : 9 + j, :] = bup_ref[j * d : (j + 1) * d].astype(F32).reshape(1, d)
    vec_s[2:3, :] = vec_s[2:3, :] * scale
    cols = vec_s[...].T
    for j in range(12):
        col_s[j * d : (j + 1) * d, :] = jnp.broadcast_to(cols[:, j : j + 1], (d, BIN))
    wqkvt_s[...] = wqkv_ref[...].T
    wqkvt_s[0:d, :] = (wqkvt_s[0:d, :].astype(F32) * scale).astype(BF16)
    wot_s[...] = wo_ref[...].T
    wupt_s[...] = wup_ref[...].T
    wdnt_s[...] = wdn_ref[...].T
    bd_s[...] = jnp.zeros_like(bd_s)
    bacc_s[...] = jnp.zeros_like(bacc_s)
    acc_s[...] = jnp.zeros_like(acc_s)

    def col(j, n=1):
        return col_s[j * d : (j + n) * d, :]

    def work_on(step, carry):
        slot = jnp.bitwise_and(step, 1)
        wait_arrivals(slot)

        @pl.when(step >= 2)
        def _():
            departures(step - 2, range(8), lambda c: c.wait())

        nhat1_ref, rstd1_ref, qkv_ref, prob_ref, act_ref, mid_ref, gatt_ref, gmid_ref = (
            place.at[pl.ds(slot, 1)] for place, _ in saved
        )
        metas = [meta.bin(step * BINS_A + b) for b in range(BINS_A)]
        rstds = {}

        def gather(b):
            lanes = bin_lanes(b)
            gath_s[:, lanes] = mm(tok_s[slot, b], bin_onehot(idx_s, *metas[b], seq), TN)

        def first_norm(b):
            lanes = bin_lanes(b)
            nhat, rstd = center(gath_s[:, lanes])
            nhat1_ref[0, :, lanes] = nhat.astype(BF16)
            rstd1_ref[0, :, lanes] = jnp.broadcast_to(rstd, (8, BIN))
            first_s[:, lanes] = (nhat * col(0) + col(1)).astype(BF16)

        def cotangent(b):
            gm_s[:, bin_lanes(b)] = mm(og_s[slot, b], bin_slots(*metas[b][2:]), TN).astype(BF16)

        def project(t):
            lanes = pair_lanes(t)
            qkv_ref[0, :, lanes] = (mm(wqkvt_s[...], first_s[:, lanes]) + two(col(2, 3))).astype(BF16)

        def scores(b, p):
            lanes = bin_lanes(b)
            f0 = p * 2 * hs
            at = b * (HEADS // 2) + p
            bd_s[at, 0:hs, 0:BIN] = qkv_ref[0, f0 : f0 + hs, lanes]
            bd_s[at, hs : 2 * hs, BIN:PAIR] = qkv_ref[0, f0 + hs : f0 + 2 * hs, lanes]
            score_s[at] = mm(qkv_ref[0, d + f0 : d + f0 + 2 * hs, lanes], bd_s[at], TN)

        def softmax(b):
            mask = two(bin_mask(*metas[b][2:]))
            for p in range(HEADS // 2):
                s = score_s[b * (HEADS // 2) + p] + mask
                e = jnp.exp(s - jnp.max(s, axis=0, keepdims=True))
                prob_ref[0, b, :, pair_lanes(p)] = (e * (1.0 / jnp.sum(e, axis=0, keepdims=True))).astype(BF16)

        def attend(b, p):
            lanes = bin_lanes(b)
            f0 = p * 2 * hs
            both = mm(qkv_ref[0, 2 * d + f0 : 2 * d + f0 + 2 * hs, lanes], prob_ref[0, b, :, pair_lanes(p)])
            for h in range(2):
                att_s[f0 + h * hs : f0 + (h + 1) * hs, lanes] = both[h * hs : (h + 1) * hs, bin_lanes(h)].astype(BF16)

        def residual(t):
            lanes = pair_lanes(t)
            mid_s[:, lanes] = mm(wot_s[...], att_s[:, lanes])

        def second_norm(b):
            lanes = bin_lanes(b)
            mid = mid_s[:, lanes] + gath_s[:, lanes] + col(5)
            mid_ref[0, :, lanes] = mid.astype(BF16)
            nhat, rstds[b] = center(mid)
            nhat_s[:, lanes] = nhat
            sec_s[:, lanes] = (nhat * col(6) + col(7)).astype(BF16)

        def up(t):
            lanes = pair_lanes(t)
            u_s[:, lanes] = (mm(wupt_s[...], sec_s[:, lanes]) + two(col_s[8 * d : 8 * d + ff, :])).astype(BF16)
            ga_s[:, lanes] = mm(wdn_ref[...], gm_s[:, lanes]).astype(BF16)

        def gelu(t, rows):
            lanes = pair_lanes(t)
            u = u_s[rows, lanes]
            u2 = u * u
            sg = 0.5 * jnp.tanh(u * (u2 * GELU_B + GELU_A)) + 0.5
            act = u * sg
            gp = (act * (1.0 - sg) * (u2 * (6.0 * GELU_B) + 2.0 * GELU_A) + sg) * ga_s[rows, lanes]
            act_ref[0, rows, lanes] = act
            gp_s[rows, lanes] = gp
            bacc_s[d + rows.start : d + rows.stop, :] += (gp[:, 0:BIN] + gp[:, BIN:PAIR]).astype(F32)

        def grad_second(t):
            lanes = pair_lanes(t)
            gs_s[:, lanes] = mm(wup_ref[...], gp_s[:, lanes])

        def second_norm_back(b):
            lanes = bin_lanes(b)
            gs = gs_s[:, lanes]
            nhat = nhat_s[:, lanes]
            bacc_s[0:d, :] += gs * nhat
            a = gs * col(6)
            m1 = jnp.mean(a, axis=0, keepdims=True)
            m2 = jnp.mean(a * nhat, axis=0, keepdims=True)
            gm = gm_s[:, lanes].astype(F32)
            gmid = gm + rstds[b] * (a - m1 - nhat * m2)
            gmid_ref[0, :, lanes] = gmid.astype(BF16)
            bacc_s[d + ff : 2 * d + ff, :] += gm
            bacc_s[2 * d + ff : 3 * d + ff, :] += gmid

        def grad_attended(t):
            lanes = pair_lanes(t)
            gatt_ref[0, :, lanes] = mm(wo_ref[...], gmid_ref[0, :, lanes]).astype(BF16)

        def work(count):
            bins, tiles, chunk, lanes = range(count), range(count // 2), 64, slice(0, count * BIN)
            pairs = [[(b, p) for b in (2 * t, 2 * t + 1) for p in range(HEADS // 2)] for t in tiles]
            stages = dict(
                cotangent=lambda t: [cotangent(b) for b in (2 * t, 2 * t + 1)],
                first_norm=lambda t: [first_norm(b) for b in (2 * t, 2 * t + 1)],
                project=project,
                scores=lambda t: [scores(b, p) for b, p in pairs[t]],
                softmax=lambda t: [softmax(b) for b in (2 * t, 2 * t + 1)],
                attend=lambda t: [attend(b, p) for b, p in pairs[t]],
                residual=residual,
                second_norm=lambda t: [second_norm(b) for b in (2 * t, 2 * t + 1)],
                up=up,
                gelu=lambda t: [gelu(t, slice(j, j + chunk)) for j in range(0, ff, chunk)],
                grad_second=grad_second,
            )
            arrivals(jnp.minimum(step + 1, steps - 1), 1 - slot)
            for b in bins:
                gather(b)
            for when in range(len(tiles) + len(stages) - 1):
                for n, stage in enumerate(stages.values()):
                    if 0 <= when - n < len(tiles):
                        stage(when - n)
            departures(step, range(6), lambda c: c.start())
            acc_s[0:ff, :] += mm(act_ref[0, :, lanes], gm_s[:, lanes], NT)
            for b in bins[: count // 2]:
                second_norm_back(b)
            acc_s[ff : 2 * ff, :] += mm(gp_s[:, lanes], sec_s[:, lanes], NT)
            for b in bins[count // 2 :]:
                second_norm_back(b)
            acc_s[2 * ff : 2 * ff + d, :] += mm(att_s[:, lanes], gmid_ref[0, :, lanes], NT)
            for t in tiles:
                grad_attended(t)

        full = 2 * step + 1 < meta.tiles()

        @pl.when(full)
        def _():
            work(BINS_A)

        @pl.when(jnp.logical_not(full))
        def _():
            work(BINS)

        departures(step, range(6, 8), lambda c: c.start())
        return carry

    lax.fori_loop(0, steps, work_on, 0)
    keep_half(meta, acc_s, keep_ref, send_ref)
    for j in range(7):
        dvec_ref[j : j + 1, :] = lanes_into_rows(bacc_s[j * d : (j + 1) * d, :])
    dvec_ref[7:8, :] = jnp.zeros((1, d), F32)
    wait_arrivals(jnp.bitwise_and(steps, 1))

    @pl.when(steps >= 2)
    def _():
        departures(steps - 2, range(8), lambda c: c.wait())

    departures(steps - 1, range(8), lambda c: c.wait())


def attention_kernel(
    traj,
    meta_ref,
    nhat1_hbm,
    qkv_hbm,
    prob_hbm,
    gatt_hbm,
    dvec_ref,
    gq_hbm,
    keep_ref,
    send_ref,
    nhat1_s,
    qkv_s,
    prob_s,
    gatt_s,
    gq_s,
    in_sem,
    out_sem,
    bd_s,
    bdq_s,
    dp_s,
    ds_s,
    bacc_s,
    acc_s,
):
    d = nhat1_hbm.shape[1]
    hs = d // HEADS
    scale = hs**-0.5
    meta = Meta(meta_ref, traj)
    steps = lax.shift_right_logical(meta.tiles() + 1, 1)

    def come(i, act):
        slot = jnp.bitwise_and(i, 1)
        for k, (ref, place) in enumerate(
            ((gatt_hbm, gatt_s), (qkv_hbm, qkv_s), (prob_hbm, prob_s), (nhat1_hbm, nhat1_s))
        ):
            act(pltpu.make_async_copy(ref.at[i], place.at[slot], in_sem.at[slot, k]))

    def leave(i, act):
        slot = jnp.bitwise_and(i, 1)
        act(pltpu.make_async_copy(gq_s.at[slot], gq_hbm.at[i], out_sem.at[slot]))

    come(0, lambda c: c.start())
    bd_s[...] = jnp.zeros_like(bd_s)
    bdq_s[...] = jnp.zeros_like(bdq_s)
    bacc_s[...] = jnp.zeros_like(bacc_s)
    acc_s[...] = jnp.zeros_like(acc_s)

    def step(i, carry):
        slot = jnp.bitwise_and(i, 1)
        come(i, lambda c: c.wait())

        @pl.when(i + 1 < steps)
        def _():
            come(i + 1, lambda c: c.start())

        @pl.when(i >= 2)
        def _():
            leave(i - 2, lambda c: c.wait())

        refs = [ref.at[pl.ds(slot, 1)] for ref in (nhat1_s, qkv_s, prob_s, gatt_s, gq_s)]

        @pl.when(2 * i + 1 < meta.tiles())
        def _():
            work(BINS_A, *refs)

        @pl.when(2 * i + 1 == meta.tiles())
        def _():
            work(BINS, *refs)

        leave(i, lambda c: c.start())
        return carry

    def work(count, nhat1_ref, qkv_ref, prob_ref, gatt_ref, gq_ref):
        pairs = [(b, p * 2 * hs, b * (HEADS // 2) + p, p) for b in range(count) for p in range(HEADS // 2)]
        for b, f0, at, _ in pairs:
            lanes = bin_lanes(b)
            bd_s[at, 0:hs, 0:BIN] = gatt_ref[0, f0 : f0 + hs, lanes]
            bd_s[at, hs : 2 * hs, BIN:PAIR] = gatt_ref[0, f0 + hs : f0 + 2 * hs, lanes]
            bdq_s[at, 0:hs, 0:BIN] = qkv_ref[0, f0 : f0 + hs, lanes]
            bdq_s[at, hs : 2 * hs, BIN:PAIR] = qkv_ref[0, f0 + hs : f0 + 2 * hs, lanes]
        for b, f0, at, _ in pairs:
            dp_s[at] = mm(qkv_ref[0, 2 * d + f0 : 2 * d + f0 + 2 * hs, bin_lanes(b)], bd_s[at], TN)
        for b, f0, at, p in pairs:
            pr = prob_ref[0, b, :, pair_lanes(p)].astype(F32)
            t = pr * dp_s[at]
            ds_s[at] = (t - pr * jnp.sum(t, axis=0, keepdims=True)).astype(BF16)

        def put(b, row, part):
            gq_ref[0, row : row + 2 * hs, bin_lanes(b)] = part.astype(BF16)
            bacc_s[row : row + 2 * hs, :] += part

        for b, f0, at, _ in pairs:
            both = mm(qkv_ref[0, d + f0 : d + f0 + 2 * hs, bin_lanes(b)], ds_s[at]) * scale
            put(b, f0, jnp.concatenate([both[0:hs, 0:BIN], both[hs : 2 * hs, BIN:PAIR]], axis=0))
        for b, f0, at, _ in pairs:
            put(b, d + f0, mm(bdq_s[at], ds_s[at], NT))
        for b, f0, at, p in pairs:
            put(b, 2 * d + f0, mm(bd_s[at], prob_ref[0, b, :, pair_lanes(p)], NT))
        lanes = slice(0, count * BIN)
        acc_s[0 : 3 * d, :] += mm(gq_ref[0, :, lanes], nhat1_ref[0, :, lanes], NT)

    lax.fori_loop(0, steps, step, 0)
    for j in range(3):
        acc_s[3 * d + j : 3 * d + j + 1, :] = lanes_into_rows(bacc_s[j * d : (j + 1) * d, :])
    acc_s[3 * d + 3 : 3 * d + 11, :] = dvec_ref[...]
    keep_half(meta, acc_s, keep_ref, send_ref)

    @pl.when(steps >= 2)
    def _():
        leave(steps - 2, lambda c: c.wait())

    leave(steps - 1, lambda c: c.wait())


def token_kernel(share, meta_ref, g1_ref, idx_ref, wqkv_ref, nhat1_ref, rstd1_ref, gq_ref, gmid_ref, *refs):
    tg_ref, idx_in, wqkv_s, nhat1_s, rstd1_s, gq_s, gmid_s, sems, idx_s, col_s, gg_s, rows_s, out_sems = refs[-13:]
    traj, slots = idx_ref.shape
    seq, d = tg_ref.shape[1:]
    meta = Meta(meta_ref, traj)

    def prepare():
        idx_s[...] = jnp.zeros_like(idx_s)
        idx_s[:, 0:slots] = idx_in[...]
        row = jnp.broadcast_to(g1_ref[...].astype(F32).reshape(1, d), (8, d))
        col_s[...] = jnp.broadcast_to(row.T[:, 0:1], (d, BIN))

    def rows_of(tile, slot):
        for b in range(BINS):
            gg_s[:, bin_lanes(b)] = bin_onehot(idx_s, *meta.bin(tile * BINS + b), seq)
        gfs = [mm(wqkv_s[...], gq_s[slot, :, pair_lanes(t)]) for t in range(BINS // 2)]
        grads = []
        for b in range(BINS):
            lanes = bin_lanes(b)
            nhat = nhat1_s[slot, :, lanes].astype(F32)
            a = gfs[b // 2][:, bin_lanes(b % 2)] * col_s[...]
            m1 = jnp.mean(a, axis=0, keepdims=True)
            m2 = jnp.mean(a * nhat, axis=0, keepdims=True)
            rstd = rstd1_s[slot, 0:1, lanes]
            grads.append((gmid_s[slot, :, lanes].astype(F32) + rstd * (a - m1 - nhat * m2)).astype(BF16))
        for b in range(BINS):
            rows_s[slot, b] = mm(gg_s[:, bin_lanes(b)], grads[b], NT).astype(BF16)

    store_tiles(
        share,
        meta,
        [(idx_ref, idx_in), (wqkv_ref, wqkv_s)],
        [(nhat1_ref, nhat1_s), (rstd1_ref, rstd1_s), (gq_ref, gq_s), (gmid_ref, gmid_s)],
        sems,
        prepare,
        rows_of,
        rows_s,
        tg_ref,
        seq,
        out_sems,
    )


def store_tiles(share, meta, once, each, sems, prepare, rows_of, rows_s, to_ref, rows, out_sems):
    first, stop = share.start(meta.tiles()), share.stop(meta.tiles())
    done = stop - first

    def constant(act):
        for k, (ref, place) in enumerate(once):
            act(pltpu.make_async_copy(ref, place, sems.at[2, k]))

    def come(tile, slot, act):
        lanes = pl.ds(pl.multiple_of(jnp.bitwise_and(tile, 1) * TILE, TILE), TILE)
        for k, (ref, place) in enumerate(each):
            act(
                pltpu.make_async_copy(
                    ref.at[lax.shift_right_logical(tile, 1), :, lanes], place.at[slot], sems.at[slot, k]
                )
            )

    def wait_left(i):
        slot = jnp.bitwise_and(i, 1)
        wait_rows(rows_s.at[slot], 2 * BINS * rows, out_sems.at[slot])

    constant(lambda c: c.start())
    come(first, 0, lambda c: c.start())
    constant(lambda c: c.wait())
    prepare()

    def step(i, carry):
        slot = jnp.bitwise_and(i, 1)
        come(first + i, slot, lambda c: c.wait())

        @pl.when(i + 1 < done)
        def _():
            come(first + i + 1, 1 - slot, lambda c: c.start())

        @pl.when(i >= 2)
        def _():
            wait_left(i - 2)

        rows_of(first + i, slot)
        departures(meta, first + i, rows_s, slot, to_ref, rows, out_sems)
        return carry

    lax.fori_loop(0, done, step, 0)

    @pl.when(done >= 2)
    def _():
        wait_left(done - 2)

    wait_left(done - 1)


def output_kernel(share, traj, meta_ref, bdn_ref, wdnt_ref, act_ref, mid_ref, *refs):
    lay_ref, wdnt_s, act_s, mid_s, sems, col_s, y_s, sel_s, rows_s, out_sems = refs[-10:]
    slots, d = lay_ref.shape[1:]
    meta = Meta(meta_ref, traj)

    def prepare():
        row = jnp.broadcast_to(bdn_ref[...].astype(F32).reshape(1, d), (8, d))
        col_s[...] = jnp.broadcast_to(row.T[:, 0:1], (d, BIN))

    def rows_of(tile, slot):
        mlps = [mm(wdnt_s[...], act_s[slot, :, pair_lanes(t)]) for t in range(BINS // 2)]
        for b in range(BINS):
            sel_s[b] = bin_slots(*meta.bin(tile * BINS + b)[2:])
        for t in range(BINS // 2):
            lanes = pair_lanes(t)
            y_s[:, lanes] = (mlps[t] + mid_s[slot, :, lanes].astype(F32) + two(col_s[...])).astype(BF16)
        for b in range(BINS):
            rows_s[slot, b] = mm(sel_s[b], y_s[:, bin_lanes(b)], NT).astype(BF16)

    store_tiles(
        share,
        meta,
        [(wdnt_ref, wdnt_s)],
        [(act_ref, act_s), (mid_ref, mid_s)],
        sems,
        prepare,
        rows_of,
        rows_s,
        lay_ref,
        slots,
        out_sems,
    )


CORE, Y, X, Z = 0, 1, 2, 3


def row_at(const=0, **bits):
    return const, tuple(({"core": CORE, "y": Y, "x": X, "z": Z}[name], coef) for name, coef in bits.items())


def mine(bit, rows, base=0):
    return base, ((bit, rows),)


def other(bit, rows, base=0):
    return base + rows, ((bit, -rows),)


class Step:
    def __init__(self, inputs, out_rows, parts, sends=()):
        self.inputs, self.out_rows, self.parts, self.sends = list(inputs), list(out_rows), list(parts), dict(sends)


def combine_kernel(step, bits_at, meta_ref, *refs):
    ins, outs = refs[: len(step.inputs)], refs[len(step.inputs) :]

    def row(start):
        if isinstance(start, int):
            return start
        const, bits = start
        for bit, coef in bits:
            const = const + meta_ref[bits_at + bit] * coef
        return const

    def rows(start, n):
        return pl.ds(start if isinstance(start, int) else pl.multiple_of(start, 8), n)

    for n, terms, goes in step.parts:
        for out, start, first, count in goes:
            total = None
            for ref, at in terms:
                term = ins[ref][rows(row(at) + row(first), count), :]
                total = term if total is None else total + term
            outs[out][rows(row(start), count), :] = total


def combine(step, meta, bits_at, width):
    vmem = pl.BlockSpec(memory_space=pltpu.VMEM)
    return pl.pallas_call(
        lambda *refs: combine_kernel(step, bits_at, *refs),
        in_specs=[pl.BlockSpec(memory_space=pltpu.SMEM)] + [vmem] * len(step.inputs),
        out_specs=[vmem] * len(step.out_rows),
        out_shape=[jax.ShapeDtypeStruct((n, width), F32) for n in step.out_rows],
        compiler_params=pltpu.CompilerParams(vmem_limit_bytes=2 * MIB),
        name="combine",
    )(meta, *step.inputs)


def bucket_sum(bits, keep, send, half, halve_z):
    h, e, f = half // 4, half // 8, half // 16
    _, (got,) = yield Step([send], [], [], {0: (CORE,)})

    def part(x, y):
        return (0 if x else 2 * h) + (0 if y else h), ((X, 2 * h if x else -2 * h), (Y, h if y else -h))

    (k, _, _, _), got = yield Step(
        [keep, got],
        [h] * 4,
        [
            (h, [(0, part(x, y)), (1, part(x, y))], [(out, row_at(), 0, h)])
            for out, (x, y) in enumerate(((True, True), (False, True), (True, False), (False, False)))
        ],
        {1: (X,), 2: (Y,), 3: (X, Y)},
    )
    four = [k, *got]
    if halve_z:
        (z, _), (got,) = yield Step(
            four,
            [e, e],
            [
                (
                    e,
                    [(n, row_at(c * e)) for n in range(4)],
                    [(0, row_at(c * f), mine(Z, f), f), (1, row_at(c * f), other(Z, f), f)],
                )
                for c in range(2)
            ],
            {1: (Z,)},
        )
        for bit in [*range(Z + 1, bits), Z]:
            (z,), (got,) = yield Step(
                [z, got], [e], [(e, [(0, row_at()), (1, row_at())], [(0, row_at(), 0, e)])], {0: (bit,)}
            )
        (e0, e1), (g0, g1) = yield Step(
            [z, got],
            [e, e],
            [
                (f, [(ref, row_at(c * f))], [(c, side(Z, f), 0, f)])
                for ref, side in enumerate((mine, other))
                for c in range(2)
            ],
            {0: (Y,), 1: (X,)},
        )
    else:
        (z,), (got,) = yield Step(
            four, [h], [(h, [(n, row_at()) for n in range(4)], [(0, row_at(), 0, h)])], {0: (bits - 1,)}
        )
        for bit in range(bits - 2, Z - 1, -1):
            (z,), (got,) = yield Step(
                [z, got], [h], [(h, [(0, row_at()), (1, row_at())], [(0, row_at(), 0, h)])], {0: (bit,)}
            )
        (e0, e1), (g0, g1) = yield Step(
            [z, got],
            [e, e],
            [(h, [(0, row_at()), (1, row_at())], [(0, row_at(), 0, e), (1, row_at(), e, e)])],
            {0: (Y,), 1: (X,)},
        )
    (f0, f1), (g0, g1) = yield Step(
        [e0, e1, g0, g1],
        [h, h],
        [
            (e, [(0, row_at())], [(0, mine(Y, e), 0, e)]),
            (e, [(2, row_at())], [(0, other(Y, e), 0, e)]),
            (e, [(1, row_at())], [(1, mine(X, e), 0, e)]),
            (e, [(3, row_at())], [(1, other(X, e), 0, e)]),
        ],
        {0: (X,), 1: (Y,)},
    )
    (near,), (far,) = yield Step(
        [f0, f1, g0, g1],
        [half],
        [
            (h, [(0, row_at())], [(0, mine(X, 2 * h, y * h), y * e, e) for y in range(2)]),
            (h, [(2, row_at())], [(0, other(X, 2 * h, y * h), y * e, e) for y in range(2)]),
            (h, [(1, row_at())], [(0, mine(Y, h, x * 2 * h + e), x * e, e) for x in range(2)]),
            (h, [(3, row_at())], [(0, other(Y, h, x * 2 * h + e), x * e, e) for x in range(2)]),
        ],
        {0: (CORE,)},
    )
    return near, far


class Sums:
    def __init__(self, ranks, meta, bits_at, width):
        self.ranks, self.meta, self.bits_at, self.width = ranks, meta, bits_at, width
        self.arrays, self.arrived, self.sent = [], [], []
        self.running, self.results = {}, {}

    def view(self, array):
        self.arrays.append(array)
        return (len(self.arrays) - 1, 0)

    def add(self, name, steps):
        self.running[name] = (steps, next(steps))

    def advance(self, after=None):
        if after is not None and self.arrived:
            tied = lax.optimization_barrier((*[self.arrays[k] for k in self.arrived], after))
            for k, array in zip(self.arrived, tied):
                self.arrays[k] = array
        inputs, out_rows, parts, places, sends = [], [], [], {}, {}
        for name, (_, step) in self.running.items():
            outs = []
            for out, rows in enumerate(step.out_rows):
                bit = step.sends.get(out)
                if bit in sends:
                    at = sends[bit]
                    outs.append((at, out_rows[at]))
                    out_rows[at] += rows
                    continue
                if bit is not None:
                    sends[bit] = len(out_rows)
                outs.append((len(out_rows), 0))
                out_rows.append(rows)
            places[name] = outs
            for rows, terms, goes in step.parts:
                moved = []
                for ref, (const, bits) in terms:
                    k, row = step.inputs[ref]
                    if k not in inputs:
                        inputs.append(k)
                    moved.append((inputs.index(k), (const + row, bits)))
                parts.append(
                    (
                        rows,
                        moved,
                        [(outs[out][0], (const + outs[out][1], bits), *rest) for out, (const, bits), *rest in goes],
                    )
                )
        base = len(self.arrays)
        if out_rows:
            merged = Step([self.arrays[k] for k in inputs], out_rows, parts)
            self.arrays += list(combine(merged, self.meta, self.bits_at, self.width))
        to_send = {bit: base + out for bit, out in sends.items()}
        raw = {name: step for name, (_, step) in self.running.items() if not step.parts}
        for step in raw.values():
            for out, bit in step.sends.items():
                to_send[(bit, id(step))] = step.inputs[out][0]
        self.sent = [self.arrays[k] for k in to_send.values()]
        received = {}
        for key, k in to_send.items():
            mask = sum(1 << bit for bit in (key[0] if isinstance(key[0], tuple) else key))
            perm = [(r, r ^ mask) for r in range(self.ranks)]
            received[key] = self.view(lax.ppermute(self.arrays[k], AXES, perm))[0]
        self.arrived = list(received.values())
        for name, (steps, step) in list(self.running.items()):
            if name in raw:
                outs = []
                got = [(received[(bit, id(step))], 0) for bit in step.sends.values()]
            else:
                outs = [(base + out, row) for out, row in places[name]]
                got = [(received[bit], places[name][out][1]) for out, bit in step.sends.items()]
            try:
                self.running[name] = (steps, steps.send((outs, got)))
            except StopIteration as stop:
                self.results[name] = stop.value
                del self.running[name]

    def ordered(self, value):
        return lax.optimization_barrier((value, *self.sent))[0]


def finish_kernel(
    bits_at, rows_at, meta_ref, late0_ref, late1_ref, first0_ref, first1_ref, g1_ref, c1_ref, wqkv_ref, wup_ref,
    dwn_ref, dup_ref, dwo_ref, dqkv_ref, dg1_ref, dc1_ref, dbq_ref, dbv_ref, dbo_ref, dg2_ref, dc2_ref, dbup_ref, dbdn_ref,
    late_s, first_s, first_sem, late_sem, out_sem,
):
    ff, d = dwn_ref.shape
    core = meta_ref[bits_at + CORE]
    late_near, late_far, first_near, first_far = rows_at
    first, late = [], []
    for to_s, copies, sems, sides in (
        (late_s, late, late_sem, ((late0_ref, late_near, core), (late1_ref, late_far, 1 - core))),
        (first_s, first, first_sem, ((first0_ref, first_near, core), (first1_ref, first_far, 1 - core))),
    ):
        half = to_s.shape[0] // 2
        for k, (ref, row, side) in enumerate(sides):
            to = to_s.at[pl.ds(pl.multiple_of(side * half, 8), half)]
            copies.append(pltpu.make_async_copy(ref.at[pl.ds(row, half)], to, sems.at[k]))
    for copy in late + first:
        copy.start()
    for copy in late:
        copy.wait()
    copies = [
        pltpu.make_async_copy(late_s.at[pl.ds(0, ff)], dwn_ref, out_sem.at[0]),
        pltpu.make_async_copy(late_s.at[pl.ds(2 * ff, d)], dwo_ref, out_sem.at[1]),
    ]
    for copy in copies:
        copy.start()
    for j in range(ff // d):
        dup_ref[:, j * d : (j + 1) * d] = late_s[ff + j * d : ff + (j + 1) * d, :].T
    for copy in first:
        copy.wait()

    def late_row(j):
        return first_s[3 * d + 3 + j : 3 * d + 4 + j, :].reshape(d)

    dg2_ref[...] = late_row(0)
    for j in range(ff // d):
        dbup_ref[j * d : (j + 1) * d] = late_row(1 + j)
    dbdn_ref[...] = late_row(5)
    dbo_ref[...] = late_row(6)

    def times(weight_ref, row, n):
        total = jnp.zeros((8, d), F32)
        for j in range(n):
            left = jnp.broadcast_to(first_s[row + j : row + j + 1, :], (8, d))
            for _ in range(3):
                low = left.astype(BF16)
                left = left - low.astype(F32)
                total = total + mm(low, weight_ref[:, j * d : (j + 1) * d], NT)
        return total[0:1, :]

    dc2_ref[...] = times(wup_ref, 3 * d + 4, ff // d).reshape(d)
    dc1_ref[...] = times(wqkv_ref, 3 * d, 3).reshape(d)

    gain = jnp.broadcast_to(g1_ref[...].astype(F32).reshape(1, d), (8, d)).T[:, 0:1]
    bias = jnp.broadcast_to(c1_ref[...].astype(F32).reshape(1, d), (8, d)).T[:, 0:1]
    gain_grad = jnp.zeros((d, d), F32)
    for j in range(3):
        block = slice(j * d, (j + 1) * d)
        total = first_s[3 * d + j : 3 * d + j + 1, :]
        product = first_s[block, :].T
        weight = wqkv_ref[:, block].astype(F32)
        dqkv_ref[:, block] = gain * product + bias * total
        gain_grad += weight * product
    dg1_ref[...] = jnp.sum(gain_grad.T, axis=0, keepdims=True).reshape(d)
    dbq_ref[...] = first_s[3 * d : 3 * d + 1, :].reshape(d)
    dbv_ref[...] = first_s[3 * d + 2 : 3 * d + 3, :].reshape(d)
    for copy in copies:
        copy.wait()


def doubled(shape):
    if len(shape) == 3:
        return (2 * shape[0],) + shape[1:]
    return shape[:-1] + (2 * shape[-1],)


SHARES_C = shares(0, 10, 16)
SHARES_D = shares(0, 5, 8, 16)


def body(
    ranks,
    tokens,
    visible_index,
    visible_count,
    ln1_gain,
    ln1_bias,
    qkv_weight,
    query_bias,
    value_bias,
    out_weight,
    out_bias,
    ln2_gain,
    ln2_bias,
    up_weight,
    up_bias,
    down_weight,
    down_bias,
    out_grad,
):
    traj, slots = visible_index.shape
    seq, d = tokens.shape[1:]
    ff = up_weight.shape[1]
    hs = d // HEADS
    steps_a = -(-traj // BINS_A)
    tiles = 2 * steps_a
    tiles_at = Meta.size(traj) - 16
    bits = ranks.bit_length() - 1
    rank = lax.axis_index(AXES).astype(jnp.int32).reshape(1)
    meta = make_plan(visible_count, rank, slots)
    sums = Sums(ranks, meta, tiles_at + 1, d)

    shapes = dict(
        nhat=((d, TILE), BF16),
        rstd=((8, TILE), F32),
        qkv=((3 * d, TILE), BF16),
        prob=((BINS, BIN, HEADS * BIN), BF16),
        gatt=((d, TILE), BF16),
        gmid=((d, TILE), BF16),
        act=((ff, TILE), BF16),
        mid=((d, TILE), BF16),
    )

    def stored(name):
        shape, kind = shapes[name]
        return jax.ShapeDtypeStruct((steps_a,) + doubled(shape), kind)

    smem, vmem = (pl.BlockSpec(memory_space=m) for m in (pltpu.SMEM, pltpu.VMEM))

    def step_places(*names):
        return [pltpu.VMEM((2,) + doubled(shapes[n][0]), shapes[n][1]) for n in names]

    late_shape = (2 * ff + d, d)
    vectors = [ln1_gain, ln1_bias, query_bias, value_bias, out_bias, ln2_gain, ln2_bias, up_bias]
    weights = [qkv_weight, out_weight, up_weight, down_weight]
    down_weight_t, nhat, rstd, qkv, prob, gatt, gmid, act, mid, late_keep, late_send, late_vectors = pl.pallas_call(
        late_kernel,
        in_specs=[smem, vmem, HBM, HBM] + [vmem] * len(vectors + weights),
        out_specs=[vmem] + [HBM] * len(shapes) + [vmem] * 3,
        scratch_shapes=[
            pltpu.VMEM((2, BINS_A, 2 * seq, d), BF16),
            pltpu.VMEM((2, BINS_A, 2 * BIN, d), BF16),
            pltpu.SemaphoreType.DMA((2, 2)),
            *step_places(*shapes),
            pltpu.SemaphoreType.DMA((2, 8)),
            pltpu.VMEM((traj, BIN), jnp.int32),
            pltpu.VMEM((16, d), F32),
            pltpu.VMEM((12 * d, BIN), F32),
            pltpu.VMEM((3 * d, d), BF16),
            pltpu.VMEM((d, d), BF16),
            pltpu.VMEM((ff, d), BF16),
            pltpu.VMEM((d, TILE_A), F32),
            pltpu.VMEM((d, TILE_A), BF16),
            pltpu.VMEM((BINS_A * HEADS // 2, 2 * hs, PAIR), BF16),
            pltpu.VMEM((BINS_A * HEADS // 2, BIN, PAIR), F32),
            pltpu.VMEM((d, TILE_A), BF16),
            pltpu.VMEM((d, TILE_A), F32),
            pltpu.VMEM((d, TILE_A), BF16),
            pltpu.VMEM((d, TILE_A), BF16),
            pltpu.VMEM((ff, TILE_A), BF16),
            pltpu.VMEM((ff, TILE_A), BF16),
            pltpu.VMEM((ff, TILE_A), BF16),
            pltpu.VMEM((d, TILE_A), F32),
            pltpu.VMEM((d, TILE_A), F32),
            pltpu.VMEM(late_shape, F32),
            pltpu.VMEM((3 * d + ff, BIN), F32),
        ],
        out_shape=[jax.ShapeDtypeStruct((d, ff), BF16)]
        + [stored(n) for n in shapes]
        + [jax.ShapeDtypeStruct(n, F32) for n in ((late_shape[0] // 2, d), (late_shape[0] // 2, d), (8, d))],
        compiler_params=pltpu.CompilerParams(vmem_limit_bytes=58 * MIB),
        name="forward_mlp",
    )(meta, visible_index, tokens, out_grad, *vectors, *weights)
    late = bucket_sum(bits, sums.view(late_keep), sums.view(late_send), late_shape[0] // 2, True)
    sums.add("late", late)
    sums.advance()

    acc_shape = (-(-(3 * d + 11) // 128) * 128, d)
    send_shape = (acc_shape[0] // 2, d)
    grad_qkv, first_keep, first_send = pl.pallas_call(
        lambda *refs: attention_kernel(traj, *refs),
        in_specs=[smem] + [HBM] * 4 + [vmem],
        out_specs=[HBM, vmem, vmem],
        scratch_shapes=step_places("nhat", "qkv", "prob", "gatt")
        + [pltpu.VMEM((2, 3 * d, TILE_A), BF16), pltpu.SemaphoreType.DMA((2, 4)), pltpu.SemaphoreType.DMA((2,))]
        + [pltpu.VMEM((BINS_A * HEADS // 2, 2 * hs, PAIR), BF16)] * 2
        + [
            pltpu.VMEM((BINS_A * HEADS // 2, BIN, PAIR), F32),
            pltpu.VMEM((BINS_A * HEADS // 2, BIN, PAIR), BF16),
            pltpu.VMEM((3 * d, BIN), F32),
            pltpu.VMEM(acc_shape, F32),
        ],
        out_shape=[jax.ShapeDtypeStruct((steps_a, 3 * d, TILE_A), BF16)] + [jax.ShapeDtypeStruct(send_shape, F32)] * 2,
        compiler_params=pltpu.CompilerParams(vmem_limit_bytes=56 * MIB),
        cost_estimate=pl.CostEstimate(flops=5 * 10**9, bytes_accessed=16 * 10**6, transcendentals=0),
        name="attention_backward",
    )(sums.ordered(meta), nhat, qkv, prob, gatt, late_vectors)
    first = bucket_sum(bits, sums.view(first_keep), sums.view(first_send), send_shape[0], False)
    sums.add("first", first)
    sums.advance(first_keep)

    def tile_places(*names):
        shapes_of = dict(shapes, gq=((3 * d, TILE), BF16))
        return [pltpu.VMEM((2,) + shapes_of[n][0], shapes_of[n][1]) for n in names]

    def stores(kernel, name, vector, inputs, rows, scratch, earlier):
        given = [] if earlier is None else [earlier]
        return pl.pallas_call(
            kernel,
            in_specs=[smem, vmem] + [HBM] * (len(inputs) + len(given)),
            out_specs=HBM,
            scratch_shapes=scratch
            + [pltpu.VMEM((2, BINS, 2 * BIN, d), BF16), pltpu.SemaphoreType.DMA((2,))],
            out_shape=jax.ShapeDtypeStruct((traj, rows, d), BF16),
            input_output_aliases={2 + len(inputs): 0} if given else {},
            compiler_params=pltpu.CompilerParams(vmem_limit_bytes=56 * MIB),
            cost_estimate=pl.CostEstimate(flops=2 * 10**9, bytes_accessed=8 * 10**6, transcendentals=0),
            name=name,
        )(sums.ordered(meta), vector, *inputs, *given)

    tokens_grad = None
    for share in SHARES_C:
        tokens_grad = stores(
            lambda *refs, share=share: token_kernel(share, *refs),
            "tokens_backward",
            ln1_gain,
            [visible_index, qkv_weight, nhat, rstd, grad_qkv, gmid],
            seq,
            [pltpu.VMEM((traj, slots), jnp.int32), pltpu.VMEM((d, 3 * d), BF16)]
            + tile_places("nhat", "rstd", "gq", "gmid")
            + [pltpu.SemaphoreType.DMA((3, 4))]
            + [pltpu.VMEM((traj, BIN), jnp.int32), pltpu.VMEM((d, BIN), F32), pltpu.VMEM((d, TILE), BF16)],
            tokens_grad,
        )
        sums.advance(tokens_grad)
        if share is SHARES_C[0]:
            sums.advance()
    layer_out = None
    for share in SHARES_D:
        layer_out = stores(
            lambda *refs, share=share: output_kernel(share, traj, *refs),
            "layer_output",
            down_bias,
            [down_weight_t, act, mid],
            slots,
            [pltpu.VMEM((d, ff), BF16)]
            + tile_places("act", "mid")
            + [pltpu.SemaphoreType.DMA((3, 4))]
            + [pltpu.VMEM((d, BIN), F32), pltpu.VMEM((d, TILE), BF16), pltpu.VMEM((BINS, 2 * BIN, BIN), BF16)],
            layer_out,
        )
        sums.advance(layer_out)
    while sums.running:
        sums.advance()
    views = sums.results["late"] + sums.results["first"]
    near_far = [sums.arrays[k] for k, _ in views]
    rows_at = tuple(row for _, row in views)

    vmem = pl.BlockSpec(memory_space=pltpu.VMEM)
    vector = jax.ShapeDtypeStruct((d,), F32)
    dwn, dup, dwo, dqkv, dg1, dc1, dbq, dbv, dbo, dg2, dc2, dbup, dbdn = pl.pallas_call(
        lambda *refs: finish_kernel(tiles_at + 1, rows_at, *refs),
        in_specs=[pl.BlockSpec(memory_space=pltpu.SMEM)] + [HBM] * 4 + [vmem] * 4,
        out_specs=[HBM, vmem, HBM] + [vmem] * 10,
        out_shape=[
            jax.ShapeDtypeStruct((ff, d), F32),
            jax.ShapeDtypeStruct((d, ff), F32),
            jax.ShapeDtypeStruct((d, d), F32),
            jax.ShapeDtypeStruct((d, 3 * d), F32),
        ]
        + [vector] * 7
        + [jax.ShapeDtypeStruct((ff,), F32), vector],
        scratch_shapes=[
            pltpu.VMEM(late_shape, F32),
            pltpu.VMEM(acc_shape, F32),
            pltpu.SemaphoreType.DMA((2,)),
            pltpu.SemaphoreType.DMA((2,)),
            pltpu.SemaphoreType.DMA((2,)),
        ],
        compiler_params=pltpu.CompilerParams(vmem_limit_bytes=24 * MIB),
        name="finish",
    )(meta, *near_far, ln1_gain, ln1_bias, qkv_weight, up_weight)
    return layer_out, tokens_grad, dg1, dc1, dqkv, dbq, dbv, dwo, dbo, dg2, dc2, dup, dbup, dwn, dbdn


def solution(mesh):
    devices = mesh.devices
    ranks = devices.size
    mesh = Mesh(devices.reshape(devices.shape[0], devices.shape[1] // 2, 2), AXES)
    rows = P(AXES)
    placed = (rows, rows, rows) + (P(),) * 13 + (rows,)
    return jax.shard_map(
        lambda *args: body(ranks, *args),
        mesh=mesh,
        in_specs=placed,
        out_specs=(rows, rows) + (P(),) * 13,
        check_vma=False,
    )
```

```python
import jax
import jax.numpy as jnp
from jax import lax
from jax.experimental import pallas as pl
from jax.experimental.pallas import tpu as pltpu
from jax.sharding import Mesh, PartitionSpec as P

AXES = ("wide", "square", "core")
HEADS = 4
EPS = 1e-05
BIN = 128
PAIR = 2 * BIN
BINS = 4
TILE = BINS * BIN
BINS_A = 8
TILE_A = BINS_A * BIN
F32 = jnp.float32
BF16 = jnp.bfloat16
GELU_A = 0.7978845608028654
GELU_B = 0.044715 * GELU_A

NN = (((1,), (0,)), ((), ()))
NT = (((1,), (1,)), ((), ()))
TN = (((0,), (0,)), ((), ()))

MIB = 1024 * 1024
HBM = pl.BlockSpec(memory_space=pl.ANY)


def mm(left, right, dims=NN):
    return lax.dot_general(left, right, dims, preferred_element_type=F32)


class Meta:
    def __init__(self, ref, traj):
        self.ref = ref
        self.width = traj + 8

    @staticmethod
    def size(traj):
        return 4 * (traj + 8) + 16

    def bin(self, b):
        return tuple(self.ref[j * self.width + b] for j in range(4))

    def put(self, b, *values):
        for j, value in enumerate(values):
            self.ref[j * self.width + b] = value

    @property
    def tiles_at(self):
        return 4 * self.width

    def tiles(self):
        return self.ref[self.tiles_at]

    def bins(self):
        return self.ref[self.tiles_at + 15]

    def bit(self, b):
        return self.ref[self.tiles_at + 1 + b]


def plan_kernel(count_ref, rank_ref, meta_ref, first_ref, order_ref):
    traj = count_ref.shape[0]
    top = first_ref.shape[0]
    meta = Meta(meta_ref, traj)

    def clear(v, carry):
        first_ref[v] = 0
        return carry

    lax.fori_loop(0, top, clear, 0, unroll=16)

    def tally(t, carry):
        c = count_ref[t]
        first_ref[c] = first_ref[c] + 1
        return carry

    lax.fori_loop(0, traj, tally, 0, unroll=8)

    def starts(i, run):
        v = top - 1 - i
        n = first_ref[v]
        first_ref[v] = run
        return run + n

    lax.fori_loop(0, top, starts, 0, unroll=16)

    def place(t, carry):
        c = count_ref[t]
        at = first_ref[c]
        order_ref[at] = t
        first_ref[c] = at + 1
        return carry

    lax.fori_loop(0, traj, place, 0, unroll=8)

    def pair(carry):
        hi, lo, n = carry
        t_hi = order_ref[hi]
        t_lo = order_ref[lo]
        c_hi = count_ref[t_hi]
        c_lo = count_ref[t_lo]
        fits = jnp.logical_and(hi < lo, c_hi + c_lo <= BIN)
        meta.put(n, t_hi, jnp.where(fits, t_lo, t_hi), c_hi, jnp.where(fits, c_lo, 0))
        return hi + 1, jnp.where(fits, lo - 1, lo), n + 1

    _, _, n = lax.while_loop(lambda c: c[0] <= c[1], pair, (jnp.int32(0), jnp.int32(traj - 1), jnp.int32(0)))
    last = meta_ref[n - 1]
    for j in range(BINS_A - 1):
        meta.put(n + j, last, last, 0, 0)
    meta_ref[meta.tiles_at] = lax.shift_right_logical(n + BINS - 1, BINS.bit_length() - 1)
    meta_ref[meta.tiles_at + 15] = n
    for b in range(14):
        meta_ref[meta.tiles_at + 1 + b] = jnp.bitwise_and(lax.shift_right_logical(rank_ref[0], b), 1)


def make_plan(counts, rank, slots):
    traj = counts.shape[0]
    smem = pl.BlockSpec(memory_space=pltpu.SMEM)
    return pl.pallas_call(
        plan_kernel,
        in_specs=[smem, smem],
        out_specs=smem,
        out_shape=jax.ShapeDtypeStruct((Meta.size(traj),), jnp.int32),
        scratch_shapes=[pltpu.SMEM((-(-(slots + 1) // 16) * 16,), jnp.int32), pltpu.SMEM((traj,), jnp.int32)],
        name="plan",
    )(counts, rank)


def bin_onehot(idx_ref, ta, tb, ca, cb, seq):
    lane = lax.broadcasted_iota(jnp.int32, (8, BIN), 1)
    ia = jnp.broadcast_to(idx_ref[pl.ds(ta, 1), :], (8, BIN))
    ib = jnp.broadcast_to(idx_ref[pl.ds(tb, 1), :], (8, BIN))
    ib = pltpu.roll(ib, ca, 1)
    code = jnp.where(lane < ca, ia, jnp.where(lane < ca + cb, ib + seq, -1))[0:1, :]
    pos = lax.broadcasted_iota(jnp.int32, (2 * seq, BIN), 0)
    return jnp.where(pos == code, 1.0, 0.0).astype(BF16)


def bin_slots(ca, cb):
    row = lax.broadcasted_iota(jnp.int32, (BIN, BIN), 0)
    lane = lax.broadcasted_iota(jnp.int32, (BIN, BIN), 1)
    first = jnp.logical_and(lane == row, row < ca)
    second = jnp.logical_and(lane == row + ca, row < cb)
    return jnp.concatenate([jnp.where(x, 1.0, 0.0).astype(BF16) for x in (first, second)], axis=0)


def bin_mask(ca, cb):
    row = lax.broadcasted_iota(jnp.int32, (BIN, BIN), 0)
    lane = lax.broadcasted_iota(jnp.int32, (BIN, BIN), 1)
    key = jnp.where(row < ca, 0, jnp.where(row < ca + cb, 1, 2))
    query = jnp.where(lane < ca, 0, jnp.where(lane < ca + cb, 1, 3))
    return jnp.where(key == query, 0.0, -1e30)


def center(x):
    mean = jnp.mean(x, axis=0, keepdims=True)
    xc = x - mean
    var = jnp.mean(xc * xc, axis=0, keepdims=True)
    rstd = lax.rsqrt(var + EPS)
    return xc * rstd, rstd


def lanes_into_rows(acc):
    return jnp.sum(acc.T, axis=0, keepdims=True)


def two(x):
    return jnp.concatenate([x, x], axis=1)


def bin_lanes(b):
    return slice(b * BIN, (b + 1) * BIN)


def pair_lanes(t):
    return slice(t * PAIR, (t + 1) * PAIR)


def wait_rows(place, rows, sem):
    _, m, _ = place.shape
    parts = [place.at[pl.ds(0, rows // m)]] if rows >= m else []
    if rows % m:
        parts.append(place.at[pl.ds(0, 1), pl.ds(0, rows % m)])
    for part in parts:
        pltpu.make_async_copy(part, part, sem).wait()


def departures(meta, tile, rows_s, slot, to_ref, rows, sems):
    half = rows_s.shape[2] // 2
    last = jnp.bitwise_and(meta.bins() - 1, BINS - 1)
    for b in range(BINS):
        ta, tb, ca, cb = meta.bin(tile * BINS + b)
        source = jnp.where(ca > 0, b, last)
        for part, (t, row) in enumerate(((ta, 0), (tb, jnp.where(cb > 0, half, 0)))):
            rows_of_t = pl.ds(pl.multiple_of(row, half) if part else 0, rows)
            pltpu.make_async_copy(rows_s.at[slot, source, rows_of_t], to_ref.at[t], sems.at[slot]).start()


class Share:
    def __init__(self, first, last):
        self.first, self.last = first, last

    def start(self, tiles):
        return lax.shift_right_logical(tiles * self.first, 4)

    def stop(self, tiles):
        return lax.shift_right_logical(tiles * self.last, 4)


def shares(*cuts):
    return [Share(a, b) for a, b in zip(cuts[:-1], cuts[1:])]


def keep_half(meta, acc_s, keep_ref, send_ref):
    half = keep_ref.shape[0]
    core = meta.bit(CORE)
    keep_ref[...] = acc_s[pl.ds(pl.multiple_of(core * half, 8), half), :]
    send_ref[...] = acc_s[pl.ds(pl.multiple_of((1 - core) * half, 8), half), :]


def late_kernel(
    meta_ref,
    idx_ref,
    tok_ref,
    og_ref,
    g1_ref,
    c1_ref,
    bq_ref,
    bv_ref,
    bo_ref,
    g2_ref,
    c2_ref,
    bup_ref,
    wqkv_ref,
    wo_ref,
    wup_ref,
    wdn_ref,
    wdnt_s,
    nhat1_hbm,
    rstd1_hbm,
    qkv_hbm,
    prob_hbm,
    gatt_hbm,
    gmid_hbm,
    act_hbm,
    mid_hbm,
    keep_ref,
    send_ref,
    dvec_ref,
    tok_s,
    og_s,
    in_sem,
    nhat1_b,
    rstd1_b,
    qkv_b,
    prob_b,
    gatt_b,
    gmid_b,
    act_b,
    mid_b,
    out_sem,
    idx_s,
    vec_s,
    col_s,
    wqkvt_s,
    wot_s,
    wupt_s,
    gath_s,
    first_s,
    bd_s,
    score_s,
    att_s,
    nhat_s,
    sec_s,
    gm_s,
    u_s,
    ga_s,
    gp_s,
    mid_s,
    gs_s,
    acc_s,
    bacc_s,
):
    traj, seq, d = tok_ref.shape
    slots = og_ref.shape[1]
    ff = wup_ref.shape[1]
    hs = d // HEADS
    scale = hs**-0.5
    meta = Meta(meta_ref, traj)
    steps = lax.shift_right_logical(meta.tiles() + 1, 1)

    def arrivals(i, slot):
        for b in range(BINS_A):
            for part, t in enumerate(meta.bin(i * BINS_A + b)[0:2]):
                to_tok = tok_s.at[slot, b, pl.ds(part * seq, seq)]
                to_og = og_s.at[slot, b, pl.ds(part * BIN, slots)]
                pltpu.make_async_copy(tok_ref.at[t], to_tok, in_sem.at[slot, 0]).start()
                pltpu.make_async_copy(og_ref.at[t], to_og, in_sem.at[slot, 1]).start()

    def wait_arrivals(slot):
        wait_rows(tok_s.at[slot], 2 * BINS_A * seq, in_sem.at[slot, 0])
        wait_rows(og_s.at[slot], 2 * BINS_A * slots, in_sem.at[slot, 1])

    saved = (
        (nhat1_b, nhat1_hbm), (rstd1_b, rstd1_hbm), (qkv_b, qkv_hbm), (prob_b, prob_hbm),
        (act_b, act_hbm), (mid_b, mid_hbm), (gatt_b, gatt_hbm), (gmid_b, gmid_hbm),
    )

    def departures(i, which, act):
        slot = jnp.bitwise_and(i, 1)
        for k in which:
            place, ref = saved[k]
            act(pltpu.make_async_copy(place.at[slot], ref.at[i], out_sem.at[slot, k]))

    for part in range(2):
        og_s[:, :, part * BIN + slots : (part + 1) * BIN, :] = jnp.zeros((2, BINS_A, BIN - slots, d), BF16)
    arrivals(0, 0)
    idx_s[...] = jnp.zeros_like(idx_s)
    idx_s[:, 0:slots] = idx_ref[...]
    vec_s[...] = jnp.zeros_like(vec_s)
    rows = [(0, g1_ref), (1, c1_ref), (2, bq_ref), (4, bv_ref), (5, bo_ref), (6, g2_ref), (7, c2_ref)]
    for j, ref in rows:
        vec_s[j : j + 1, :] = ref[...].astype(F32).reshape(1, d)
    for j in range(ff // d):
        vec_s[8 + j : 9 + j, :] = bup_ref[j * d : (j + 1) * d].astype(F32).reshape(1, d)
    vec_s[2:3, :] = vec_s[2:3, :] * scale
    cols = vec_s[...].T
    for j in range(12):
        col_s[j * d : (j + 1) * d, :] = jnp.broadcast_to(cols[:, j : j + 1], (d, BIN))
    wqkvt_s[...] = wqkv_ref[...].T
    wqkvt_s[0:d, :] = (wqkvt_s[0:d, :].astype(F32) * scale).astype(BF16)
    wot_s[...] = wo_ref[...].T
    wupt_s[...] = wup_ref[...].T
    wdnt_s[...] = wdn_ref[...].T
    bd_s[...] = jnp.zeros_like(bd_s)
    bacc_s[...] = jnp.zeros_like(bacc_s)
    acc_s[...] = jnp.zeros_like(acc_s)

    def col(j, n=1):
        return col_s[j * d : (j + n) * d, :]

    def work_on(step, carry):
        slot = jnp.bitwise_and(step, 1)
        wait_arrivals(slot)

        @pl.when(step >= 2)
        def _():
            departures(step - 2, range(8), lambda c: c.wait())

        nhat1_ref, rstd1_ref, qkv_ref, prob_ref, act_ref, mid_ref, gatt_ref, gmid_ref = (
            place.at[pl.ds(slot, 1)] for place, _ in saved
        )
        metas = [meta.bin(step * BINS_A + b) for b in range(BINS_A)]
        rstds = {}

        def gather(b):
            lanes = bin_lanes(b)
            gath_s[:, lanes] = mm(tok_s[slot, b], bin_onehot(idx_s, *metas[b], seq), TN)

        def first_norm(b):
            lanes = bin_lanes(b)
            nhat, rstd = center(gath_s[:, lanes])
            nhat1_ref[0, :, lanes] = nhat.astype(BF16)
            rstd1_ref[0, :, lanes] = jnp.broadcast_to(rstd, (8, BIN))
            first_s[:, lanes] = (nhat * col(0) + col(1)).astype(BF16)

        def cotangent(b):
            gm_s[:, bin_lanes(b)] = mm(og_s[slot, b], bin_slots(*metas[b][2:]), TN).astype(BF16)

        def project(t):
            lanes = pair_lanes(t)
            qkv_ref[0, :, lanes] = (mm(wqkvt_s[...], first_s[:, lanes]) + two(col(2, 3))).astype(BF16)

        def scores(b, p):
            lanes = bin_lanes(b)
            f0 = p * 2 * hs
            at = b * (HEADS // 2) + p
            bd_s[at, 0:hs, 0:BIN] = qkv_ref[0, f0 : f0 + hs, lanes]
            bd_s[at, hs : 2 * hs, BIN:PAIR] = qkv_ref[0, f0 + hs : f0 + 2 * hs, lanes]
            score_s[at] = mm(qkv_ref[0, d + f0 : d + f0 + 2 * hs, lanes], bd_s[at], TN)

        def softmax(b):
            mask = two(bin_mask(*metas[b][2:]))
            for p in range(HEADS // 2):
                s = score_s[b * (HEADS // 2) + p] + mask
                e = jnp.exp(s - jnp.max(s, axis=0, keepdims=True))
                prob_ref[0, b, :, pair_lanes(p)] = (e * (1.0 / jnp.sum(e, axis=0, keepdims=True))).astype(BF16)

        def attend(b, p):
            lanes = bin_lanes(b)
            f0 = p * 2 * hs
            both = mm(qkv_ref[0, 2 * d + f0 : 2 * d + f0 + 2 * hs, lanes], prob_ref[0, b, :, pair_lanes(p)])
            for h in range(2):
                att_s[f0 + h * hs : f0 + (h + 1) * hs, lanes] = both[h * hs : (h + 1) * hs, bin_lanes(h)].astype(BF16)

        def residual(t):
            lanes = pair_lanes(t)
            mid_s[:, lanes] = mm(wot_s[...], att_s[:, lanes])

        def second_norm(b):
            lanes = bin_lanes(b)
            mid = mid_s[:, lanes] + gath_s[:, lanes] + col(5)
            mid_ref[0, :, lanes] = mid.astype(BF16)
            nhat, rstds[b] = center(mid)
            nhat_s[:, lanes] = nhat
            sec_s[:, lanes] = (nhat * col(6) + col(7)).astype(BF16)

        def up(t):
            lanes = pair_lanes(t)
            u_s[:, lanes] = (mm(wupt_s[...], sec_s[:, lanes]) + two(col_s[8 * d : 8 * d + ff, :])).astype(BF16)
            ga_s[:, lanes] = mm(wdn_ref[...], gm_s[:, lanes]).astype(BF16)

        def gelu(t, rows):
            lanes = pair_lanes(t)
            u = u_s[rows, lanes]
            u2 = u * u
            sg = 0.5 * jnp.tanh(u * (u2 * GELU_B + GELU_A)) + 0.5
            act = u * sg
            gp = (act * (1.0 - sg) * (u2 * (6.0 * GELU_B) + 2.0 * GELU_A) + sg) * ga_s[rows, lanes]
            act_ref[0, rows, lanes] = act
            gp_s[rows, lanes] = gp
            bacc_s[d + rows.start : d + rows.stop, :] += (gp[:, 0:BIN] + gp[:, BIN:PAIR]).astype(F32)

        def grad_second(t):
            lanes = pair_lanes(t)
            gs_s[:, lanes] = mm(wup_ref[...], gp_s[:, lanes])

        def second_norm_back(b):
            lanes = bin_lanes(b)
            gs = gs_s[:, lanes]
            nhat = nhat_s[:, lanes]
            bacc_s[0:d, :] += gs * nhat
            a = gs * col(6)
            m1 = jnp.mean(a, axis=0, keepdims=True)
            m2 = jnp.mean(a * nhat, axis=0, keepdims=True)
            gm = gm_s[:, lanes].astype(F32)
            gmid = gm + rstds[b] * (a - m1 - nhat * m2)
            gmid_ref[0, :, lanes] = gmid.astype(BF16)
            bacc_s[d + ff : 2 * d + ff, :] += gm
            bacc_s[2 * d + ff : 3 * d + ff, :] += gmid

        def grad_attended(t):
            lanes = pair_lanes(t)
            gatt_ref[0, :, lanes] = mm(wo_ref[...], gmid_ref[0, :, lanes]).astype(BF16)

        def work(count):
            bins, tiles, chunk, lanes = range(count), range(count // 2), 64, slice(0, count * BIN)
            pairs = [[(b, p) for b in (2 * t, 2 * t + 1) for p in range(HEADS // 2)] for t in tiles]
            stages = dict(
                cotangent=lambda t: [cotangent(b) for b in (2 * t, 2 * t + 1)],
                first_norm=lambda t: [first_norm(b) for b in (2 * t, 2 * t + 1)],
                project=project,
                scores=lambda t: [scores(b, p) for b, p in pairs[t]],
                softmax=lambda t: [softmax(b) for b in (2 * t, 2 * t + 1)],
                attend=lambda t: [attend(b, p) for b, p in pairs[t]],
                residual=residual,
                second_norm=lambda t: [second_norm(b) for b in (2 * t, 2 * t + 1)],
                up=up,
                gelu=lambda t: [gelu(t, slice(j, j + chunk)) for j in range(0, ff, chunk)],
                grad_second=grad_second,
            )
            arrivals(jnp.minimum(step + 1, steps - 1), 1 - slot)
            for b in bins:
                gather(b)
            for when in range(len(tiles) + len(stages) - 1):
                for n, stage in enumerate(stages.values()):
                    if 0 <= when - n < len(tiles):
                        stage(when - n)
            departures(step, range(6), lambda c: c.start())
            acc_s[0:ff, :] += mm(act_ref[0, :, lanes], gm_s[:, lanes], NT)
            for b in bins[: count // 2]:
                second_norm_back(b)
            acc_s[ff : 2 * ff, :] += mm(gp_s[:, lanes], sec_s[:, lanes], NT)
            for b in bins[count // 2 :]:
                second_norm_back(b)
            acc_s[2 * ff : 2 * ff + d, :] += mm(att_s[:, lanes], gmid_ref[0, :, lanes], NT)
            for t in tiles:
                grad_attended(t)

        full = 2 * step + 1 < meta.tiles()

        @pl.when(full)
        def _():
            work(BINS_A)

        @pl.when(jnp.logical_not(full))
        def _():
            work(BINS)

        departures(step, range(6, 8), lambda c: c.start())
        return carry

    lax.fori_loop(0, steps, work_on, 0)
    keep_half(meta, acc_s, keep_ref, send_ref)
    for j in range(7):
        dvec_ref[j : j + 1, :] = lanes_into_rows(bacc_s[j * d : (j + 1) * d, :])
    dvec_ref[7:8, :] = jnp.zeros((1, d), F32)
    wait_arrivals(jnp.bitwise_and(steps, 1))

    @pl.when(steps >= 2)
    def _():
        departures(steps - 2, range(8), lambda c: c.wait())

    departures(steps - 1, range(8), lambda c: c.wait())


def attention_kernel(
    traj,
    meta_ref,
    nhat1_hbm,
    qkv_hbm,
    prob_hbm,
    gatt_hbm,
    dvec_ref,
    gq_hbm,
    keep_ref,
    send_ref,
    nhat1_s,
    qkv_s,
    prob_s,
    gatt_s,
    gq_s,
    in_sem,
    out_sem,
    bd_s,
    bdq_s,
    dp_s,
    ds_s,
    bacc_s,
    acc_s,
):
    d = nhat1_hbm.shape[1]
    hs = d // HEADS
    scale = hs**-0.5
    meta = Meta(meta_ref, traj)
    steps = lax.shift_right_logical(meta.tiles() + 1, 1)

    def come(i, act):
        slot = jnp.bitwise_and(i, 1)
        for k, (ref, place) in enumerate(
            ((gatt_hbm, gatt_s), (qkv_hbm, qkv_s), (prob_hbm, prob_s), (nhat1_hbm, nhat1_s))
        ):
            act(pltpu.make_async_copy(ref.at[i], place.at[slot], in_sem.at[slot, k]))

    def leave(i, act):
        slot = jnp.bitwise_and(i, 1)
        act(pltpu.make_async_copy(gq_s.at[slot], gq_hbm.at[i], out_sem.at[slot]))

    come(0, lambda c: c.start())
    bd_s[...] = jnp.zeros_like(bd_s)
    bdq_s[...] = jnp.zeros_like(bdq_s)
    bacc_s[...] = jnp.zeros_like(bacc_s)
    acc_s[...] = jnp.zeros_like(acc_s)

    def step(i, carry):
        slot = jnp.bitwise_and(i, 1)
        come(i, lambda c: c.wait())

        @pl.when(i + 1 < steps)
        def _():
            come(i + 1, lambda c: c.start())

        @pl.when(i >= 2)
        def _():
            leave(i - 2, lambda c: c.wait())

        refs = [ref.at[pl.ds(slot, 1)] for ref in (nhat1_s, qkv_s, prob_s, gatt_s, gq_s)]

        @pl.when(2 * i + 1 < meta.tiles())
        def _():
            work(BINS_A, *refs)

        @pl.when(2 * i + 1 == meta.tiles())
        def _():
            work(BINS, *refs)

        leave(i, lambda c: c.start())
        return carry

    def work(count, nhat1_ref, qkv_ref, prob_ref, gatt_ref, gq_ref):
        pairs = [(b, p * 2 * hs, b * (HEADS // 2) + p, p) for b in range(count) for p in range(HEADS // 2)]
        for b, f0, at, _ in pairs:
            lanes = bin_lanes(b)
            bd_s[at, 0:hs, 0:BIN] = gatt_ref[0, f0 : f0 + hs, lanes]
            bd_s[at, hs : 2 * hs, BIN:PAIR] = gatt_ref[0, f0 + hs : f0 + 2 * hs, lanes]
            bdq_s[at, 0:hs, 0:BIN] = qkv_ref[0, f0 : f0 + hs, lanes]
            bdq_s[at, hs : 2 * hs, BIN:PAIR] = qkv_ref[0, f0 + hs : f0 + 2 * hs, lanes]
        for b, f0, at, _ in pairs:
            dp_s[at] = mm(qkv_ref[0, 2 * d + f0 : 2 * d + f0 + 2 * hs, bin_lanes(b)], bd_s[at], TN)
        for b, f0, at, p in pairs:
            pr = prob_ref[0, b, :, pair_lanes(p)].astype(F32)
            t = pr * dp_s[at]
            ds_s[at] = (t - pr * jnp.sum(t, axis=0, keepdims=True)).astype(BF16)

        def put(b, row, part):
            gq_ref[0, row : row + 2 * hs, bin_lanes(b)] = part.astype(BF16)
            bacc_s[row : row + 2 * hs, :] += part

        for b, f0, at, _ in pairs:
            both = mm(qkv_ref[0, d + f0 : d + f0 + 2 * hs, bin_lanes(b)], ds_s[at]) * scale
            put(b, f0, jnp.concatenate([both[0:hs, 0:BIN], both[hs : 2 * hs, BIN:PAIR]], axis=0))
        for b, f0, at, _ in pairs:
            put(b, d + f0, mm(bdq_s[at], ds_s[at], NT))
        for b, f0, at, p in pairs:
            put(b, 2 * d + f0, mm(bd_s[at], prob_ref[0, b, :, pair_lanes(p)], NT))
        lanes = slice(0, count * BIN)
        acc_s[0 : 3 * d, :] += mm(gq_ref[0, :, lanes], nhat1_ref[0, :, lanes], NT)

    lax.fori_loop(0, steps, step, 0)
    for j in range(3):
        acc_s[3 * d + j : 3 * d + j + 1, :] = lanes_into_rows(bacc_s[j * d : (j + 1) * d, :])
    acc_s[3 * d + 3 : 3 * d + 11, :] = dvec_ref[...]
    keep_half(meta, acc_s, keep_ref, send_ref)

    @pl.when(steps >= 2)
    def _():
        leave(steps - 2, lambda c: c.wait())

    leave(steps - 1, lambda c: c.wait())


def token_kernel(share, meta_ref, g1_ref, idx_ref, wqkv_ref, nhat1_ref, rstd1_ref, gq_ref, gmid_ref, *refs):
    tg_ref, idx_in, wqkv_s, nhat1_s, rstd1_s, gq_s, gmid_s, sems, idx_s, col_s, gg_s, rows_s, out_sems = refs[-13:]
    traj, slots = idx_ref.shape
    seq, d = tg_ref.shape[1:]
    meta = Meta(meta_ref, traj)

    def prepare():
        idx_s[...] = jnp.zeros_like(idx_s)
        idx_s[:, 0:slots] = idx_in[...]
        row = jnp.broadcast_to(g1_ref[...].astype(F32).reshape(1, d), (8, d))
        col_s[...] = jnp.broadcast_to(row.T[:, 0:1], (d, BIN))

    def rows_of(tile, slot):
        for b in range(BINS):
            gg_s[:, bin_lanes(b)] = bin_onehot(idx_s, *meta.bin(tile * BINS + b), seq)
        gfs = [mm(wqkv_s[...], gq_s[slot, :, pair_lanes(t)]) for t in range(BINS // 2)]
        grads = []
        for b in range(BINS):
            lanes = bin_lanes(b)
            nhat = nhat1_s[slot, :, lanes].astype(F32)
            a = gfs[b // 2][:, bin_lanes(b % 2)] * col_s[...]
            m1 = jnp.mean(a, axis=0, keepdims=True)
            m2 = jnp.mean(a * nhat, axis=0, keepdims=True)
            rstd = rstd1_s[slot, 0:1, lanes]
            grads.append((gmid_s[slot, :, lanes].astype(F32) + rstd * (a - m1 - nhat * m2)).astype(BF16))
        for b in range(BINS):
            rows_s[slot, b] = mm(gg_s[:, bin_lanes(b)], grads[b], NT).astype(BF16)

    store_tiles(
        share,
        meta,
        [(idx_ref, idx_in), (wqkv_ref, wqkv_s)],
        [(nhat1_ref, nhat1_s), (rstd1_ref, rstd1_s), (gq_ref, gq_s), (gmid_ref, gmid_s)],
        sems,
        prepare,
        rows_of,
        rows_s,
        tg_ref,
        seq,
        out_sems,
    )


def store_tiles(share, meta, once, each, sems, prepare, rows_of, rows_s, to_ref, rows, out_sems):
    first, stop = share.start(meta.tiles()), share.stop(meta.tiles())
    done = stop - first

    def constant(act):
        for k, (ref, place) in enumerate(once):
            act(pltpu.make_async_copy(ref, place, sems.at[2, k]))

    def come(tile, slot, act):
        lanes = pl.ds(pl.multiple_of(jnp.bitwise_and(tile, 1) * TILE, TILE), TILE)
        for k, (ref, place) in enumerate(each):
            act(
                pltpu.make_async_copy(
                    ref.at[lax.shift_right_logical(tile, 1), :, lanes], place.at[slot], sems.at[slot, k]
                )
            )

    def wait_left(i):
        slot = jnp.bitwise_and(i, 1)
        wait_rows(rows_s.at[slot], 2 * BINS * rows, out_sems.at[slot])

    constant(lambda c: c.start())
    come(first, 0, lambda c: c.start())
    constant(lambda c: c.wait())
    prepare()

    def step(i, carry):
        slot = jnp.bitwise_and(i, 1)
        come(first + i, slot, lambda c: c.wait())

        @pl.when(i + 1 < done)
        def _():
            come(first + i + 1, 1 - slot, lambda c: c.start())

        @pl.when(i >= 2)
        def _():
            wait_left(i - 2)

        rows_of(first + i, slot)
        departures(meta, first + i, rows_s, slot, to_ref, rows, out_sems)
        return carry

    lax.fori_loop(0, done, step, 0)

    @pl.when(done >= 2)
    def _():
        wait_left(done - 2)

    wait_left(done - 1)


def output_kernel(share, traj, meta_ref, bdn_ref, wdnt_ref, act_ref, mid_ref, *refs):
    lay_ref, wdnt_s, act_s, mid_s, sems, col_s, y_s, sel_s, rows_s, out_sems = refs[-10:]
    slots, d = lay_ref.shape[1:]
    meta = Meta(meta_ref, traj)

    def prepare():
        row = jnp.broadcast_to(bdn_ref[...].astype(F32).reshape(1, d), (8, d))
        col_s[...] = jnp.broadcast_to(row.T[:, 0:1], (d, BIN))

    def rows_of(tile, slot):
        mlps = [mm(wdnt_s[...], act_s[slot, :, pair_lanes(t)]) for t in range(BINS // 2)]
        for b in range(BINS):
            sel_s[b] = bin_slots(*meta.bin(tile * BINS + b)[2:])
        for t in range(BINS // 2):
            lanes = pair_lanes(t)
            y_s[:, lanes] = (mlps[t] + mid_s[slot, :, lanes].astype(F32) + two(col_s[...])).astype(BF16)
        for b in range(BINS):
            rows_s[slot, b] = mm(sel_s[b], y_s[:, bin_lanes(b)], NT).astype(BF16)

    store_tiles(
        share,
        meta,
        [(wdnt_ref, wdnt_s)],
        [(act_ref, act_s), (mid_ref, mid_s)],
        sems,
        prepare,
        rows_of,
        rows_s,
        lay_ref,
        slots,
        out_sems,
    )


CORE, Y, X, Z = 0, 1, 2, 3


def row_at(const=0, **bits):
    return const, tuple(({"core": CORE, "y": Y, "x": X, "z": Z}[name], coef) for name, coef in bits.items())


def mine(bit, rows, base=0):
    return base, ((bit, rows),)


def other(bit, rows, base=0):
    return base + rows, ((bit, -rows),)


class Step:
    def __init__(self, inputs, out_rows, parts, sends=()):
        self.inputs, self.out_rows, self.parts, self.sends = list(inputs), list(out_rows), list(parts), dict(sends)


def combine_kernel(step, bits_at, meta_ref, *refs):
    ins, outs = refs[: len(step.inputs)], refs[len(step.inputs) :]

    def row(start):
        if isinstance(start, int):
            return start
        const, bits = start
        for bit, coef in bits:
            const = const + meta_ref[bits_at + bit] * coef
        return const

    def rows(start, n):
        return pl.ds(start if isinstance(start, int) else pl.multiple_of(start, 8), n)

    for n, terms, goes in step.parts:
        for out, start, first, count in goes:
            total = None
            for ref, at in terms:
                term = ins[ref][rows(row(at) + row(first), count), :]
                total = term if total is None else total + term
            outs[out][rows(row(start), count), :] = total


def combine(step, meta, bits_at, width):
    vmem = pl.BlockSpec(memory_space=pltpu.VMEM)
    return pl.pallas_call(
        lambda *refs: combine_kernel(step, bits_at, *refs),
        in_specs=[pl.BlockSpec(memory_space=pltpu.SMEM)] + [vmem] * len(step.inputs),
        out_specs=[vmem] * len(step.out_rows),
        out_shape=[jax.ShapeDtypeStruct((n, width), F32) for n in step.out_rows],
        compiler_params=pltpu.CompilerParams(vmem_limit_bytes=2 * MIB),
        name="combine",
    )(meta, *step.inputs)


def bucket_sum(bits, keep, send, half, halve_z):
    h, e, f = half // 4, half // 8, half // 16
    _, (got,) = yield Step([send], [], [], {0: (CORE,)})

    def part(x, y):
        return (0 if x else 2 * h) + (0 if y else h), ((X, 2 * h if x else -2 * h), (Y, h if y else -h))

    (k, _, _, _), got = yield Step(
        [keep, got],
        [h] * 4,
        [
            (h, [(0, part(x, y)), (1, part(x, y))], [(out, row_at(), 0, h)])
            for out, (x, y) in enumerate(((True, True), (False, True), (True, False), (False, False)))
        ],
        {1: (X,), 2: (Y,), 3: (X, Y)},
    )
    four = [k, *got]
    if halve_z:
        (z, _), (got,) = yield Step(
            four,
            [e, e],
            [
                (
                    e,
                    [(n, row_at(c * e)) for n in range(4)],
                    [(0, row_at(c * f), mine(Z, f), f), (1, row_at(c * f), other(Z, f), f)],
                )
                for c in range(2)
            ],
            {1: (Z,)},
        )
        for bit in [*range(Z + 1, bits), Z]:
            (z,), (got,) = yield Step(
                [z, got], [e], [(e, [(0, row_at()), (1, row_at())], [(0, row_at(), 0, e)])], {0: (bit,)}
            )
        (e0, e1), (g0, g1) = yield Step(
            [z, got],
            [e, e],
            [
                (f, [(ref, row_at(c * f))], [(c, side(Z, f), 0, f)])
                for ref, side in enumerate((mine, other))
                for c in range(2)
            ],
            {0: (Y,), 1: (X,)},
        )
    else:
        (z,), (got,) = yield Step(
            four, [h], [(h, [(n, row_at()) for n in range(4)], [(0, row_at(), 0, h)])], {0: (bits - 1,)}
        )
        for bit in range(bits - 2, Z - 1, -1):
            (z,), (got,) = yield Step(
                [z, got], [h], [(h, [(0, row_at()), (1, row_at())], [(0, row_at(), 0, h)])], {0: (bit,)}
            )
        (e0, e1), (g0, g1) = yield Step(
            [z, got],
            [e, e],
            [(h, [(0, row_at()), (1, row_at())], [(0, row_at(), 0, e), (1, row_at(), e, e)])],
            {0: (Y,), 1: (X,)},
        )
    (f0, f1), (g0, g1) = yield Step(
        [e0, e1, g0, g1],
        [h, h],
        [
            (e, [(0, row_at())], [(0, mine(Y, e), 0, e)]),
            (e, [(2, row_at())], [(0, other(Y, e), 0, e)]),
            (e, [(1, row_at())], [(1, mine(X, e), 0, e)]),
            (e, [(3, row_at())], [(1, other(X, e), 0, e)]),
        ],
        {0: (X,), 1: (Y,)},
    )
    (near,), (far,) = yield Step(
        [f0, f1, g0, g1],
        [half],
        [
            (h, [(0, row_at())], [(0, mine(X, 2 * h, y * h), y * e, e) for y in range(2)]),
            (h, [(2, row_at())], [(0, other(X, 2 * h, y * h), y * e, e) for y in range(2)]),
            (h, [(1, row_at())], [(0, mine(Y, h, x * 2 * h + e), x * e, e) for x in range(2)]),
            (h, [(3, row_at())], [(0, other(Y, h, x * 2 * h + e), x * e, e) for x in range(2)]),
        ],
        {0: (CORE,)},
    )
    return near, far


class Sums:
    def __init__(self, ranks, meta, bits_at, width):
        self.ranks, self.meta, self.bits_at, self.width = ranks, meta, bits_at, width
        self.arrays, self.arrived, self.sent = [], [], []
        self.running, self.results = {}, {}

    def view(self, array):
        self.arrays.append(array)
        return (len(self.arrays) - 1, 0)

    def add(self, name, steps):
        self.running[name] = (steps, next(steps))

    def advance(self, after=None):
        if after is not None and self.arrived:
            tied = lax.optimization_barrier((*[self.arrays[k] for k in self.arrived], after))
            for k, array in zip(self.arrived, tied):
                self.arrays[k] = array
        inputs, out_rows, parts, places, sends = [], [], [], {}, {}
        for name, (_, step) in self.running.items():
            outs = []
            for out, rows in enumerate(step.out_rows):
                bit = step.sends.get(out)
                if bit in sends:
                    at = sends[bit]
                    outs.append((at, out_rows[at]))
                    out_rows[at] += rows
                    continue
                if bit is not None:
                    sends[bit] = len(out_rows)
                outs.append((len(out_rows), 0))
                out_rows.append(rows)
            places[name] = outs
            for rows, terms, goes in step.parts:
                moved = []
                for ref, (const, bits) in terms:
                    k, row = step.inputs[ref]
                    if k not in inputs:
                        inputs.append(k)
                    moved.append((inputs.index(k), (const + row, bits)))
                parts.append(
                    (
                        rows,
                        moved,
                        [(outs[out][0], (const + outs[out][1], bits), *rest) for out, (const, bits), *rest in goes],
                    )
                )
        base = len(self.arrays)
        if out_rows:
            merged = Step([self.arrays[k] for k in inputs], out_rows, parts)
            self.arrays += list(combine(merged, self.meta, self.bits_at, self.width))
        to_send = {bit: base + out for bit, out in sends.items()}
        raw = {name: step for name, (_, step) in self.running.items() if not step.parts}
        for step in raw.values():
            for out, bit in step.sends.items():
                to_send[(bit, id(step))] = step.inputs[out][0]
        self.sent = [self.arrays[k] for k in to_send.values()]
        received = {}
        for key, k in to_send.items():
            mask = sum(1 << bit for bit in (key[0] if isinstance(key[0], tuple) else key))
            perm = [(r, r ^ mask) for r in range(self.ranks)]
            received[key] = self.view(lax.ppermute(self.arrays[k], AXES, perm))[0]
        self.arrived = list(received.values())
        for name, (steps, step) in list(self.running.items()):
            if name in raw:
                outs = []
                got = [(received[(bit, id(step))], 0) for bit in step.sends.values()]
            else:
                outs = [(base + out, row) for out, row in places[name]]
                got = [(received[bit], places[name][out][1]) for out, bit in step.sends.items()]
            try:
                self.running[name] = (steps, steps.send((outs, got)))
            except StopIteration as stop:
                self.results[name] = stop.value
                del self.running[name]

    def ordered(self, value):
        return lax.optimization_barrier((value, *self.sent))[0]


def finish_kernel(
    bits_at, rows_at, meta_ref, late0_ref, late1_ref, first0_ref, first1_ref, g1_ref, c1_ref, wqkv_ref, wup_ref,
    dwn_ref, dup_ref, dwo_ref, dqkv_ref, dg1_ref, dc1_ref, dbq_ref, dbv_ref, dbo_ref, dg2_ref, dc2_ref, dbup_ref, dbdn_ref,
    late_s, first_s, first_sem, late_sem, out_sem,
):
    ff, d = dwn_ref.shape
    core = meta_ref[bits_at + CORE]
    late_near, late_far, first_near, first_far = rows_at
    first, late = [], []
    for to_s, copies, sems, sides in (
        (late_s, late, late_sem, ((late0_ref, late_near, core), (late1_ref, late_far, 1 - core))),
        (first_s, first, first_sem, ((first0_ref, first_near, core), (first1_ref, first_far, 1 - core))),
    ):
        half = to_s.shape[0] // 2
        for k, (ref, row, side) in enumerate(sides):
            to = to_s.at[pl.ds(pl.multiple_of(side * half, 8), half)]
            copies.append(pltpu.make_async_copy(ref.at[pl.ds(row, half)], to, sems.at[k]))
    for copy in late + first:
        copy.start()
    for copy in late:
        copy.wait()
    copies = [
        pltpu.make_async_copy(late_s.at[pl.ds(0, ff)], dwn_ref, out_sem.at[0]),
        pltpu.make_async_copy(late_s.at[pl.ds(2 * ff, d)], dwo_ref, out_sem.at[1]),
    ]
    for copy in copies:
        copy.start()
    for j in range(ff // d):
        dup_ref[:, j * d : (j + 1) * d] = late_s[ff + j * d : ff + (j + 1) * d, :].T
    for copy in first:
        copy.wait()

    def late_row(j):
        return first_s[3 * d + 3 + j : 3 * d + 4 + j, :].reshape(d)

    dg2_ref[...] = late_row(0)
    for j in range(ff // d):
        dbup_ref[j * d : (j + 1) * d] = late_row(1 + j)
    dbdn_ref[...] = late_row(5)
    dbo_ref[...] = late_row(6)

    def times(weight_ref, row, n):
        total = jnp.zeros((8, d), F32)
        for j in range(n):
            left = jnp.broadcast_to(first_s[row + j : row + j + 1, :], (8, d))
            for _ in range(3):
                low = left.astype(BF16)
                left = left - low.astype(F32)
                total = total + mm(low, weight_ref[:, j * d : (j + 1) * d], NT)
        return total[0:1, :]

    dc2_ref[...] = times(wup_ref, 3 * d + 4, ff // d).reshape(d)
    dc1_ref[...] = times(wqkv_ref, 3 * d, 3).reshape(d)

    gain = jnp.broadcast_to(g1_ref[...].astype(F32).reshape(1, d), (8, d)).T[:, 0:1]
    bias = jnp.broadcast_to(c1_ref[...].astype(F32).reshape(1, d), (8, d)).T[:, 0:1]
    gain_grad = jnp.zeros((d, d), F32)
    for j in range(3):
        block = slice(j * d, (j + 1) * d)
        total = first_s[3 * d + j : 3 * d + j + 1, :]
        product = first_s[block, :].T
        weight = wqkv_ref[:, block].astype(F32)
        dqkv_ref[:, block] = gain * product + bias * total
        gain_grad += weight * product
    dg1_ref[...] = jnp.sum(gain_grad.T, axis=0, keepdims=True).reshape(d)
    dbq_ref[...] = first_s[3 * d : 3 * d + 1, :].reshape(d)
    dbv_ref[...] = first_s[3 * d + 2 : 3 * d + 3, :].reshape(d)
    for copy in copies:
        copy.wait()


def doubled(shape):
    if len(shape) == 3:
        return (2 * shape[0],) + shape[1:]
    return shape[:-1] + (2 * shape[-1],)


SHARES_C = shares(0, 10, 16)
SHARES_D = shares(0, 4, 7, 10, 16)


def body(
    ranks,
    tokens,
    visible_index,
    visible_count,
    ln1_gain,
    ln1_bias,
    qkv_weight,
    query_bias,
    value_bias,
    out_weight,
    out_bias,
    ln2_gain,
    ln2_bias,
    up_weight,
    up_bias,
    down_weight,
    down_bias,
    out_grad,
):
    traj, slots = visible_index.shape
    seq, d = tokens.shape[1:]
    ff = up_weight.shape[1]
    hs = d // HEADS
    steps_a = -(-traj // BINS_A)
    tiles = 2 * steps_a
    tiles_at = Meta.size(traj) - 16
    bits = ranks.bit_length() - 1
    rank = lax.axis_index(AXES).astype(jnp.int32).reshape(1)
    meta = make_plan(visible_count, rank, slots)
    sums = Sums(ranks, meta, tiles_at + 1, d)

    shapes = dict(
        nhat=((d, TILE), BF16),
        rstd=((8, TILE), F32),
        qkv=((3 * d, TILE), BF16),
        prob=((BINS, BIN, HEADS * BIN), BF16),
        gatt=((d, TILE), BF16),
        gmid=((d, TILE), BF16),
        act=((ff, TILE), BF16),
        mid=((d, TILE), BF16),
    )

    def stored(name):
        shape, kind = shapes[name]
        return jax.ShapeDtypeStruct((steps_a,) + doubled(shape), kind)

    smem, vmem = (pl.BlockSpec(memory_space=m) for m in (pltpu.SMEM, pltpu.VMEM))

    def step_places(*names):
        return [pltpu.VMEM((2,) + doubled(shapes[n][0]), shapes[n][1]) for n in names]

    late_shape = (2 * ff + d, d)
    vectors = [ln1_gain, ln1_bias, query_bias, value_bias, out_bias, ln2_gain, ln2_bias, up_bias]
    weights = [qkv_weight, out_weight, up_weight, down_weight]
    down_weight_t, nhat, rstd, qkv, prob, gatt, gmid, act, mid, late_keep, late_send, late_vectors = pl.pallas_call(
        late_kernel,
        in_specs=[smem, vmem, HBM, HBM] + [vmem] * len(vectors + weights),
        out_specs=[vmem] + [HBM] * len(shapes) + [vmem] * 3,
        scratch_shapes=[
            pltpu.VMEM((2, BINS_A, 2 * seq, d), BF16),
            pltpu.VMEM((2, BINS_A, 2 * BIN, d), BF16),
            pltpu.SemaphoreType.DMA((2, 2)),
            *step_places(*shapes),
            pltpu.SemaphoreType.DMA((2, 8)),
            pltpu.VMEM((traj, BIN), jnp.int32),
            pltpu.VMEM((16, d), F32),
            pltpu.VMEM((12 * d, BIN), F32),
            pltpu.VMEM((3 * d, d), BF16),
            pltpu.VMEM((d, d), BF16),
            pltpu.VMEM((ff, d), BF16),
            pltpu.VMEM((d, TILE_A), F32),
            pltpu.VMEM((d, TILE_A), BF16),
            pltpu.VMEM((BINS_A * HEADS // 2, 2 * hs, PAIR), BF16),
            pltpu.VMEM((BINS_A * HEADS // 2, BIN, PAIR), F32),
            pltpu.VMEM((d, TILE_A), BF16),
            pltpu.VMEM((d, TILE_A), F32),
            pltpu.VMEM((d, TILE_A), BF16),
            pltpu.VMEM((d, TILE_A), BF16),
            pltpu.VMEM((ff, TILE_A), BF16),
            pltpu.VMEM((ff, TILE_A), BF16),
            pltpu.VMEM((ff, TILE_A), BF16),
            pltpu.VMEM((d, TILE_A), F32),
            pltpu.VMEM((d, TILE_A), F32),
            pltpu.VMEM(late_shape, F32),
            pltpu.VMEM((3 * d + ff, BIN), F32),
        ],
        out_shape=[jax.ShapeDtypeStruct((d, ff), BF16)]
        + [stored(n) for n in shapes]
        + [jax.ShapeDtypeStruct(n, F32) for n in ((late_shape[0] // 2, d), (late_shape[0] // 2, d), (8, d))],
        compiler_params=pltpu.CompilerParams(vmem_limit_bytes=58 * MIB),
        name="forward_mlp",
    )(meta, visible_index, tokens, out_grad, *vectors, *weights)
    late = bucket_sum(bits, sums.view(late_keep), sums.view(late_send), late_shape[0] // 2, True)
    sums.add("late", late)
    sums.advance()

    acc_shape = (-(-(3 * d + 11) // 128) * 128, d)
    send_shape = (acc_shape[0] // 2, d)
    grad_qkv, first_keep, first_send = pl.pallas_call(
        lambda *refs: attention_kernel(traj, *refs),
        in_specs=[smem] + [HBM] * 4 + [vmem],
        out_specs=[HBM, vmem, vmem],
        scratch_shapes=step_places("nhat", "qkv", "prob", "gatt")
        + [pltpu.VMEM((2, 3 * d, TILE_A), BF16), pltpu.SemaphoreType.DMA((2, 4)), pltpu.SemaphoreType.DMA((2,))]
        + [pltpu.VMEM((BINS_A * HEADS // 2, 2 * hs, PAIR), BF16)] * 2
        + [
            pltpu.VMEM((BINS_A * HEADS // 2, BIN, PAIR), F32),
            pltpu.VMEM((BINS_A * HEADS // 2, BIN, PAIR), BF16),
            pltpu.VMEM((3 * d, BIN), F32),
            pltpu.VMEM(acc_shape, F32),
        ],
        out_shape=[jax.ShapeDtypeStruct((steps_a, 3 * d, TILE_A), BF16)] + [jax.ShapeDtypeStruct(send_shape, F32)] * 2,
        compiler_params=pltpu.CompilerParams(vmem_limit_bytes=56 * MIB),
        cost_estimate=pl.CostEstimate(flops=5 * 10**9, bytes_accessed=16 * 10**6, transcendentals=0),
        name="attention_backward",
    )(sums.ordered(meta), nhat, qkv, prob, gatt, late_vectors)
    first = bucket_sum(bits, sums.view(first_keep), sums.view(first_send), send_shape[0], False)
    sums.add("first", first)
    sums.advance(first_keep)

    def tile_places(*names):
        shapes_of = dict(shapes, gq=((3 * d, TILE), BF16))
        return [pltpu.VMEM((2,) + shapes_of[n][0], shapes_of[n][1]) for n in names]

    def stores(kernel, name, vector, inputs, rows, scratch, earlier):
        given = [] if earlier is None else [earlier]
        return pl.pallas_call(
            kernel,
            in_specs=[smem, vmem] + [HBM] * (len(inputs) + len(given)),
            out_specs=HBM,
            scratch_shapes=scratch
            + [pltpu.VMEM((2, BINS, 2 * BIN, d), BF16), pltpu.SemaphoreType.DMA((2,))],
            out_shape=jax.ShapeDtypeStruct((traj, rows, d), BF16),
            input_output_aliases={2 + len(inputs): 0} if given else {},
            compiler_params=pltpu.CompilerParams(vmem_limit_bytes=56 * MIB),
            cost_estimate=pl.CostEstimate(flops=2 * 10**9, bytes_accessed=8 * 10**6, transcendentals=0),
            name=name,
        )(sums.ordered(meta), vector, *inputs, *given)

    def tokens_piece(share, earlier):
        return stores(
            lambda *refs, share=share: token_kernel(share, *refs),
            "tokens_backward",
            ln1_gain,
            [visible_index, qkv_weight, nhat, rstd, grad_qkv, gmid],
            seq,
            [pltpu.VMEM((traj, slots), jnp.int32), pltpu.VMEM((d, 3 * d), BF16)]
            + tile_places("nhat", "rstd", "gq", "gmid")
            + [pltpu.SemaphoreType.DMA((3, 4))]
            + [pltpu.VMEM((traj, BIN), jnp.int32), pltpu.VMEM((d, BIN), F32), pltpu.VMEM((d, TILE), BF16)],
            earlier,
        )

    def output_piece(share, earlier):
        return stores(
            lambda *refs, share=share: output_kernel(share, traj, *refs),
            "layer_output",
            down_bias,
            [down_weight_t, act, mid],
            slots,
            [pltpu.VMEM((d, ff), BF16)]
            + tile_places("act", "mid")
            + [pltpu.SemaphoreType.DMA((3, 4))]
            + [pltpu.VMEM((d, BIN), F32), pltpu.VMEM((d, TILE), BF16), pltpu.VMEM((BINS, 2 * BIN, BIN), BF16)],
            earlier,
        )

    tokens_grad = layer_out = None
    pieces = [(tokens_piece, SHARES_C[0]), (output_piece, SHARES_D[0]), (tokens_piece, SHARES_C[1])]
    for piece, share in pieces + [(output_piece, share) for share in SHARES_D[1:]]:
        if piece is tokens_piece:
            tokens_grad = piece(share, tokens_grad)
            sums.advance(tokens_grad)
        else:
            layer_out = piece(share, layer_out)
            sums.advance(layer_out)
    while sums.running:
        sums.advance()
    views = sums.results["late"] + sums.results["first"]
    near_far = [sums.arrays[k] for k, _ in views]
    rows_at = tuple(row for _, row in views)

    vmem = pl.BlockSpec(memory_space=pltpu.VMEM)
    vector = jax.ShapeDtypeStruct((d,), F32)
    dwn, dup, dwo, dqkv, dg1, dc1, dbq, dbv, dbo, dg2, dc2, dbup, dbdn = pl.pallas_call(
        lambda *refs: finish_kernel(tiles_at + 1, rows_at, *refs),
        in_specs=[pl.BlockSpec(memory_space=pltpu.SMEM)] + [HBM] * 4 + [vmem] * 4,
        out_specs=[HBM, vmem, HBM] + [vmem] * 10,
        out_shape=[
            jax.ShapeDtypeStruct((ff, d), F32),
            jax.ShapeDtypeStruct((d, ff), F32),
            jax.ShapeDtypeStruct((d, d), F32),
            jax.ShapeDtypeStruct((d, 3 * d), F32),
        ]
        + [vector] * 7
        + [jax.ShapeDtypeStruct((ff,), F32), vector],
        scratch_shapes=[
            pltpu.VMEM(late_shape, F32),
            pltpu.VMEM(acc_shape, F32),
            pltpu.SemaphoreType.DMA((2,)),
            pltpu.SemaphoreType.DMA((2,)),
            pltpu.SemaphoreType.DMA((2,)),
        ],
        compiler_params=pltpu.CompilerParams(vmem_limit_bytes=24 * MIB),
        name="finish",
    )(meta, *near_far, ln1_gain, ln1_bias, qkv_weight, up_weight)
    return layer_out, tokens_grad, dg1, dc1, dqkv, dbq, dbv, dwo, dbo, dg2, dc2, dup, dbup, dwn, dbdn


def solution(mesh):
    devices = mesh.devices
    ranks = devices.size
    mesh = Mesh(devices.reshape(devices.shape[0], devices.shape[1] // 2, 2), AXES)
    rows = P(AXES)
    placed = (rows, rows, rows) + (P(),) * 13 + (rows,)
    return jax.shard_map(
        lambda *args: body(ranks, *args),
        mesh=mesh,
        in_specs=placed,
        out_specs=(rows, rows) + (P(),) * 13,
        check_vma=False,
    )
```
